32 devices in a mesh: var: 4 (over y, x), item: 8 (over z, core).
Axes of the slice: x: 2, y: 2, z: 4, core: 2. Of those that a mesh axis runs over, the one named last changes fastest.
Arguments:
- fields: bfloat16 [8, 12, 4, 2048], P('item', 'var'), may hold values from -6 to 6
- var_mask: int32 [8, 12], P('item'), may hold values from 0 to 1, as said below
- embed_weight: bfloat16 [12, 4, 1024], P('var'), may hold values from -3 to 3
- var_embed: bfloat16 [12, 1024], P('var'), may hold values from -6 to 6
- agg_query: bfloat16 [1024], replicated, may hold values from -6 to 6
- agg_key: bfloat16 [1024, 1024], replicated, may hold values from -0.1875 to 0.1875
- agg_value: bfloat16 [1024, 1024], replicated, may hold values from -0.1875 to 0.1875
- agg_out: bfloat16 [1024, 1024], replicated, may hold values from -0.375 to 0.375
- norm1_gain: float32 [1024], replicated, may hold values from 0.25 to 1.75
- norm1_bias: float32 [1024], replicated, may hold values from -3 to 3
- attn_qkv: bfloat16 [1024, 3072], replicated, may hold values from -0.1875 to 0.1875
- attn_proj: bfloat16 [1024, 1024], replicated, may hold values from -0.75 to 0.75
- norm2_gain: float32 [1024], replicated, may hold values from 0.25 to 1.75
- norm2_bias: float32 [1024], replicated, may hold values from -3 to 3
- mlp_in: bfloat16 [1024, 4096], replicated, may hold values from -0.1875 to 0.1875
- mlp_out: bfloat16 [4096, 1024], replicated, may hold values from -0.09375 to 0.09375
- cotangent: bfloat16 [8, 2048, 1024], P('item', 'var'), may hold values from -6 to 6
Outputs:
- output: bfloat16 [8, 2048, 1024], P('item', 'var')
- fields_grad: float32 [8, 12, 4, 2048], P('item', 'var')
- embed_weight_grad: float32 [12, 4, 1024], P('var', None, 'item')
- var_embed_grad: float32 [12, 1024], P('var', 'item')
- agg_query_grad: float32 [1024], P('item')
- agg_key_grad: float32 [1024, 1024], P('item')
- agg_value_grad: float32 [1024, 1024], P('item')
- agg_out_grad: float32 [1024, 1024], P('item')
- norm1_gain_grad: float32 [1024], P('item')
- norm1_bias_grad: float32 [1024], P('item')
- attn_qkv_grad: float32 [1024, 3072], P('item')
- attn_proj_grad: float32 [1024, 1024], P('item')
- norm2_gain_grad: float32 [1024], P('item')
- norm2_bias_grad: float32 [1024], P('item')
- mlp_in_grad: float32 [1024, 4096], P('item')
- mlp_out_grad: float32 [4096, 1024], P('item')
The draws below stay inside these ranges and needn't reach their ends.
Inputs may be any that keep to these rules, and one draw needn't show every extreme that they name: `var_mask`: in every item at least 7 of the 12 slots are 1; which ones differs from item to item.
All inputs are finite; a program needn't handle non-finite values.
Results may differ from the reference program's by a relative error of at most 0.018.
Values may be sent and summed in bfloat16 or wider, within the bound.
No kernel may reach another device: no remote copies, remote signals or barrier semaphores. Data moves between devices by JAX's collectives and lax.ppermute only.
A program may use at most 448 MiB of HBM per device.

```python
import jax
import jax.numpy as jnp
from jax import lax

D = 1024
HEADS = 16
FF = 4096
HEAD_DIM = 64
VARS = 12
PATCHES = 2048
ITEMS = 8


def draw_var_mask(key, part):
    key = jax.random.fold_in(key, 7)
    count_key, order_key = jax.random.split(key)
    least = VARS * 5 // 8
    counts = jax.random.randint(count_key, (ITEMS,), least, VARS + 1)
    ranks = jax.vmap(lambda item_key: jax.random.permutation(item_key, VARS))(jax.random.split(order_key, ITEMS))
    return (ranks < counts[:, None]).astype(jnp.int32)


def block_scale(key, shape, pieces, smallest, high):
    def one(axis_at, blocks):
        draws = jax.random.uniform(jax.random.fold_in(jax.random.fold_in(key, 6), axis_at), (blocks,), jnp.float32, smallest / len(pieces), high / len(pieces))
        return jnp.repeat(jnp.exp(draws), shape[axis_at] // blocks).reshape((-1,) + (1,) * (len(shape) - axis_at - 1))

    loudness = one(*pieces[0])
    for cut in pieces[1:]:
        loudness = loudness * one(*cut)
    return loudness


def gaussian(stream_key, extent, scale, bound, pieces=(), kind=jnp.bfloat16):
    values = scale * jax.random.normal(stream_key, extent, jnp.float32)
    if pieces:
        values = values * block_scale(stream_key, extent, pieces, -0.22, 0.18)
    return jnp.clip(values, -bound, bound).astype(kind)


def setup_inputs(seed: int = 0) -> dict:
    key_of = jax.random.split(jax.random.key(seed), 18)
    fields = gaussian(key_of[0], (ITEMS, VARS, 4, PATCHES), 1.0, 6.0, ((0, 8), (1, 4)))
    var_mask = draw_var_mask(jax.random.fold_in(key_of[17], 71), 0)
    embed_weight = gaussian(key_of[2], (VARS, 4, D), 4 ** -0.5, 3.0, ((0, 4),))
    var_embed = gaussian(key_of[3], (VARS, D), 1.0, 6.0, ((0, 4),))
    agg_query = gaussian(key_of[4], (D,), 1.0, 6.0)
    agg_key = gaussian(key_of[5], (D, D), D ** -0.5, 0.1875)
    agg_value = gaussian(key_of[6], (D, D), D ** -0.5, 0.1875)
    agg_out = gaussian(key_of[7], (D, D), (D // 4) ** -0.5, 0.375)
    norm1_gain = jnp.clip(1.0 + 0.15 * jax.random.normal(key_of[8], (D,), jnp.float32), 0.25, 1.75)
    norm1_bias = gaussian(key_of[9], (D,), 0.5, 3.0, (), jnp.float32)
    attn_qkv = gaussian(key_of[10], (D, 3 * D), D ** -0.5, 0.1875)
    attn_proj = gaussian(key_of[11], (D, D), (D // 16) ** -0.5, 0.75)
    norm2_gain = jnp.clip(1.0 + 0.15 * jax.random.normal(key_of[12], (D,), jnp.float32), 0.25, 1.75)
    norm2_bias = gaussian(key_of[13], (D,), 0.5, 3.0, (), jnp.float32)
    mlp_in = gaussian(key_of[14], (D, FF), D ** -0.5, 0.1875)
    mlp_out = gaussian(key_of[15], (FF, D), FF ** -0.5, 0.09375)
    cotangent = gaussian(key_of[16], (ITEMS, PATCHES, D), 1.0, 6.0, ((0, 8), (1, 4)))
    return dict(fields=fields, var_mask=var_mask, embed_weight=embed_weight, var_embed=var_embed, agg_query=agg_query, agg_key=agg_key, agg_value=agg_value, agg_out=agg_out, norm1_gain=norm1_gain, norm1_bias=norm1_bias, attn_qkv=attn_qkv, attn_proj=attn_proj, norm2_gain=norm2_gain, norm2_bias=norm2_bias, mlp_in=mlp_in, mlp_out=mlp_out, cotangent=cotangent)


@jax.custom_vjp
def low(v):
    return lax.optimization_barrier(v.astype(jnp.bfloat16)).astype(jnp.float32)

@jax.custom_vjp
def low_back(v):
    return v

def low_keep(v):
    return (low(v), None)

def low_pass(kept, grad):
    return (grad,)

def back_keep(v):
    return (v, None)

def back_low(kept, grad):
    return (low(grad),)
low.defvjp(low_keep, low_pass)
low_back.defvjp(back_keep, back_low)
epsilon = 1e-05
highest = lax.Precision.HIGHEST
masked_score = -1e+30

def layer_norm(stream, norm_gain, norm_bias):
    centred = stream - lax.optimization_barrier(jnp.mean(stream, axis=-1, keepdims=True))
    inverse = lax.rsqrt(lax.optimization_barrier(jnp.mean(centred * centred, axis=-1, keepdims=True)) + epsilon)
    return centred * inverse * norm_gain + norm_bias

def one_item(pixels, real_vars, params):
    embed_weight, var_embed, agg_query, agg_key, agg_value, agg_out, norm1_gain, norm1_bias, attn_qkv, attn_proj, norm2_gain, norm2_bias, mlp_in, mlp_out = params
    score_scale = HEAD_DIM ** (-0.5)
    tokens = jnp.einsum('vcp,vcd->vpd', pixels, embed_weight, precision=highest) + var_embed[:, None, :]
    tokens = low(low_back(tokens))
    key_heads = agg_key.reshape(D, HEADS, HEAD_DIM)
    query_keys = low(jnp.einsum('dhe,he->dh', key_heads, agg_query.reshape(HEADS, HEAD_DIM), precision=highest) * score_scale)
    scores = low_back(jnp.einsum('vpd,dh->phv', tokens, query_keys, precision=highest))
    scores = jnp.where(real_vars[None, None, :] > 0, scores, masked_score)
    weights = low(jax.nn.softmax(scores, axis=-1))
    pooled = low(low_back(jnp.einsum('phv,vpd->phd', weights, tokens, precision=highest)))
    values = jnp.einsum('phd,dhe->phe', pooled, agg_value.reshape(D, HEADS, HEAD_DIM), precision=highest)
    values = low(low_back(values.reshape(PATCHES, D)))
    merged = jnp.dot(values, agg_out, precision=highest)
    normed = low(low_back(layer_norm(merged, norm1_gain, norm1_bias)))
    packed = low(low_back(jnp.dot(normed, attn_qkv, precision=highest)))
    queries = packed[:, :D].reshape(PATCHES, HEADS, HEAD_DIM)
    key_rows = packed[:, D:2 * D].reshape(PATCHES, HEADS, HEAD_DIM)
    value_rows = packed[:, 2 * D:].reshape(PATCHES, HEADS, HEAD_DIM)
    logits = low_back(jnp.einsum('phe,khe->hpk', queries, key_rows, precision=highest) * score_scale)
    attn_probs = low(jax.nn.softmax(logits, axis=-1))
    attended = jnp.einsum('hpk,khe->phe', attn_probs, value_rows, precision=highest).reshape(PATCHES, D)
    attended = low(low_back(attended))
    stream = merged + jnp.dot(attended, attn_proj, precision=highest)
    normed_two = low(low_back(layer_norm(stream, norm2_gain, norm2_bias)))
    hidden = low_back(jnp.dot(normed_two, mlp_in, precision=highest))
    active = low(jax.nn.gelu(hidden, approximate=False))
    return stream + jnp.dot(active, mlp_out, precision=highest)

def reference(fields, var_mask, embed_weight, var_embed, agg_query, agg_key, agg_value, agg_out, norm1_gain, norm1_bias, attn_qkv, attn_proj, norm2_gain, norm2_bias, mlp_in, mlp_out, cotangent):
    params = tuple((weight.astype(jnp.float32) for weight in (embed_weight, var_embed, agg_query, agg_key, agg_value, agg_out, norm1_gain, norm1_bias, attn_qkv, attn_proj, norm2_gain, norm2_bias, mlp_in, mlp_out)))

    def forward(fields_wide, weights_all):
        item_step = jax.checkpoint(one_item)
        return lax.map(lambda item_pair: item_step(item_pair[0], item_pair[1], weights_all), (fields_wide, var_mask))
    result, pullback = jax.vjp(forward, fields.astype(jnp.float32), params)
    fields_grad, grads = pullback(cotangent.astype(jnp.float32))
    return (result.astype(jnp.bfloat16), fields_grad, grads[0], grads[1], grads[2], grads[3], grads[4], grads[5], grads[6], grads[7], grads[8], grads[9], grads[10], grads[11], grads[12], grads[13])
```

```python
from functools import partial

import jax
import jax.numpy as jnp
from jax import lax
from jax.experimental import pallas as pl
from jax.experimental.pallas import tpu as pltpu
from jax.sharding import Mesh
from jax.sharding import PartitionSpec as P

HEADS = 16
TABLES = 5

epsilon = 1e-05
masked_score = -1e30
highest = lax.Precision.HIGHEST
f32 = jnp.float32
bf16 = jnp.bfloat16
COST = 0.05
VMEM_BYTES = 56 * 1024 * 1024
LOG2E = 1.4426950408889634


def dot(a, b):
    return lax.dot_general(a, b, (((1,), (0,)), ((), ())), preferred_element_type=f32)


def dot_nt(a, b):
    return lax.dot_general(a, b, (((1,), (1,)), ((), ())), preferred_element_type=f32)


def dot_tn(a, b):
    return lax.dot_general(a, b, (((0,), (0,)), ((), ())), preferred_element_type=f32)


def split_two(wide):
    high = wide.astype(bf16)
    return high, (wide - high.astype(f32)).astype(bf16)


def split_three(wide):
    high, rest = split_two(wide)
    low = wide - high.astype(f32) - rest.astype(f32)
    return high, rest, low.astype(bf16)


def columns(parts, rows, width):
    lane = lax.broadcasted_iota(jnp.int32, (rows, width), 1)
    out = jnp.zeros((rows, width), f32)
    for i, part in enumerate(parts):
        out = jnp.where(lane == i, part.astype(f32), out)
    return out.astype(bf16)


def whole(shape):
    return pl.BlockSpec(shape, lambda *_: (0,) * len(shape))


def params(vmem=VMEM_BYTES):
    return pltpu.CompilerParams(vmem_limit_bytes=vmem)


def cost(flops, bytes_accessed, transcendentals=0, share=COST):
    return pl.CostEstimate(
        flops=int(flops * share), bytes_accessed=int(bytes_accessed * share), transcendentals=0
    )


def norm_parts(stream):
    centred = stream - jnp.mean(stream, axis=-1, keepdims=True)
    inverse = lax.rsqrt(jnp.mean(centred * centred, axis=-1, keepdims=True) + epsilon)
    return centred * inverse, inverse


def norm_back(upstream, unit_rows, inverse, gain):
    scaled = upstream * gain
    return inverse * (
        scaled
        - jnp.mean(scaled, axis=-1, keepdims=True)
        - unit_rows * jnp.mean(scaled * unit_rows, axis=-1, keepdims=True)
    )


def variable_probs(pixel_rows, score_high, score_low, real, slots):
    scores = dot(score_high, pixel_rows) + dot(score_low, pixel_rows)
    scores = scores.reshape(HEADS, slots, pixel_rows.shape[1])
    scores = jnp.where(real[None] > 0, scores, masked_score)
    powers = jnp.exp(scores - jnp.max(scores, axis=1, keepdims=True))
    return powers / jnp.sum(powers, axis=1, keepdims=True)


def prep_kernel(count, vars_here, patches, *refs):
    place_ref = refs[0]
    pieces = refs[1 : 1 + count]
    query_ref, key_ref, value_ref = refs[1 + count : 4 + count]
    (
        pix_ref, tables_ref, shi_ref, slo_ref, sthi_ref, stlo_ref, front_ref, back_ref, keys_ref,
        qk_ref, spread_ref, all_s,
    ) = refs[4 + count :]
    me = place_ref[0]
    depth, width = tables_ref.shape
    slots = depth // TABLES
    size = width // HEADS
    rows = TABLES * vars_here
    total = None
    for d in range(count):
        row = lax.broadcasted_iota(jnp.int32, (depth, rows), 0)
        col = lax.broadcasted_iota(jnp.int32, (depth, rows), 1)
        want = (col % TABLES) * slots + (me ^ d) * vars_here + col // TABLES
        part = dot(jnp.where(row == want, 1.0, 0.0).astype(bf16), pieces[d][...])
        total = part if total is None else total + part
    all_s[...] = total.astype(bf16)
    mine = patches // count
    for d in range(count):
        at = pl.multiple_of((me ^ d) * mine, mine)
        pix_ref[:, d * mine : (d + 1) * mine] = all_s[:, pl.ds(at, mine)]
    tables = all_s[:, patches:]
    tables_ref[...] = tables
    head = lax.broadcasted_iota(jnp.int32, (HEADS, width), 0)
    same = lax.broadcasted_iota(jnp.int32, (HEADS, width), 1) // size == head
    spread = jnp.where(same, query_ref[...].astype(f32), 0.0)
    scale = size ** (-0.5)
    spread_ref[...] = (spread * scale).astype(bf16)
    query_keys = (dot_nt(key_ref[...], spread.astype(bf16)) * scale).astype(bf16)
    qk_ref[...] = query_keys
    halves = split_two(dot(tables, query_keys))
    wide = HEADS * slots
    picks = lax.broadcasted_iota(jnp.int32, (wide, HEADS), 0) // slots
    picks = jnp.where(picks == lax.broadcasted_iota(jnp.int32, (wide, HEADS), 1), 1.0, 0.0).astype(bf16)
    for half, tall, flat in zip(halves, (shi_ref, slo_ref), (sthi_ref, stlo_ref)):
        row = lax.broadcasted_iota(jnp.int32, (wide, depth), 0) % slots
        col = lax.broadcasted_iota(jnp.int32, (wide, depth), 1) % slots
        tall[...] = jnp.where(row == col, dot_nt(picks, half), 0.0).astype(bf16)
        row = lax.broadcasted_iota(jnp.int32, (depth, wide), 0) % slots
        col = lax.broadcasted_iota(jnp.int32, (depth, wide), 1) % slots
        flat[...] = jnp.where(row == col, dot_nt(half, picks), 0.0).astype(bf16)
    mixed = dot(tables, value_ref[...])
    high, low = split_two(mixed)
    high_wide, low_wide = high.astype(f32), low.astype(f32)
    front_ref[...] = jnp.concatenate([high_wide, high_wide, low_wide], axis=0).T.astype(bf16)
    both = jnp.concatenate([high, low], axis=0)
    for h in range(HEADS):
        back_ref[h] = both[:, h * size : (h + 1) * size]
    keys_ref[...] = dot(tables, key_ref[...])


def front_kernel(
    own_blocks, n_z, place_ref, pix_ref, shi_ref, slo_ref, real_ref, ev_ref, out_w_ref, gain_ref,
    bias_ref, wq_ref, wk_ref, wv_ref,
    values_ref, merged_ref, send_ref, keep_ref, q_ref, k_ref, v_ref, flat_ref, tall_s,
):
    slots = real_ref.shape[0]
    pixel_rows = pix_ref[...]
    probs = variable_probs(pixel_rows, shi_ref[...], slo_ref[...], real_ref[...], slots)
    weights = probs.astype(bf16).astype(f32)
    pixels = pixel_rows.astype(f32).reshape(TABLES, slots, -1)
    size = ev_ref.shape[0] // HEADS
    for h in range(HEADS):
        mixed = (weights[h][None] * pixels).reshape(pixel_rows.shape)
        high, low = split_two(mixed)
        flat_ref[h * size : (h + 1) * size, :] = dot(
            ev_ref[h * size : (h + 1) * size, :], jnp.concatenate([high, low, high], axis=0)
        )
    values = flat_ref[...].astype(bf16)
    merged = dot(values.T, out_w_ref[...])

    @pl.when(pl.program_id(0) < own_blocks)
    def _():
        values_ref[...] = values
        merged_ref[...] = merged

    unit_rows, _ = norm_parts(merged)
    normed = (unit_rows * gain_ref[...] + bias_ref[...]).astype(bf16)
    tall_s[...] = normed.T
    core, shard = place_ref[1], tall_s.shape[0] // (2 * n_z)
    for zz in range(n_z):
        at = slice(zz * shard, (zz + 1) * shard)
        keep_ref[at] = tall_s[pl.ds(pl.multiple_of((2 * zz + core) * shard, shard), shard), :]
        send_ref[at] = tall_s[pl.ds(pl.multiple_of((2 * zz + 1 - core) * shard, shard), shard), :]
    queries = dot(normed, wq_ref[...]).astype(bf16).astype(f32) * size ** (-0.5)
    keys = dot(normed, wk_ref[...])
    values = dot(normed, wv_ref[...])
    ones = jnp.where(lax.broadcasted_iota(jnp.int32, (keys.shape[0], size), 1) < 3, 1.0, 0.0)
    for h in range(q_ref.shape[0]):
        at = h * size
        q_ref[h] = queries[:, at : at + size].astype(bf16)
        key = keys[:, at : at + size]
        k_ref[h] = jnp.concatenate([key, key], axis=1).astype(bf16)
        v_ref[h] = jnp.concatenate([values[:, at : at + size], ones], axis=1).astype(bf16)


def attend_kernel(q_ref, k_ref, v_ref, out_ref, aug_ref):
    here, rows, size = q_ref.shape
    for h in range(here):
        aug_ref[h, :, : 2 * size] = jnp.concatenate(
            split_two(q_ref[h].astype(f32) * LOG2E), axis=1
        )

    def scores_of(h):
        return dot_nt(aug_ref[h, :, : 2 * size], k_ref[h])

    def finish(h, powers, top):
        mixed = dot(powers, v_ref[h])
        total = mixed[:, size : size + 1]
        lse = top + jnp.log(total) * LOG2E
        return (mixed[:, :size] / total).astype(bf16), columns(split_three(-lse), rows, 2 * size)

    done, waiting = [], None
    scores = scores_of(0)
    for h in range(here):
        later = scores_of(h + 1) if h + 1 < here else None
        top = jnp.max(scores, axis=-1, keepdims=True)
        powers = jnp.exp2(scores - top).astype(bf16)
        if waiting is not None:
            done.append(finish(*waiting))
        waiting = (h, powers, top)
        scores = later
    done.append(finish(*waiting))
    for h in range(here):
        aug_ref[h, :, 2 * size :] = done[h][1]
    out_ref[...] = jnp.concatenate([part for part, _ in done], axis=-1)


def attend_back_kernel(count, extra, *refs):
    extra_refs, refs = refs[:extra], refs[extra:]
    q_ref, k_ref, v_ref = refs[:3]
    aug_refs = refs[3 : 3 + count]
    out_refs = refs[3 + count : 3 + 2 * count]
    up_refs = refs[3 + 2 * count : 3 + 3 * count]
    full_ref = refs[3 + 3 * count]
    piece_refs = refs[4 + 3 * count : 4 + 4 * count]
    up_s, gq_ref, prob_s, slope_s = refs[4 + 4 * count :]
    step = pl.program_id(0)
    here, patches, size = q_ref.shape
    block = k_ref.shape[1]
    width = here * size
    mine = patches // count

    @pl.when(step == 0)
    def _():
        for h in range(here):
            at = h * size
            for d in range(count):
                upstream = up_refs[d][:, at : at + size]
                product = upstream.astype(f32) * out_refs[d][:, at : at + size].astype(f32)
                total = jnp.sum(product, axis=-1, keepdims=True)
                up_s[h, d * mine : (d + 1) * mine] = jnp.concatenate(
                    [upstream, columns(split_three(-total), mine, size)], axis=1
                )
            gq_ref[h] = jnp.zeros((size, patches), f32)

    chunk = min(256, mine)
    key_parts, value_parts = [], []
    ones = jnp.where(lax.broadcasted_iota(jnp.int32, (block, 2 * size), 1) < 3, 1.0, 0.0).astype(bf16)
    for h in range(here):
        keys, values = k_ref[h], v_ref[h]
        keys_wide = jnp.concatenate([keys, ones], axis=1)
        for at in range(0, patches, chunk):
            span = slice(at, at + chunk)
            rows = slice(at % mine, at % mine + chunk)
            probs = jnp.exp2(dot_nt(keys_wide, aug_refs[at // mine][h, rows]))
            prob_s[h, :, span] = probs.astype(bf16)
            slope_s[h, :, span] = (probs * dot_nt(values, up_s[h, span])).astype(bf16)
        value_parts.append(dot(prob_s[h], up_s[h])[:, :size])
        key_parts.append(dot(slope_s[h], q_ref[h]))
        gq_ref[h] += dot(keys.astype(f32).T[:size].astype(bf16), slope_s[h])
    rows = pl.ds(pl.multiple_of(step * block, block), block)
    full_ref[rows, width : 2 * width] = jnp.concatenate(key_parts, axis=-1).astype(bf16)
    full_ref[rows, 2 * width :] = jnp.concatenate(value_parts, axis=-1).astype(bf16)

    @pl.when(step == pl.num_programs(0) - 1)
    def _():
        scale = size ** (-0.5)
        query_parts = [gq_ref[h].T for h in range(here)]
        full_ref[:, :width] = (jnp.concatenate(query_parts, axis=-1) * scale).astype(bf16)
        for d in range(count):
            piece_refs[d][:, : 3 * width] = full_ref[d * mine : (d + 1) * mine, :]

    if extra:

        @pl.when(step == 0)
        def _():
            for d in range(count):
                piece_refs[d][:, 3 * width :] = extra_refs[d][...]


def mlp_kernel(pieces, count, *refs):
    place_ref = refs[0]
    att_refs = refs[1 : 1 + pieces]
    merged_ref, proj_ref, gain_ref, bias_ref, cot_ref, win_ref, wout_ref = refs[1 + pieces : 8 + pieces]
    outs = refs[8 + pieces :]
    (
        out_ref, att_t_ref, normed_t_ref, send_ref, keep_ref, ghid_ref, gstream_ref, glow_ref,
        gains_ref,
    ) = outs[:9]
    gatt_refs = outs[9 : 9 + count]
    att_s, normed_s, stream_s, unit_s, inv_s, out_s, gn_s, tall_s = outs[9 + count :]
    step = pl.program_id(0)
    me = place_ref[0]
    cols = gatt_refs[0].shape[1]

    @pl.when(step == 0)
    def _():
        if pieces == 1:
            attended = att_refs[0][...]
        else:
            for d in range(pieces):
                att_s[:, pl.ds(pl.multiple_of((me ^ d) * cols, cols), cols)] = att_refs[d][...]
            attended = att_s[...]
        att_t_ref[...] = attended.T
        stream = merged_ref[...] + dot(attended, proj_ref[...])
        unit_rows, inverse = norm_parts(stream)
        stream_s[...] = stream
        unit_s[...] = unit_rows
        inv_s[...] = inverse
        normed = (unit_rows * gain_ref[...] + bias_ref[...]).astype(bf16)
        normed_s[...] = normed
        normed_t_ref[...] = normed.T
        out_s[...] = jnp.zeros_like(out_s)
        gn_s[...] = jnp.zeros_like(gn_s)

    tile = ghid_ref.shape[1]
    sub = min(256, tile)
    spans = [slice(at, at + sub) for at in range(0, tile, sub)]
    normed_rows, upstream_rows = normed_s[...], cot_ref[...]

    def products(span):
        return dot(normed_rows, win_ref[:, span]), dot_nt(upstream_rows, wout_ref[span, :])

    def shape(hidden, g_active):
        below = 0.5 + 0.5 * lax.erf(hidden * (0.5**0.5))
        density = jnp.exp(-0.5 * hidden * hidden) * ((2.0 * jnp.pi) ** (-0.5))
        return (hidden * below).astype(bf16), (g_active * (below + hidden * density)).astype(bf16)

    actives, grads, sums = [], [], []

    def add(first, last):
        span = slice(spans[first].start, spans[last].stop)
        active = jnp.concatenate(actives[first : last + 1], axis=1)
        grad = jnp.concatenate(grads[first : last + 1], axis=1)
        sums.append((dot(active, wout_ref[span, :]), dot_nt(grad, win_ref[:, span])))

    ready = products(spans[0])
    for i, span in enumerate(spans):
        later = products(spans[i + 1]) if i + 1 < len(spans) else None
        if i == len(spans) // 2 + 1:
            add(0, len(spans) // 2 - 1)
        active, grad = shape(*ready)
        actives.append(active)
        grads.append(grad)
        ready = later
    add(len(spans) // 2 if sums else 0, len(spans) - 1)
    for span, active, grad in zip(spans, actives, grads):
        ghid_ref[:, span] = grad
        tall_s[span, :] = active.T
    half = tile // 2
    core = place_ref[1]
    send_ref[...] = tall_s[pl.ds(pl.multiple_of((1 - core) * half, half), half), :]
    keep_ref[...] = tall_s[pl.ds(pl.multiple_of(core * half, half), half), :]
    out_s[...] += sum(pair[0] for pair in sums)
    gn_s[...] += sum(pair[1] for pair in sums)

    @pl.when(step == pl.num_programs(0) - 1)
    def _():
        out_ref[...] = (stream_s[...] + out_s[...]).astype(bf16)
        upstream = gn_s[...].astype(bf16).astype(f32)
        unit_rows = unit_s[...]
        g_stream = cot_ref[...].astype(f32) + norm_back(
            upstream, unit_rows, inv_s[...], gain_ref[...]
        )
        gstream_ref[...] = g_stream
        low = g_stream.astype(bf16)
        glow_ref[...] = low
        for d in range(count):
            rows = pl.ds(pl.multiple_of((me ^ d) * cols, cols), cols)
            gatt_refs[d][...] = dot_nt(low, proj_ref[rows, :]).astype(bf16)
        gains_ref[0:1, :] = jnp.sum(upstream * unit_rows, axis=0, keepdims=True)
        gains_ref[1:2, :] = jnp.sum(upstream, axis=0, keepdims=True)


def send_kernel(place_ref, main_rows, main_cols, side_rows, side_cols, out_ref):
    last = pl.program_id(0) == pl.num_programs(0) - 1

    def product(rows_ref, cols_ref):
        tall = rows_ref[...].reshape(-1, rows_ref.shape[-1])
        return dot(tall, cols_ref[...]).astype(bf16)

    @pl.when(jnp.logical_not(last))
    def _():
        out_ref[...] = product(main_rows, main_cols)

    @pl.when(last)
    def _():
        out_ref[...] = product(side_rows, side_cols)


def keep_kernel(count, *refs):
    main_rows, main_cols, main_got, side_rows, side_cols, side_got = refs[1:7]
    outs = refs[7:]
    step = pl.program_id(0)

    def product(rows_ref, cols_ref, got_ref):
        tall = rows_ref[...].reshape(-1, rows_ref.shape[-1])
        return (dot(tall, cols_ref[...]) + got_ref[...].astype(f32)).astype(bf16)

    for d in range(count):

        @pl.when(step == d)
        def _():
            first, second = outs[d], outs[count + d]
            main = product(main_rows, main_cols, main_got)
            cut = first.shape[1]
            rest = main.shape[1] - cut
            first[...] = main[:, :cut]
            second[:, :rest] = main[:, cut:]
            second[:, rest:] = product(side_rows, side_cols, side_got)


def pair_kernel(count, channels, vars_here, late_rows, *refs):
    place_ref = refs[0]
    keep_ref, got_ref, n_keep_ref, n_got_ref, fields_ref = refs[1:6]
    outs = refs[6:]
    depth, mine = fields_ref.shape
    rows = late_rows
    span = outs[0].shape[1]
    slots = depth // TABLES
    n_blocks = n_keep_ref.shape[1] // span
    f_rows = (outs[0].shape[0] - rows - n_blocks * HEADS) // (mine // span)
    row = lax.broadcasted_iota(jnp.int32, (f_rows, depth), 0)
    col = lax.broadcasted_iota(jnp.int32, (f_rows, depth), 1)
    n_total = (n_keep_ref[...] + n_got_ref[...].astype(f32)).astype(bf16)
    for d in range(count):
        q = place_ref[0] ^ d

        def block(ref):
            if len(ref.shape) == 3:
                return ref[d, :rows].astype(f32)
            return ref[:rows, pl.ds(pl.multiple_of(q * span, span), span)].astype(f32)

        outs[d][:rows] = (block(keep_ref) + block(got_ref)).astype(bf16)
        want = (row % channels) * slots + q * vars_here + row // channels
        picks = jnp.where((want == col) & (row < channels * vars_here), 1.0, 0.0).astype(bf16)
        picked = dot(picks, fields_ref[...]).astype(bf16)
        at = rows
        for b in range(n_blocks):
            outs[d][at : at + HEADS] = n_total[:, b * span : (b + 1) * span]
            at += HEADS
        for b in range(mine // span):
            outs[d][at : at + f_rows] = picked[:, b * span : (b + 1) * span]
            at += f_rows


def z_pieces_kernel(count, shard, n_z, *refs):
    pieces, outs, fields_ref, total_s = refs[1 : 1 + count], refs[1 + count : -2], refs[-2], refs[-1]
    me, z_at = refs[0][0], refs[0][2]
    rows, span = total_s.shape
    f_rows = fields_ref.shape[0]
    mine = fields_ref.shape[1] // count
    total = pieces[0][:rows].astype(f32)
    for piece in pieces[1:]:
        total = total + piece[:rows].astype(f32)
    total_s[...] = total.astype(bf16)
    for d in range(n_z):
        start = pl.multiple_of((z_at ^ d) * shard, shard)
        outs[d][:shard] = total_s[pl.ds(start, shard), :]
        outs[d][shard:] = total_s[n_z * shard :, :]
    for d in range(count):
        blocks = [
            pieces[d][rows + b * f_rows : rows + (b + 1) * f_rows] for b in range(mine // span)
        ]
        at = pl.multiple_of((me ^ d) * mine, mine)
        fields_ref[:, pl.ds(at, mine)] = jnp.concatenate(blocks, axis=1).astype(f32)


def assemble_kernel(count, parts, size, halves, *refs):
    me = refs[0][0]
    blocks, outs = refs[1 : 1 + count + halves], refs[1 + count + halves :]
    in_ref, proj_ref, qkv_ref, out_ref = outs
    a = in_ref.shape[1] // count
    b = proj_ref.shape[1] // count
    width = proj_ref.shape[1]
    for d in range(count):
        if halves and d == count - 1:
            rows = jnp.concatenate([ref[...] for ref in blocks[d:]], axis=1)
        else:
            rows = blocks[d][...]
        rows = rows.astype(f32)
        q = me ^ d if halves else d

        def span(at, step):
            return pl.ds(pl.multiple_of(at, step) if halves else at, step)

        in_ref[:, span(q * a, a)] = rows[:, :a]
        proj_ref[:, span(q * b, b)] = rows[:, a : a + b]
        at = a + b
        for part in range(parts):
            for third in range(3):
                to = third * width + q * b + part * size
                qkv_ref[:, span(to, size)] = rows[:, at : at + size]
                at += size
        out_ref[q] = rows[:, at:]


def z_sum_kernel(count, *refs):
    pieces, (rows_ref, n_ref) = refs[:count], refs[count:]
    total = pieces[0][...].astype(f32)
    for piece in pieces[1:]:
        total = total + piece[...].astype(f32)
    rows, span = rows_ref.shape
    rows_ref[...] = total[:rows].astype(bf16)
    for b in range(n_ref.shape[1] // span):
        n_ref[:, b * span : (b + 1) * span] = total[rows + b * HEADS : rows + (b + 1) * HEADS]


def final_kernel(count, *refs):
    place_ref = refs[0]
    pieces = refs[1 : 1 + count]
    n_ref, tables_ref, spread_ref, keys_ref, value_ref, qk_ref = refs[1 + count : 7 + count]
    outg_ref, valg_ref, keyg_ref, queryg_ref, embedg_ref, varg_ref, gains_ref, m_s = refs[7 + count :]
    shard, depth = tables_ref.shape
    width = m_s.shape[1]
    for d in range(count):
        span = pieces[d].shape[1]
        at = 0 if count == 1 else pl.multiple_of((place_ref[0] ^ d) * span, span)
        outg_ref[:, pl.ds(at, span)] = pieces[d][:shard].astype(f32)
        m_s[:, pl.ds(at, span)] = pieces[d][shard:].astype(f32)
    m_low = m_s[:depth, :].astype(bf16)
    n_high, n_low = split_two(n_ref[:, :depth])
    tables = tables_ref[...]
    valg_ref[...] = dot(tables, m_low)
    g_qk = dot_nt(tables, n_high) + dot_nt(tables, n_low)
    qk_high, qk_low = split_two(g_qk)
    spread = spread_ref[...]
    keyg_ref[...] = dot(qk_high, spread) + dot(qk_low, spread)
    head_at = lax.broadcasted_iota(jnp.int32, (HEADS, width), 1) // (width // HEADS)
    same = head_at == lax.broadcasted_iota(jnp.int32, (HEADS, width), 0)
    ones = jnp.where(same, 1.0, 0.0).astype(bf16)
    n_wide = dot(n_high.astype(f32).T.astype(bf16), ones) + dot(n_low.astype(f32).T.astype(bf16), ones)
    queryg_ref[...] = jnp.sum(n_wide * keys_ref[...], axis=0, keepdims=True)
    qk = qk_ref[...]
    table_grad = split_three(
        dot_nt(m_low, value_ref[...])
        + dot_nt(n_high.astype(f32).T.astype(bf16), qk)
        + dot_nt(n_low.astype(f32).T.astype(bf16), qk)
    )
    slots = depth // TABLES
    vars_here = varg_ref.shape[0]
    for ref, first, each in ((embedg_ref, 0, TABLES - 1), (varg_ref, TABLES - 1, 1)):
        row = lax.broadcasted_iota(jnp.int32, (each * vars_here, depth), 0)
        col = lax.broadcasted_iota(jnp.int32, (each * vars_here, depth), 1)
        want = (first + row % each) * slots + place_ref[0] * vars_here + row // each
        picks = jnp.where(want == col, 1.0, 0.0).astype(bf16)
        ref[...] = sum(dot(picks, part) for part in table_grad)
    gains_ref[...] = m_s[depth : depth + 8, :]


def back_kernel(count, parts, n_z, *refs):
    place_ref = refs[0]
    piece_refs = refs[1 : 1 + count * parts]
    (
        qkv_ref, merged_ref, gain_ref, gs_ref, out_w_ref, pix_ref, shi_ref, slo_ref, sthi_ref,
        stlo_ref, real_ref, ev_ref, values_ref, gains_two_ref,
        fields_ref, send_ref, keep_ref, slope_s, packed_s, m_ref, n_ref, grad_s,
    ) = refs[1 + count * parts :]
    step = pl.program_id(0)
    slots = real_ref.shape[0]
    if count == 1:
        packed = piece_refs[0][...]
    else:
        span = piece_refs[0].shape[1] // 3
        for third in range(3):
            for part in range(parts):
                for d in range(count):
                    at = third * (count * parts) + (place_ref[0] ^ d) * parts + part
                    packed_s[:, pl.ds(pl.multiple_of(at * span, span), span)] = piece_refs[
                        part * count + d
                    ][:, third * span : (third + 1) * span]
        packed = packed_s[...]
    unit_rows, inverse = norm_parts(merged_ref[...])
    upstream = dot_nt(packed, qkv_ref[...]).astype(bf16).astype(f32)
    g_merged = gs_ref[...] + norm_back(upstream, unit_rows, inverse, gain_ref[...])
    low = g_merged.astype(bf16)
    depth = pix_ref.shape[0]

    @pl.when(step == 0)
    def _():
        m_ref[...] = jnp.zeros_like(m_ref)
        n_ref[...] = jnp.zeros_like(n_ref)
        grad_s[...] = jnp.zeros_like(grad_s)
        m_ref[depth + 2 : depth + 4, :] = gains_two_ref[...]

    grad_s[...] += dot(values_ref[...], low)
    m_ref[depth : depth + 1, :] += jnp.sum(upstream * unit_rows, axis=0, keepdims=True)
    m_ref[depth + 1 : depth + 2, :] += jnp.sum(upstream, axis=0, keepdims=True)
    g_values = dot_nt(low, out_w_ref[...]).astype(bf16)

    pixel_rows = pix_ref[...]
    probs = variable_probs(pixel_rows, shi_ref[...], slo_ref[...], real_ref[...], slots)
    weights = probs.astype(bf16).astype(f32)
    pixels = pixel_rows.astype(f32).reshape(TABLES, slots, -1)
    size = ev_ref.shape[2]
    g_fields = jnp.zeros(pixels.shape, f32)
    for h in range(HEADS):
        rows = g_values[:, h * size : (h + 1) * size]
        both = dot_nt(ev_ref[h], rows)
        table = (both[:depth] + both[depth:]).reshape(pixels.shape)
        g_weights = jnp.sum(pixels * table, axis=0)
        total = jnp.sum(g_weights * probs[h], axis=0, keepdims=True)
        slope_s[h * slots : (h + 1) * slots, :] = (probs[h] * (g_weights - total)).astype(bf16)
        g_fields += weights[h][None] * table
        mixed = (weights[h][None] * pixels).reshape(pixel_rows.shape)
        pair = dot(jnp.concatenate(split_two(mixed), axis=0), rows)
        m_ref[:depth, h * size : (h + 1) * size] += pair[:depth] + pair[depth:]
    slopes = slope_s[...]
    fields_ref[...] = (
        g_fields.reshape(pixel_rows.shape) + dot(sthi_ref[...], slopes) + dot(stlo_ref[...], slopes)
    ).astype(bf16)
    n_ref[...] += dot_nt(pixel_rows, slopes)

    @pl.when(step == pl.num_programs(0) - 1)
    def _():
        core = place_ref[1]
        shard = grad_s.shape[0] // (2 * n_z)
        for zz in range(n_z):
            at = slice(zz * shard, (zz + 1) * shard)
            keep_ref[at] = grad_s[pl.ds(pl.multiple_of((2 * zz + core) * shard, shard), shard), :]
            send_ref[at] = grad_s[
                pl.ds(pl.multiple_of((2 * zz + 1 - core) * shard, shard), shard), :
            ].astype(bf16)
        top = n_z * shard
        middle = top + m_ref.shape[0]
        tables = m_ref[...]
        keep_ref[top:middle] = tables
        send_ref[top:middle] = tables.astype(bf16)
        columns = lax.broadcasted_iota(jnp.int32, n_ref.shape, 1)
        same = columns % slots == lax.broadcasted_iota(jnp.int32, n_ref.shape, 0) % slots
        n_high, n_low = split_two(jnp.where(same, n_ref[...], 0.0))
        heads = (HEADS, n_ref.shape[1])
        picks = lax.broadcasted_iota(jnp.int32, heads, 1) // slots
        picks = jnp.where(picks == lax.broadcasted_iota(jnp.int32, heads, 0), 1.0, 0.0).astype(bf16)
        n_rows = dot_nt(picks, n_high) + dot_nt(picks, n_low)
        keep_ref[middle:] = jnp.zeros((HEADS, keep_ref.shape[1]), f32)
        keep_ref[middle:, :depth] = n_rows
        send_ref[middle:] = keep_ref[middle:].astype(bf16)


def per_device(
    n_var, n_z, fields, var_mask, embed_weight, var_embed, agg_query, agg_key, agg_value, agg_out,
    norm1_gain, norm1_bias, attn_qkv, attn_proj, norm2_gain, norm2_bias, mlp_in, mlp_out, cotangent,
):
    n_item = 2 * n_z
    width = agg_key.shape[0]
    size = width // HEADS
    scale = size ** (-0.5)
    hidden_width = mlp_in.shape[1]
    vars_here, channels, patches = fields.shape[1:]
    slot_count = var_mask.shape[1]
    slots = -(-slot_count // 16) * 16
    mine = patches // n_var
    here = HEADS // n_var
    cols = here * size
    shard = width // n_item
    me = lax.axis_index("var")
    core = lax.axis_index("core")
    z_at = lax.axis_index("z")
    item = z_at * 2 + core
    rel = me ^ jnp.arange(n_var)
    rel_z = z_at ^ jnp.arange(n_z)
    place = jnp.stack([me, core, z_at]).astype(jnp.int32)
    lanes_fit = cols % 128 == 0

    def send(array, other):
        return lax.ppermute(array, "var", [(i, i ^ other) for i in range(n_var)])

    def send_z(array, other):
        return lax.ppermute(array, "z", [(i, i ^ other) for i in range(n_z)])

    def swap_core(array):
        return lax.ppermute(array, "core", [(0, 1), (1, 0)])

    def canonical(by_distance):
        return jnp.take(jnp.stack(by_distance, axis=0), rel, axis=0)

    def call(kernel, grid, in_specs, out_specs, out_shape, scratch, estimate, name, *args):
        return pl.pallas_call(
            kernel,
            grid_spec=pltpu.PrefetchScalarGridSpec(
                num_scalar_prefetch=1,
                grid=grid,
                in_specs=in_specs,
                out_specs=out_specs,
                scratch_shapes=scratch,
            ),
            out_shape=out_shape,
            compiler_params=params(),
            cost_estimate=estimate,
            name=name,
        )(place, *args)

    depth = TABLES * slots
    pixel_part = jnp.concatenate([fields[0], jnp.ones((vars_here, 1, patches), bf16)], axis=1)
    table_part = jnp.concatenate([embed_weight, var_embed[:, None, :]], axis=1)
    piece = jnp.concatenate([pixel_part, table_part], axis=2).reshape(TABLES * vars_here, -1)
    pieces = [piece] + [send(piece, d) for d in range(1, n_var)]
    real = jnp.pad(var_mask[0], (0, slots - slot_count)).astype(f32)[:, None]
    prep_in = pieces + [agg_query[None], agg_key, agg_value]
    maps = [(HEADS * slots, depth)] * 2 + [(depth, HEADS * slots)] * 2
    prep_out = (
        [((depth, patches), bf16), ((depth, width), bf16)]
        + [(shape, bf16) for shape in maps]
        + [
            ((width, 3 * depth), bf16),
            ((HEADS, 2 * depth, size), bf16),
            ((depth, width), f32),
            ((width, HEADS), bf16),
            ((HEADS, width), bf16),
        ]
    )
    (
        pixels, tables, score_high, score_low, score_high_t, score_low_t, ev_front, ev_back,
        table_keys, query_keys, spread,
    ) = call(
        partial(prep_kernel, n_var, vars_here, patches),
        (1,),
        [whole(array.shape) for array in prep_in],
        [whole(shape) for shape, _ in prep_out],
        [jax.ShapeDtypeStruct(shape, kind) for shape, kind in prep_out],
        [pltpu.VMEM((depth, patches + width), bf16)],
        cost(8 * depth * width * width, 4 * width * width),
        "prep",
        *prep_in,
    )

    gain_one, bias_one = norm1_gain[None], norm1_bias[None]
    gain_two, bias_two = norm2_gain[None], norm2_bias[None]

    if lanes_fit:
        qkv_parts = [attn_qkv] * 3
        qkv_specs = [
            pl.BlockSpec((width, cols), lambda i, at, third=third: (0, third * n_var + at[0]))
            for third in range(3)
        ]
    else:
        qkv_mine = lax.dynamic_index_in_dim(
            attn_qkv.reshape(width, 3, n_var, cols), me, axis=2, keepdims=False
        )
        qkv_parts = [qkv_mine[:, third] for third in range(3)]
        qkv_specs = [whole((width, cols))] * 3

    block = min(512, mine)
    steps = patches // block
    own = mine // block
    heads_shape = jax.ShapeDtypeStruct((here, patches, size), bf16)
    heads_spec = pl.BlockSpec((here, block, size), lambda i, _: (0, i, 0))
    wide_shape = jax.ShapeDtypeStruct((here, patches, 2 * size), bf16)
    wide_spec = pl.BlockSpec((here, block, 2 * size), lambda i, _: (0, i, 0))
    agg_values_t, merged, normed_send, normed_keep, queries, keys, values = call(
        partial(front_kernel, own, n_z),
        (steps,),
        [
            pl.BlockSpec((depth, block), lambda i, _: (0, i)),
            whole(score_high.shape),
            whole(score_low.shape),
            whole(real.shape),
            whole(ev_front.shape),
            whole(agg_out.shape),
            whole(gain_one.shape),
            whole(bias_one.shape),
        ]
        + qkv_specs,
        [
            pl.BlockSpec((width, block), lambda i, _: (0, jnp.minimum(i, own - 1))),
            pl.BlockSpec((block, width), lambda i, _: (jnp.minimum(i, own - 1), 0)),
            pl.BlockSpec((width // 2, block), lambda i, _: (0, i)),
            pl.BlockSpec((width // 2, block), lambda i, _: (0, i)),
            heads_spec,
            wide_spec,
            wide_spec,
        ],
        [
            jax.ShapeDtypeStruct((width, mine), bf16),
            jax.ShapeDtypeStruct((mine, width), f32),
            jax.ShapeDtypeStruct((width // 2, patches), bf16),
            jax.ShapeDtypeStruct((width // 2, patches), bf16),
            heads_shape,
            wide_shape,
            wide_shape,
        ],
        [pltpu.VMEM((width, block), f32), pltpu.VMEM((width, block), bf16)],
        cost(2 * patches * width * (width + 3 * cols + 256), 16 * patches * width),
        "front",
        pixels, score_high, score_low, real, ev_front, agg_out, gain_one, bias_one, *qkv_parts,
    )

    def attend(distance):
        return pl.pallas_call(
            attend_kernel,
            grid=(1,),
            in_specs=[
                pl.BlockSpec((here, mine, size), lambda i: (0, distance, 0)),
                whole(keys.shape),
                whole(values.shape),
            ],
            out_specs=[whole((mine, cols)), whole((here, mine, 4 * size))],
            out_shape=[
                jax.ShapeDtypeStruct((mine, cols), bf16),
                jax.ShapeDtypeStruct((here, mine, 4 * size), bf16),
            ],
            compiler_params=params(),
            cost_estimate=cost(
                4 * mine * patches * here * 256, 4 * patches * cols * 2, mine * patches * here
            ),
            name=f"attend{distance}",
        )(queries, keys, values)

    attended_by, aug_by, arrived = [None] * n_var, [None] * n_var, [None] * n_var
    for distance in reversed(range(n_var)):
        attended_by[distance], aug_by[distance] = attend(distance)
        arrived[distance] = (
            send(attended_by[distance], distance) if distance else attended_by[distance]
        )
    if not lanes_fit:
        arrived = [canonical(arrived).transpose(1, 0, 2).reshape(mine, width)]

    cot = cotangent[0]
    tile = 2 * hidden_width // n_item
    row_f32 = jax.ShapeDtypeStruct((mine, width), f32)
    row_bf16 = jax.ShapeDtypeStruct((mine, width), bf16)
    row_spec = whole((mine, width))
    tall_spec = whole((width, mine))
    tall_bf16 = jax.ShapeDtypeStruct((width, mine), bf16)
    piece_spec = whole((mine, cols))
    (
        output, attended_t, normed_two_t, active_send, active_keep, g_hidden, g_stream, g_stream_low,
        gains_two,
        *g_attended,
    ) = call(
        partial(mlp_kernel, len(arrived), n_var),
        (hidden_width // tile,),
        [whole(piece.shape) for piece in arrived]
        + [
            row_spec,
            whole((width, width)),
            whole(gain_two.shape),
            whole(bias_two.shape),
            row_spec,
            pl.BlockSpec((width, tile), lambda i, _: (0, i)),
            pl.BlockSpec((tile, width), lambda i, _: (i, 0)),
        ],
        [
            row_spec,
            tall_spec,
            tall_spec,
            pl.BlockSpec((tile // 2, mine), lambda i, _: (i, 0)),
            pl.BlockSpec((tile // 2, mine), lambda i, _: (i, 0)),
            pl.BlockSpec((mine, tile), lambda i, _: (0, i)),
            row_spec,
            row_spec,
            whole((2, width)),
        ]
        + [piece_spec] * n_var,
        [
            row_bf16,
            tall_bf16,
            tall_bf16,
            jax.ShapeDtypeStruct((hidden_width // 2, mine), bf16),
            jax.ShapeDtypeStruct((hidden_width // 2, mine), bf16),
            jax.ShapeDtypeStruct((mine, hidden_width), bf16),
            row_f32,
            row_bf16,
            jax.ShapeDtypeStruct((2, width), f32),
        ]
        + [jax.ShapeDtypeStruct((mine, cols), bf16)] * n_var,
        [
            pltpu.VMEM((mine, width), bf16),
            pltpu.VMEM((mine, width), bf16),
            pltpu.VMEM((mine, width), f32),
            pltpu.VMEM((mine, width), f32),
            pltpu.VMEM((mine, 1), f32),
            pltpu.VMEM((mine, width), f32),
            pltpu.VMEM((mine, width), f32),
            pltpu.VMEM((tile, mine), bf16),
        ],
        cost(
            2 * mine * width * (4 * hidden_width + 2 * width),
            4 * width * hidden_width + 16 * mine * width,
        ),
        "mlp",
        *arrived, merged, attn_proj, gain_two, bias_two, cot, mlp_in, mlp_out,
    )
    g_heads = [g_attended[0]] + [send(g_attended[d], d) for d in range(1, n_var)]

    kept_rows = n_z * shard

    def pair_product(tall, grads):
        return dot(tall, grads).astype(bf16)

    def pair_own(tall, grads, got):
        return (dot(tall, grads) + got.astype(f32)).astype(bf16)

    def column_block(array, start=0, total=None):
        rows = array.shape[0]
        total = total or array.shape[1]
        span = total // n_var
        if span % 128 == 0:
            return array, pl.BlockSpec((rows, span), lambda j, at: (0, start // span + (at[0] ^ j)))
        cut = array[:, start : start + total]
        cut = jnp.take(cut.reshape(rows, n_var, span).transpose(1, 0, 2), rel, axis=0)
        return cut, pl.BlockSpec((None, rows, span), lambda j, at: (j, 0, 0))

    def pair_send_two(main, side):
        spec = pl.BlockSpec((n_z, None, shard, mine), lambda j, at: (0, 1 - at[1], 0, 0))
        tiles = hidden_width // width
        return call(
                send_kernel,
                (tiles + 1,),
                [
                    spec,
                    pl.BlockSpec((mine, width), lambda j, at: (0, jnp.minimum(j, tiles - 1))),
                    spec,
                    whole((mine, width)),
                ],
                pl.BlockSpec((kept_rows, width), lambda j, at: (0, j)),
                jax.ShapeDtypeStruct((kept_rows, hidden_width + width), bf16),
                [],
                cost(2 * kept_rows * mine * (hidden_width + width), 24 * kept_rows * width, share=2),
                "send",
                main[0].reshape(n_z, 2, shard, mine), main[1],
                side[0].reshape(n_z, 2, shard, mine), side[1],
            )

    def pair_keep(main, side, got):
        args, specs, start = [], [], 0
        for tall, grads in (main, side):
            args.append(tall.reshape(n_z, 2, shard, mine))
            specs.append(pl.BlockSpec((n_z, None, shard, mine), lambda j, at: (0, at[1], 0, 0)))
            for array, spec in (column_block(grads), column_block(got, start, grads.shape[1])):
                args.append(array)
                specs.append(spec)
            start += grads.shape[1]
        main_span, side_span = main[1].shape[1] // n_var, side[1].shape[1] // n_var
        first = 3 * main_span // 4
        spans = [first] * n_var + [main_span - first + side_span] * n_var
        outs = call(
            partial(keep_kernel, n_var),
            (n_var,),
            specs,
            [whole((kept_rows, span)) for span in spans],
            [jax.ShapeDtypeStruct((kept_rows, span), bf16) for span in spans],
            [],
            cost(
                2 * kept_rows * mine * (main_span + side_span) * n_var, 24 * kept_rows * main_span, share=2
            ),
            "keep",
            *args,
        )
        return outs[:n_var], outs[n_var:]

    def add_all(first, *others):
        total = first.astype(f32)
        for other in others:
            total = total + other.astype(f32)
        return total.astype(bf16)

    def exchange(pieces):
        return [pieces[0]] + [send(pieces[d], d) for d in range(1, n_var)]


    main, side = (normed_two_t, g_hidden), (attended_t, g_stream_low)
    sent = pair_send_two(main, side)
    sent, g_heads, active_send = lax.optimization_barrier((sent, g_heads, active_send))
    got = swap_core(sent)
    got_mlp_out = swap_core(pair_product(active_send, cot))
    first, second = pair_keep(main, side, got)
    active_keep, first, second = lax.optimization_barrier((active_keep, first, second))
    first = exchange(first)
    g_mlp_out = pair_own(active_keep, cot, got_mlp_out)
    mlp_out_rows = lax.psum_scatter(g_mlp_out, "z", scatter_dimension=0, tiled=True)
    g_heads, _ = lax.optimization_barrier((g_heads, g_mlp_out))

    group = min(2, here)
    parts = here // group
    gcols = group * size
    back_block = min(1024, patches)

    def attend_back(part, queries, extra):
        group_spec = pl.BlockSpec((group, back_block, 2 * size), lambda i: (part, i, 0))
        side_spec = pl.BlockSpec((mine, gcols), lambda i: (0, part))
        piece_cols = 3 * gcols + sum(array.shape[1] for array in extra[:1])
        full, *pieces = pl.pallas_call(
            partial(attend_back_kernel, n_var, len(extra)),
            grid=(patches // back_block,),
            in_specs=[whole(array.shape) for array in extra]
            + [
                pl.BlockSpec((group, patches, size), lambda i: (part, 0, 0)),
                group_spec,
                group_spec,
            ]
            + [pl.BlockSpec((group, mine, 4 * size), lambda i: (part, 0, 0))] * n_var
            + [side_spec] * (2 * n_var),
            out_specs=[whole((patches, 3 * gcols))] + [whole((mine, piece_cols))] * n_var,
            out_shape=[jax.ShapeDtypeStruct((patches, 3 * gcols), bf16)]
            + [jax.ShapeDtypeStruct((mine, piece_cols), bf16)] * n_var,
            scratch_shapes=[
                pltpu.VMEM((group, patches, 2 * size), bf16),
                pltpu.VMEM((group, size, patches), f32),
                pltpu.VMEM((group, back_block, patches), bf16),
                pltpu.VMEM((group, back_block, patches), bf16),
            ],
            compiler_params=params(),
            cost_estimate=cost(
                10 * patches * patches * group * 256, 8 * patches * gcols * 2, patches * patches * group
            ),
            name=f"attend_back{part}",
        )(*extra, queries, keys, values, *aug_by, *attended_by, *g_heads)
        return full, pieces

    ride = kept_rows == mine and parts > 1
    g_qkv, packed_pieces = [], []
    for part in range(parts):
        full, pieces = attend_back(part, queries, second if ride and part == 0 else [])
        if part == 0:
            full, first = lax.optimization_barrier((full, first))
            first_sum = add_all(*first)
        if part < parts - 1:
            product = pair_product(normed_send, full)
            queries, first_sum, product = lax.optimization_barrier((queries, first_sum, product))
            g_qkv.append((full, product))
        if part == parts - 1:
            pieces, packed_pieces = lax.optimization_barrier((pieces, packed_pieces))
        packed_pieces += exchange(pieces)
    if ride:
        second = [piece[:, 3 * gcols :] for piece in packed_pieces[:n_var]]
    else:
        second = exchange(second)
    g_qkv.append((full, pair_product(normed_send, full)))
    second_sum = add_all(*second)
    columns = [first_sum, second_sum]
    columns += [pair_own(normed_keep, full, swap_core(product)) for full, product in g_qkv]
    both_sum = jnp.concatenate(columns, axis=1)
    def my_slice(array, axis):
        return lax.dynamic_slice_in_dim(array, item * shard, shard, axis=axis)

    final_in = [my_slice(tables, 1).T, spread, table_keys, my_slice(agg_value, 0), my_slice(query_keys, 0)]
    packed_pieces, both_sum, final_in = lax.optimization_barrier((packed_pieces, both_sum, final_in))
    both_rows = lax.psum_scatter(both_sum, "z", scatter_dimension=0, tiled=True)
    count = n_var
    if not lanes_fit:
        packed = [
            canonical(packed_pieces[part * n_var : (part + 1) * n_var]) for part in range(parts)
        ]
        packed = jnp.stack(packed, axis=0).reshape(parts, n_var, mine, 3, gcols)
        packed_pieces = [packed.transpose(2, 3, 1, 0, 4).reshape(mine, 3 * width)]
        count, parts = 1, 1
    packed_cols = 3 * gcols if lanes_fit else 3 * width

    row_block = pl.BlockSpec((block, width), lambda i, _: (i, 0))
    table_rows = -(-(depth + 4) // 16) * 16
    late_rows = kept_rows + table_rows
    g_fields, late_send, late_keep = call(
        partial(back_kernel, count, parts, n_z),
        (own,),
        [pl.BlockSpec((block, packed_cols), lambda i, _: (i, 0)) for piece in packed_pieces]
        + [
            whole(attn_qkv.shape),
            row_block,
            whole(gain_one.shape),
            row_block,
            whole(agg_out.shape),
            pl.BlockSpec((depth, block), lambda i, _: (0, i)),
            whole(score_high.shape),
            whole(score_low.shape),
            whole((depth, HEADS * slots)),
            whole((depth, HEADS * slots)),
            whole(real.shape),
            whole(ev_back.shape),
            pl.BlockSpec((width, block), lambda i, _: (0, i)),
            whole((2, width)),
        ],
        [
            pl.BlockSpec((depth, block), lambda i, _: (0, i)),
            whole((late_rows + HEADS, width)),
            whole((late_rows + HEADS, width)),
        ],
        [
            jax.ShapeDtypeStruct((depth, mine), bf16),
            jax.ShapeDtypeStruct((late_rows + HEADS, width), bf16),
            jax.ShapeDtypeStruct((late_rows + HEADS, width), f32),
        ],
        [
            pltpu.VMEM((HEADS * slots, block), bf16),
            pltpu.VMEM((block, 3 * width), bf16),
            pltpu.VMEM((table_rows, width), f32),
            pltpu.VMEM((depth, HEADS * slots), f32),
            pltpu.VMEM((width, width), f32),
        ],
        cost(2 * mine * width * 4 * width, 8 * width * width + 20 * mine * width),
        "back",
        *packed_pieces, attn_qkv, merged, gain_one, g_stream, agg_out, pixels, score_high, score_low,
        score_high_t, score_low_t, real, ev_back, agg_values_t, gains_two,
    )

    late_send, mlp_out_rows = lax.optimization_barrier((late_send, mlp_out_rows))
    out_block = mlp_out_rows.shape[0] // n_var
    mlp_out_by = exchange(
        [
            lax.dynamic_slice_in_dim(mlp_out_rows, (me ^ d) * out_block, out_block, axis=0)
            for d in range(n_var)
        ]
    )
    mlp_out_rows = add_all(*mlp_out_by).reshape(shard, -1)

    late_got = swap_core(late_send)
    late_span = width // n_var
    n_blocks = -(-depth // late_span)
    n_spec = pl.BlockSpec((HEADS, n_blocks * late_span), lambda j, at: (late_rows // HEADS, 0))
    sum_rows = late_rows + n_blocks * HEADS
    f_rows = -(-channels * vars_here // 16) * 16
    piece_rows = sum_rows + f_rows * (mine // late_span)
    late_args = [late_keep, late_got]
    if late_span % 128:
        late_args = [
            jnp.take(array.reshape(-1, n_var, late_span).transpose(1, 0, 2), rel, axis=0)
            for array in late_args
        ]
    late_pieces = call(
        partial(pair_kernel, n_var, channels, vars_here, late_rows),
        (1,),
        [whole(array.shape) for array in late_args] + [n_spec, n_spec, whole((depth, mine))],
        [whole((piece_rows, late_span))] * n_var,
        [jax.ShapeDtypeStruct((piece_rows, late_span), bf16)] * n_var,
        [],
        cost(piece_rows * width, 8 * piece_rows * width),
        "late_pair",
        *late_args, late_keep, late_got, g_fields,
    )
    late_pieces = exchange(late_pieces)
    late_pieces, both_rows = lax.optimization_barrier((late_pieces, both_rows))
    rows_all = jnp.concatenate([both_rows, mlp_out_rows], axis=1)
    halves = 1 if n_var == 4 and lanes_fit else 0
    if halves:
        near = [send(rows_all, 1), send(rows_all, 2)]
    else:
        rows_all = list(lax.all_gather(rows_all, "var", axis=0))
    z_rows = shard + table_rows + n_blocks * HEADS
    *z_pieces, fields_grad = call(
        partial(z_pieces_kernel, n_var, shard, n_z),
        (1,),
        [whole((piece_rows, late_span))] * n_var,
        [whole((z_rows, late_span))] * n_z + [whole((f_rows, patches))],
        [jax.ShapeDtypeStruct((z_rows, late_span), bf16)] * n_z
        + [jax.ShapeDtypeStruct((f_rows, patches), f32)],
        [pltpu.VMEM((sum_rows, late_span), bf16)],
        cost(piece_rows * width, 2 * piece_rows * width),
        "late_z",
        *late_pieces,
    )
    z_pieces = [z_pieces[0]] + [send_z(z_pieces[d], d) for d in range(1, n_z)]
    late_rows_mine, n_all = pl.pallas_call(
        partial(z_sum_kernel, n_z),
        out_shape=[
            jax.ShapeDtypeStruct((shard + table_rows, late_span), bf16),
            jax.ShapeDtypeStruct((HEADS, n_blocks * late_span), f32),
        ],
        compiler_params=params(),
        cost_estimate=cost(z_rows * width, 2 * z_rows * width),
        name="late_sum",
    )(*z_pieces)

    fields_grad = fields_grad[: channels * vars_here].reshape(1, vars_here, channels, patches)
    if halves:
        late_rows_mine, near = lax.optimization_barrier((late_rows_mine, near))
        half = rows_all.shape[1] // 2
        rows_all = [rows_all] + near + [send(near[0][:, :half], 2), send(near[1][:, half:], 1)]
    late_by = exchange([late_rows_mine] * n_var)
    if late_span % 128:
        late_by = [canonical(late_by).transpose(1, 0, 2).reshape(shard + table_rows, width)]
    small_shapes = [(1, width), (channels * vars_here, shard), (vars_here, shard), (8, width)]
    final_in = [n_all] + final_in
    agg_out_grad, agg_value_grad, agg_key_grad, query_row, embed_weight_grad, var_embed_grad, gains = call(
        partial(final_kernel, len(late_by)),
        (1,),
        [whole(array.shape) for array in late_by + final_in],
        [whole((shard, width))] * 3
        + [whole(shape) for shape in small_shapes],
        [jax.ShapeDtypeStruct((shard, width), f32)] * 3
        + [jax.ShapeDtypeStruct(shape, f32) for shape in small_shapes],
        [pltpu.VMEM((table_rows, width), f32)],
        cost(2 * shard * width * 3 * depth, 12 * shard * width),
        "final",
        *late_by, *final_in,
    )
    gains = my_slice(gains, 1)
    agg_query_grad = my_slice(query_row[0], 0) * scale
    embed_weight_grad = embed_weight_grad.reshape(vars_here, channels, shard)

    row_shapes = [
        jax.ShapeDtypeStruct((shard, hidden_width), f32),
        jax.ShapeDtypeStruct((shard, width), f32),
        jax.ShapeDtypeStruct((shard, 3 * width), f32),
        jax.ShapeDtypeStruct((n_var, shard, out_block * width // shard), f32),
    ]
    mlp_in_grad, attn_proj_grad, attn_qkv_grad, mlp_out_grad = call(
        partial(assemble_kernel, n_var, here // group, gcols, halves),
        (1,),
        [whole(array.shape) for array in rows_all],
        [whole(row.shape) for row in row_shapes],
        row_shapes,
        [],
        cost(shard * 9 * width, 6 * shard * 9 * width),
        "assemble",
        *rows_all,
    )
    mlp_out_grad = mlp_out_grad.reshape(n_var * out_block, width)
    return (
        output[None],
        fields_grad,
        embed_weight_grad,
        var_embed_grad,
        agg_query_grad,
        agg_key_grad,
        agg_value_grad,
        agg_out_grad,
        gains[0],
        gains[1],
        attn_qkv_grad,
        attn_proj_grad,
        gains[2],
        gains[3],
        mlp_in_grad,
        mlp_out_grad,
    )


def solution(mesh):
    n_var, n_item = mesh.shape["var"], mesh.shape["item"]
    items = ("z", "core")
    return jax.shard_map(
        partial(per_device, n_var, n_item // 2),
        mesh=Mesh(mesh.devices.reshape(n_var, n_item // 2, 2), ("var", "z", "core")),
        in_specs=(
            P(items, "var", None, None),
            P(items, None),
            P("var", None, None),
            P("var", None),
            P(),
            P(),
            P(),
            P(),
            P(),
            P(),
            P(),
            P(),
            P(),
            P(),
            P(),
            P(),
            P(items, "var", None),
        ),
        out_specs=(
            P(items, "var", None),
            P(items, "var", None, None),
            P("var", None, items),
            P("var", items),
            P(items),
            P(items, None),
            P(items, None),
            P(items, None),
            P(items),
            P(items),
            P(items, None),
            P(items, None),
            P(items),
            P(items),
            P(items, None),
            P(items, None),
        ),
        check_vma=False,
    )
```

```python
from functools import partial

import jax
import jax.numpy as jnp
from jax import lax
from jax.experimental import pallas as pl
from jax.experimental.pallas import tpu as pltpu
from jax.sharding import Mesh
from jax.sharding import PartitionSpec as P

HEADS = 16
TABLES = 5

epsilon = 1e-05
masked_score = -1e30
highest = lax.Precision.HIGHEST
f32 = jnp.float32
bf16 = jnp.bfloat16
COST = 0.05
VMEM_BYTES = 56 * 1024 * 1024
LOG2E = 1.4426950408889634


def dot(a, b):
    return lax.dot_general(a, b, (((1,), (0,)), ((), ())), preferred_element_type=f32)


def dot_nt(a, b):
    return lax.dot_general(a, b, (((1,), (1,)), ((), ())), preferred_element_type=f32)


def dot_tn(a, b):
    return lax.dot_general(a, b, (((0,), (0,)), ((), ())), preferred_element_type=f32)


def split_two(wide):
    high = wide.astype(bf16)
    return high, (wide - high.astype(f32)).astype(bf16)


def split_three(wide):
    high, rest = split_two(wide)
    low = wide - high.astype(f32) - rest.astype(f32)
    return high, rest, low.astype(bf16)


def columns(parts, rows, width):
    lane = lax.broadcasted_iota(jnp.int32, (rows, width), 1)
    out = jnp.zeros((rows, width), f32)
    for i, part in enumerate(parts):
        out = jnp.where(lane == i, part.astype(f32), out)
    return out.astype(bf16)


def whole(shape):
    return pl.BlockSpec(shape, lambda *_: (0,) * len(shape))


def params(vmem=VMEM_BYTES):
    return pltpu.CompilerParams(vmem_limit_bytes=vmem)


def cost(flops, bytes_accessed, transcendentals=0, share=COST):
    return pl.CostEstimate(
        flops=int(flops * share), bytes_accessed=int(bytes_accessed * share), transcendentals=0
    )


def norm_parts(stream):
    centred = stream - jnp.mean(stream, axis=-1, keepdims=True)
    inverse = lax.rsqrt(jnp.mean(centred * centred, axis=-1, keepdims=True) + epsilon)
    return centred * inverse, inverse


def norm_back(upstream, unit_rows, inverse, gain):
    scaled = upstream * gain
    return inverse * (
        scaled
        - jnp.mean(scaled, axis=-1, keepdims=True)
        - unit_rows * jnp.mean(scaled * unit_rows, axis=-1, keepdims=True)
    )


def variable_probs(pixel_rows, score_high, score_low, real, slots):
    scores = dot(score_high, pixel_rows) + dot(score_low, pixel_rows)
    scores = scores.reshape(HEADS, slots, pixel_rows.shape[1])
    scores = jnp.where(real[None] > 0, scores, masked_score)
    powers = jnp.exp(scores - jnp.max(scores, axis=1, keepdims=True))
    return powers / jnp.sum(powers, axis=1, keepdims=True)


def prep_kernel(count, vars_here, patches, *refs):
    place_ref = refs[0]
    pieces = refs[1 : 1 + count]
    query_ref, key_ref, value_ref = refs[1 + count : 4 + count]
    (
        pix_ref, tables_ref, shi_ref, slo_ref, sthi_ref, stlo_ref, front_ref, back_ref, keys_ref,
        qk_ref, spread_ref, all_s,
    ) = refs[4 + count :]
    me = place_ref[0]
    depth, width = tables_ref.shape
    slots = depth // TABLES
    size = width // HEADS
    rows = TABLES * vars_here
    total = None
    for d in range(count):
        row = lax.broadcasted_iota(jnp.int32, (depth, rows), 0)
        col = lax.broadcasted_iota(jnp.int32, (depth, rows), 1)
        want = (col % TABLES) * slots + (me ^ d) * vars_here + col // TABLES
        part = dot(jnp.where(row == want, 1.0, 0.0).astype(bf16), pieces[d][...])
        total = part if total is None else total + part
    all_s[...] = total.astype(bf16)
    mine = patches // count
    for d in range(count):
        at = pl.multiple_of((me ^ d) * mine, mine)
        pix_ref[:, d * mine : (d + 1) * mine] = all_s[:, pl.ds(at, mine)]
    tables = all_s[:, patches:]
    tables_ref[...] = tables
    head = lax.broadcasted_iota(jnp.int32, (HEADS, width), 0)
    same = lax.broadcasted_iota(jnp.int32, (HEADS, width), 1) // size == head
    spread = jnp.where(same, query_ref[...].astype(f32), 0.0)
    scale = size ** (-0.5)
    spread_ref[...] = (spread * scale).astype(bf16)
    query_keys = (dot_nt(key_ref[...], spread.astype(bf16)) * scale).astype(bf16)
    qk_ref[...] = query_keys
    halves = split_two(dot(tables, query_keys))
    wide = HEADS * slots
    picks = lax.broadcasted_iota(jnp.int32, (wide, HEADS), 0) // slots
    picks = jnp.where(picks == lax.broadcasted_iota(jnp.int32, (wide, HEADS), 1), 1.0, 0.0).astype(bf16)
    for half, tall, flat in zip(halves, (shi_ref, slo_ref), (sthi_ref, stlo_ref)):
        row = lax.broadcasted_iota(jnp.int32, (wide, depth), 0) % slots
        col = lax.broadcasted_iota(jnp.int32, (wide, depth), 1) % slots
        tall[...] = jnp.where(row == col, dot_nt(picks, half), 0.0).astype(bf16)
        row = lax.broadcasted_iota(jnp.int32, (depth, wide), 0) % slots
        col = lax.broadcasted_iota(jnp.int32, (depth, wide), 1) % slots
        flat[...] = jnp.where(row == col, dot_nt(half, picks), 0.0).astype(bf16)
    mixed = dot(tables, value_ref[...])
    high, low = split_two(mixed)
    high_wide, low_wide = high.astype(f32), low.astype(f32)
    front_ref[...] = jnp.concatenate([high_wide, high_wide, low_wide], axis=0).T.astype(bf16)
    both = jnp.concatenate([high, low], axis=0)
    for h in range(HEADS):
        back_ref[h] = both[:, h * size : (h + 1) * size]
    keys_ref[...] = dot(tables, key_ref[...])


def front_kernel(
    own_blocks, n_z, place_ref, pix_ref, shi_ref, slo_ref, real_ref, ev_ref, out_w_ref, gain_ref,
    bias_ref, wq_ref, wk_ref, wv_ref,
    values_ref, merged_ref, send_ref, keep_ref, q_ref, k_ref, v_ref, flat_ref, tall_s,
):
    slots = real_ref.shape[0]
    pixel_rows = pix_ref[...]
    probs = variable_probs(pixel_rows, shi_ref[...], slo_ref[...], real_ref[...], slots)
    weights = probs.astype(bf16).astype(f32)
    pixels = pixel_rows.astype(f32).reshape(TABLES, slots, -1)
    size = ev_ref.shape[0] // HEADS
    for h in range(HEADS):
        mixed = (weights[h][None] * pixels).reshape(pixel_rows.shape)
        high, low = split_two(mixed)
        flat_ref[h * size : (h + 1) * size, :] = dot(
            ev_ref[h * size : (h + 1) * size, :], jnp.concatenate([high, low, high], axis=0)
        )
    values = flat_ref[...].astype(bf16)
    merged = dot(values.T, out_w_ref[...])

    @pl.when(pl.program_id(0) < own_blocks)
    def _():
        values_ref[...] = values
        merged_ref[...] = merged

    unit_rows, _ = norm_parts(merged)
    normed = (unit_rows * gain_ref[...] + bias_ref[...]).astype(bf16)
    tall_s[...] = normed.T
    core, shard = place_ref[1], tall_s.shape[0] // (2 * n_z)
    for zz in range(n_z):
        at = slice(zz * shard, (zz + 1) * shard)
        keep_ref[at] = tall_s[pl.ds(pl.multiple_of((2 * zz + core) * shard, shard), shard), :]
        send_ref[at] = tall_s[pl.ds(pl.multiple_of((2 * zz + 1 - core) * shard, shard), shard), :]
    queries = dot(normed, wq_ref[...]).astype(bf16).astype(f32) * size ** (-0.5)
    keys = dot(normed, wk_ref[...])
    values = dot(normed, wv_ref[...])
    for h in range(q_ref.shape[0]):
        at = h * size
        q_ref[h] = queries[:, at : at + size].astype(bf16)
        k_ref[h] = keys[:, at : at + size].astype(bf16)
        v_ref[h] = values[:, at : at + size].astype(bf16)


def attend_kernel(q_ref, k_ref, v_ref, out_ref, lse_ref):
    here, rows, size = q_ref.shape
    block = min(512, rows)
    pieces = [(h, at) for at in range(0, rows, block) for h in range(here)]

    def scores_of(piece):
        h, at = piece
        return dot_nt(q_ref[h, at : at + block], k_ref[h])

    def finish(piece, powers, top, total):
        h, at = piece
        mixed = dot(powers, v_ref[h]) / total
        lse = jnp.broadcast_to(top + jnp.log(total), (block, 128)).T[0:1]
        return mixed.astype(bf16), lse

    done, waiting = {}, None
    scores = scores_of(pieces[0])
    for i, piece in enumerate(pieces):
        later = scores_of(pieces[i + 1]) if i + 1 < len(pieces) else None
        top = jnp.max(scores, axis=-1, keepdims=True)
        powers = jnp.exp(scores - top)
        total = jnp.sum(powers, axis=-1, keepdims=True)
        if waiting is not None:
            done[waiting[0]] = finish(*waiting)
        waiting = (piece, powers.astype(bf16), top, total)
        scores = later
    done[waiting[0]] = finish(*waiting)
    for h, at in pieces:
        lse_ref[h, :, at : at + block] = done[h, at][1]
    for at in range(0, rows, block):
        out_ref[at : at + block] = jnp.concatenate([done[h, at][0] for h in range(here)], axis=-1)


def attend_back_kernel(count, extra, rows_first, *refs):
    extra_refs, refs = refs[:extra], refs[extra:]
    q_ref, k_ref, v_ref = refs[:3]
    lse_refs = refs[3 : 3 + count]
    out_refs = refs[3 + count : 3 + 2 * count]
    up_refs = refs[3 + 2 * count : 3 + 3 * count]
    full_ref = refs[3 + 3 * count]
    piece_refs = refs[4 + 3 * count : 4 + 4 * count]
    up_heads, total_rows, lse_rows, gq_ref, prob_s, slope_s = refs[4 + 4 * count :]
    step = pl.program_id(0)
    here, patches, size = q_ref.shape
    block = k_ref.shape[1]
    width = here * size
    mine = patches // count

    @pl.when(step == 0)
    def _():
        for h in range(here):
            at = h * size
            for d in range(count):
                rows = slice(d * mine, (d + 1) * mine)
                upstream = up_refs[d][:, at : at + size]
                up_heads[h, rows] = upstream
                product = upstream.astype(f32) * out_refs[d][:, at : at + size].astype(f32)
                total_rows[h, :, rows] = jnp.sum(product.T, axis=0, keepdims=True)
                lse_rows[h, :, rows] = lse_refs[d][h]
            gq_ref[h] = jnp.zeros(gq_ref.shape[1:], f32)

    chunk = min(256, patches)
    key_parts, value_parts = [], []
    for h in range(here):
        keys, values = k_ref[h], v_ref[h]
        for at in range(0, patches, chunk):
            span = slice(at, at + chunk)
            probs = jnp.exp(dot_nt(keys, q_ref[h, span]) - lse_rows[h, :, span])
            prob_s[h, :, span] = probs.astype(bf16)
            grads = dot_nt(values, up_heads[h, span])
            slope_s[h, :, span] = (probs * (grads - total_rows[h, :, span])).astype(bf16)
        value_parts.append(dot(prob_s[h], up_heads[h]))
        key_parts.append(dot(slope_s[h], q_ref[h]))
        if rows_first:
            gq_ref[h] += dot_tn(slope_s[h], keys)
        else:
            gq_ref[h] += dot(keys.astype(f32).T.astype(bf16), slope_s[h])
    rows = pl.ds(pl.multiple_of(step * block, block), block)
    full_ref[rows, width : 2 * width] = jnp.concatenate(key_parts, axis=-1).astype(bf16)
    full_ref[rows, 2 * width :] = jnp.concatenate(value_parts, axis=-1).astype(bf16)

    @pl.when(step == pl.num_programs(0) - 1)
    def _():
        scale = size ** (-0.5)
        query_parts = [gq_ref[h] if rows_first else gq_ref[h].T for h in range(here)]
        full_ref[:, :width] = (jnp.concatenate(query_parts, axis=-1) * scale).astype(bf16)
        for d in range(count):
            piece_refs[d][:, : 3 * width] = full_ref[d * mine : (d + 1) * mine, :]

    if extra:

        @pl.when(step == 0)
        def _():
            for d in range(count):
                piece_refs[d][:, 3 * width :] = extra_refs[d][...]


def mlp_kernel(pieces, count, *refs):
    place_ref = refs[0]
    att_refs = refs[1 : 1 + pieces]
    merged_ref, proj_ref, gain_ref, bias_ref, cot_ref, win_ref, wout_ref = refs[1 + pieces : 8 + pieces]
    outs = refs[8 + pieces :]
    (
        out_ref, att_t_ref, normed_t_ref, send_ref, keep_ref, ghid_ref, gstream_ref, glow_ref,
        gains_ref,
    ) = outs[:9]
    gatt_refs = outs[9 : 9 + count]
    att_s, normed_s, stream_s, unit_s, inv_s, out_s, gn_s, tall_s = outs[9 + count :]
    step = pl.program_id(0)
    me = place_ref[0]
    cols = gatt_refs[0].shape[1]

    @pl.when(step == 0)
    def _():
        if pieces == 1:
            attended = att_refs[0][...]
        else:
            for d in range(pieces):
                att_s[:, pl.ds(pl.multiple_of((me ^ d) * cols, cols), cols)] = att_refs[d][...]
            attended = att_s[...]
        att_t_ref[...] = attended.T
        stream = merged_ref[...] + dot(attended, proj_ref[...])
        unit_rows, inverse = norm_parts(stream)
        stream_s[...] = stream
        unit_s[...] = unit_rows
        inv_s[...] = inverse
        normed = (unit_rows * gain_ref[...] + bias_ref[...]).astype(bf16)
        normed_s[...] = normed
        normed_t_ref[...] = normed.T
        out_s[...] = jnp.zeros_like(out_s)
        gn_s[...] = jnp.zeros_like(gn_s)

    tile = ghid_ref.shape[1]
    sub = min(256, tile)
    spans = [slice(at, at + sub) for at in range(0, tile, sub)]
    normed_rows, upstream_rows = normed_s[...], cot_ref[...]

    def products(span):
        return dot(normed_rows, win_ref[:, span]), dot_nt(upstream_rows, wout_ref[span, :])

    def shape(hidden, g_active):
        below = 0.5 + 0.5 * lax.erf(hidden * (0.5**0.5))
        density = jnp.exp(-0.5 * hidden * hidden) * ((2.0 * jnp.pi) ** (-0.5))
        return (hidden * below).astype(bf16), (g_active * (below + hidden * density)).astype(bf16)

    actives, grads, sums = [], [], []

    def add(first, last):
        span = slice(spans[first].start, spans[last].stop)
        active = jnp.concatenate(actives[first : last + 1], axis=1)
        grad = jnp.concatenate(grads[first : last + 1], axis=1)
        sums.append((dot(active, wout_ref[span, :]), dot_nt(grad, win_ref[:, span])))

    ready = products(spans[0])
    for i, span in enumerate(spans):
        later = products(spans[i + 1]) if i + 1 < len(spans) else None
        if i == len(spans) // 2 + 1:
            add(0, len(spans) // 2 - 1)
        active, grad = shape(*ready)
        actives.append(active)
        grads.append(grad)
        ready = later
    add(len(spans) // 2 if sums else 0, len(spans) - 1)
    for span, active, grad in zip(spans, actives, grads):
        ghid_ref[:, span] = grad
        tall_s[span, :] = active.T
    half = tile // 2
    core = place_ref[1]
    send_ref[...] = tall_s[pl.ds(pl.multiple_of((1 - core) * half, half), half), :]
    keep_ref[...] = tall_s[pl.ds(pl.multiple_of(core * half, half), half), :]
    out_s[...] += sum(pair[0] for pair in sums)
    gn_s[...] += sum(pair[1] for pair in sums)

    @pl.when(step == pl.num_programs(0) - 1)
    def _():
        out_ref[...] = (stream_s[...] + out_s[...]).astype(bf16)
        upstream = gn_s[...].astype(bf16).astype(f32)
        unit_rows = unit_s[...]
        g_stream = cot_ref[...].astype(f32) + norm_back(
            upstream, unit_rows, inv_s[...], gain_ref[...]
        )
        gstream_ref[...] = g_stream
        low = g_stream.astype(bf16)
        glow_ref[...] = low
        for d in range(count):
            rows = pl.ds(pl.multiple_of((me ^ d) * cols, cols), cols)
            gatt_refs[d][...] = dot_nt(low, proj_ref[rows, :]).astype(bf16)
        gains_ref[0:1, :] = jnp.sum(upstream * unit_rows, axis=0, keepdims=True)
        gains_ref[1:2, :] = jnp.sum(upstream, axis=0, keepdims=True)


def send_kernel(place_ref, main_rows, main_cols, side_rows, side_cols, out_ref):
    last = pl.program_id(0) == pl.num_programs(0) - 1

    def product(rows_ref, cols_ref):
        tall = rows_ref[...].reshape(-1, rows_ref.shape[-1])
        return dot(tall, cols_ref[...]).astype(bf16)

    @pl.when(jnp.logical_not(last))
    def _():
        out_ref[...] = product(main_rows, main_cols)

    @pl.when(last)
    def _():
        out_ref[...] = product(side_rows, side_cols)


def keep_kernel(count, *refs):
    main_rows, main_cols, main_got, side_rows, side_cols, side_got = refs[1:7]
    outs = refs[7:]
    step = pl.program_id(0)

    def product(rows_ref, cols_ref, got_ref):
        tall = rows_ref[...].reshape(-1, rows_ref.shape[-1])
        return (dot(tall, cols_ref[...]) + got_ref[...].astype(f32)).astype(bf16)

    for d in range(count):

        @pl.when(step == d)
        def _():
            first, second = outs[d], outs[count + d]
            main = product(main_rows, main_cols, main_got)
            cut = first.shape[1]
            rest = main.shape[1] - cut
            first[...] = main[:, :cut]
            second[:, :rest] = main[:, cut:]
            second[:, rest:] = product(side_rows, side_cols, side_got)


def pair_kernel(count, channels, vars_here, late_rows, *refs):
    place_ref = refs[0]
    keep_ref, got_ref, n_keep_ref, n_got_ref, fields_ref = refs[1:6]
    outs = refs[6:]
    depth, mine = fields_ref.shape
    rows = late_rows
    span = outs[0].shape[1]
    slots = depth // TABLES
    n_blocks = n_keep_ref.shape[1] // span
    f_rows = (outs[0].shape[0] - rows - n_blocks * HEADS) // (mine // span)
    row = lax.broadcasted_iota(jnp.int32, (f_rows, depth), 0)
    col = lax.broadcasted_iota(jnp.int32, (f_rows, depth), 1)
    n_total = (n_keep_ref[...] + n_got_ref[...].astype(f32)).astype(bf16)
    for d in range(count):
        q = place_ref[0] ^ d

        def block(ref):
            if len(ref.shape) == 3:
                return ref[d, :rows].astype(f32)
            return ref[:rows, pl.ds(pl.multiple_of(q * span, span), span)].astype(f32)

        outs[d][:rows] = (block(keep_ref) + block(got_ref)).astype(bf16)
        want = (row % channels) * slots + q * vars_here + row // channels
        picks = jnp.where((want == col) & (row < channels * vars_here), 1.0, 0.0).astype(bf16)
        picked = dot(picks, fields_ref[...]).astype(bf16)
        at = rows
        for b in range(n_blocks):
            outs[d][at : at + HEADS] = n_total[:, b * span : (b + 1) * span]
            at += HEADS
        for b in range(mine // span):
            outs[d][at : at + f_rows] = picked[:, b * span : (b + 1) * span]
            at += f_rows


def z_pieces_kernel(count, shard, n_z, *refs):
    pieces, outs, fields_ref, total_s = refs[1 : 1 + count], refs[1 + count : -2], refs[-2], refs[-1]
    me, z_at = refs[0][0], refs[0][2]
    rows, span = total_s.shape
    f_rows = fields_ref.shape[0]
    mine = fields_ref.shape[1] // count
    total = pieces[0][:rows].astype(f32)
    for piece in pieces[1:]:
        total = total + piece[:rows].astype(f32)
    total_s[...] = total.astype(bf16)
    for d in range(n_z):
        start = pl.multiple_of((z_at ^ d) * shard, shard)
        outs[d][:shard] = total_s[pl.ds(start, shard), :]
        outs[d][shard:] = total_s[n_z * shard :, :]
    for d in range(count):
        blocks = [
            pieces[d][rows + b * f_rows : rows + (b + 1) * f_rows] for b in range(mine // span)
        ]
        at = pl.multiple_of((me ^ d) * mine, mine)
        fields_ref[:, pl.ds(at, mine)] = jnp.concatenate(blocks, axis=1).astype(f32)


def assemble_kernel(count, parts, size, halves, *refs):
    me = refs[0][0]
    blocks, outs = refs[1 : 1 + count + halves], refs[1 + count + halves :]
    in_ref, proj_ref, qkv_ref, out_ref = outs
    a = in_ref.shape[1] // count
    b = proj_ref.shape[1] // count
    width = proj_ref.shape[1]
    for d in range(count):
        if halves and d == count - 1:
            rows = jnp.concatenate([ref[...] for ref in blocks[d:]], axis=1)
        else:
            rows = blocks[d][...]
        rows = rows.astype(f32)
        q = me ^ d if halves else d

        def span(at, step):
            return pl.ds(pl.multiple_of(at, step) if halves else at, step)

        in_ref[:, span(q * a, a)] = rows[:, :a]
        proj_ref[:, span(q * b, b)] = rows[:, a : a + b]
        at = a + b
        for part in range(parts):
            for third in range(3):
                to = third * width + q * b + part * size
                qkv_ref[:, span(to, size)] = rows[:, at : at + size]
                at += size
        out_ref[q] = rows[:, at:]


def z_sum_kernel(count, *refs):
    pieces, (rows_ref, n_ref) = refs[:count], refs[count:]
    total = pieces[0][...].astype(f32)
    for piece in pieces[1:]:
        total = total + piece[...].astype(f32)
    rows, span = rows_ref.shape
    rows_ref[...] = total[:rows].astype(bf16)
    for b in range(n_ref.shape[1] // span):
        n_ref[:, b * span : (b + 1) * span] = total[rows + b * HEADS : rows + (b + 1) * HEADS]


def final_kernel(count, *refs):
    place_ref = refs[0]
    pieces = refs[1 : 1 + count]
    n_ref, tables_ref, spread_ref, keys_ref, value_ref, qk_ref = refs[1 + count : 7 + count]
    outg_ref, valg_ref, keyg_ref, queryg_ref, embedg_ref, varg_ref, gains_ref, m_s = refs[7 + count :]
    shard, depth = tables_ref.shape
    width = m_s.shape[1]
    for d in range(count):
        span = pieces[d].shape[1]
        at = 0 if count == 1 else pl.multiple_of((place_ref[0] ^ d) * span, span)
        outg_ref[:, pl.ds(at, span)] = pieces[d][:shard].astype(f32)
        m_s[:, pl.ds(at, span)] = pieces[d][shard:].astype(f32)
    m_low = m_s[:depth, :].astype(bf16)
    n_high, n_low = split_two(n_ref[:, :depth])
    tables = tables_ref[...]
    valg_ref[...] = dot(tables, m_low)
    g_qk = dot_nt(tables, n_high) + dot_nt(tables, n_low)
    qk_high, qk_low = split_two(g_qk)
    spread = spread_ref[...]
    keyg_ref[...] = dot(qk_high, spread) + dot(qk_low, spread)
    head_at = lax.broadcasted_iota(jnp.int32, (HEADS, width), 1) // (width // HEADS)
    same = head_at == lax.broadcasted_iota(jnp.int32, (HEADS, width), 0)
    ones = jnp.where(same, 1.0, 0.0).astype(bf16)
    n_wide = dot(n_high.astype(f32).T.astype(bf16), ones) + dot(n_low.astype(f32).T.astype(bf16), ones)
    queryg_ref[...] = jnp.sum(n_wide * keys_ref[...], axis=0, keepdims=True)
    qk = qk_ref[...]
    table_grad = split_three(
        dot_nt(m_low, value_ref[...])
        + dot_nt(n_high.astype(f32).T.astype(bf16), qk)
        + dot_nt(n_low.astype(f32).T.astype(bf16), qk)
    )
    slots = depth // TABLES
    vars_here = varg_ref.shape[0]
    for ref, first, each in ((embedg_ref, 0, TABLES - 1), (varg_ref, TABLES - 1, 1)):
        row = lax.broadcasted_iota(jnp.int32, (each * vars_here, depth), 0)
        col = lax.broadcasted_iota(jnp.int32, (each * vars_here, depth), 1)
        want = (first + row % each) * slots + place_ref[0] * vars_here + row // each
        picks = jnp.where(want == col, 1.0, 0.0).astype(bf16)
        ref[...] = sum(dot(picks, part) for part in table_grad)
    gains_ref[...] = m_s[depth : depth + 8, :]


def back_kernel(count, parts, n_z, *refs):
    place_ref = refs[0]
    piece_refs = refs[1 : 1 + count * parts]
    (
        qkv_far, merged_far, gain_ref, gs_far, out_w_far, pix_ref, shi_ref, slo_ref, sthi_ref,
        stlo_ref, real_ref, ev_ref, values_far, gains_two_ref,
        fields_ref, send_ref, keep_ref, slope_s, packed_s, m_ref, n_ref,
        qkv_s, merged_ref, gs_ref, out_w_ref, values_ref, copied,
    ) = refs[1 + count * parts :]
    width = merged_ref.shape[1]
    thirds = [
        pltpu.make_async_copy(
            qkv_far.at[:, pl.ds(third * width, width)], qkv_s.at[third], copied.at[third]
        )
        for third in range(3)
    ]
    others = [
        pltpu.make_async_copy(far, near, copied.at[3 + i])
        for i, (far, near) in enumerate(
            [
                (merged_far, merged_ref), (gs_far, gs_ref), (out_w_far, out_w_ref),
                (values_far, values_ref),
            ]
        )
    ]
    for copy in thirds + others:
        copy.start()
    slots = real_ref.shape[0]
    if count == 1:
        packed = piece_refs[0][...]
    else:
        span = piece_refs[0].shape[1] // 3
        for third in range(3):
            for part in range(parts):
                for d in range(count):
                    at = third * (count * parts) + (place_ref[0] ^ d) * parts + part
                    packed_s[:, pl.ds(pl.multiple_of(at * span, span), span)] = piece_refs[
                        part * count + d
                    ][:, third * span : (third + 1) * span]
        packed = packed_s[...]
    pixel_rows = pix_ref[...]
    probs = variable_probs(pixel_rows, shi_ref[...], slo_ref[...], real_ref[...], slots)
    weights = probs.astype(bf16).astype(f32)
    pixels = pixel_rows.astype(f32).reshape(TABLES, slots, -1)
    upstream = None
    for third, copy in enumerate(thirds):
        copy.wait()
        product = dot_nt(packed[:, third * width : (third + 1) * width], qkv_s[third])
        upstream = product if upstream is None else upstream + product
    upstream = upstream.astype(bf16).astype(f32)
    for copy in others:
        copy.wait()
    unit_rows, inverse = norm_parts(merged_ref[...])
    g_merged = gs_ref[...] + norm_back(upstream, unit_rows, inverse, gain_ref[...])
    low = g_merged.astype(bf16)
    depth = pix_ref.shape[0]
    m_ref[...] = jnp.zeros_like(m_ref)
    m_ref[depth + 2 : depth + 4, :] = gains_two_ref[...]
    m_ref[depth : depth + 1, :] = jnp.sum(upstream * unit_rows, axis=0, keepdims=True)
    m_ref[depth + 1 : depth + 2, :] = jnp.sum(upstream, axis=0, keepdims=True)
    g_values = dot_nt(low, out_w_ref[...]).astype(bf16)
    grads = dot(values_ref[...], low)
    size = ev_ref.shape[2]
    g_fields = jnp.zeros(pixels.shape, f32)
    for h in range(HEADS):
        rows = g_values[:, h * size : (h + 1) * size]
        both = dot_nt(ev_ref[h], rows)
        table = (both[:depth] + both[depth:]).reshape(pixels.shape)
        g_weights = jnp.sum(pixels * table, axis=0)
        total = jnp.sum(g_weights * probs[h], axis=0, keepdims=True)
        slope_s[h * slots : (h + 1) * slots, :] = (probs[h] * (g_weights - total)).astype(bf16)
        g_fields += weights[h][None] * table
        mixed = (weights[h][None] * pixels).reshape(pixel_rows.shape)
        pair = dot(jnp.concatenate(split_two(mixed), axis=0), rows)
        m_ref[:depth, h * size : (h + 1) * size] = pair[:depth] + pair[depth:]
    slopes = slope_s[...]
    fields_ref[...] = (
        g_fields.reshape(pixel_rows.shape) + dot(sthi_ref[...], slopes) + dot(stlo_ref[...], slopes)
    ).astype(bf16)
    n_ref[...] = dot_nt(pixel_rows, slopes)

    core = place_ref[1]
    shard = grads.shape[0] // (2 * n_z)
    for zz in range(n_z):
        at = slice(zz * shard, (zz + 1) * shard)
        even = grads[2 * zz * shard : (2 * zz + 1) * shard]
        odd = grads[(2 * zz + 1) * shard : (2 * zz + 2) * shard]
        keep_ref[at] = jnp.where(core == 0, even, odd)
        send_ref[at] = jnp.where(core == 0, odd, even).astype(bf16)
    top = n_z * shard
    middle = top + m_ref.shape[0]
    tables = m_ref[...]
    keep_ref[top:middle] = tables
    send_ref[top:middle] = tables.astype(bf16)
    columns = lax.broadcasted_iota(jnp.int32, n_ref.shape, 1)
    same = columns % slots == lax.broadcasted_iota(jnp.int32, n_ref.shape, 0) % slots
    n_high, n_low = split_two(jnp.where(same, n_ref[...], 0.0))
    heads = (HEADS, n_ref.shape[1])
    picks = lax.broadcasted_iota(jnp.int32, heads, 1) // slots
    picks = jnp.where(picks == lax.broadcasted_iota(jnp.int32, heads, 0), 1.0, 0.0).astype(bf16)
    n_rows = dot_nt(picks, n_high) + dot_nt(picks, n_low)
    keep_ref[middle:] = jnp.zeros((HEADS, keep_ref.shape[1]), f32)
    keep_ref[middle:, :depth] = n_rows
    send_ref[middle:] = keep_ref[middle:].astype(bf16)


def per_device(
    n_var, n_z, fields, var_mask, embed_weight, var_embed, agg_query, agg_key, agg_value, agg_out,
    norm1_gain, norm1_bias, attn_qkv, attn_proj, norm2_gain, norm2_bias, mlp_in, mlp_out, cotangent,
):
    n_item = 2 * n_z
    width = agg_key.shape[0]
    size = width // HEADS
    scale = size ** (-0.5)
    hidden_width = mlp_in.shape[1]
    vars_here, channels, patches = fields.shape[1:]
    slot_count = var_mask.shape[1]
    slots = -(-slot_count // 16) * 16
    mine = patches // n_var
    here = HEADS // n_var
    cols = here * size
    shard = width // n_item
    me = lax.axis_index("var")
    core = lax.axis_index("core")
    z_at = lax.axis_index("z")
    item = z_at * 2 + core
    rel = me ^ jnp.arange(n_var)
    rel_z = z_at ^ jnp.arange(n_z)
    place = jnp.stack([me, core, z_at]).astype(jnp.int32)
    lanes_fit = cols % 128 == 0

    def send(array, other):
        return lax.ppermute(array, "var", [(i, i ^ other) for i in range(n_var)])

    def send_z(array, other):
        return lax.ppermute(array, "z", [(i, i ^ other) for i in range(n_z)])

    def swap_core(array):
        return lax.ppermute(array, "core", [(0, 1), (1, 0)])

    def canonical(by_distance):
        return jnp.take(jnp.stack(by_distance, axis=0), rel, axis=0)

    def call(kernel, grid, in_specs, out_specs, out_shape, scratch, estimate, name, *args):
        return pl.pallas_call(
            kernel,
            grid_spec=pltpu.PrefetchScalarGridSpec(
                num_scalar_prefetch=1,
                grid=grid,
                in_specs=in_specs,
                out_specs=out_specs,
                scratch_shapes=scratch,
            ),
            out_shape=out_shape,
            compiler_params=params(),
            cost_estimate=estimate,
            name=name,
        )(place, *args)

    depth = TABLES * slots
    pixel_part = jnp.concatenate([fields[0], jnp.ones((vars_here, 1, patches), bf16)], axis=1)
    table_part = jnp.concatenate([embed_weight, var_embed[:, None, :]], axis=1)
    piece = jnp.concatenate([pixel_part, table_part], axis=2).reshape(TABLES * vars_here, -1)
    pieces = [piece] + [send(piece, d) for d in range(1, n_var)]
    real = jnp.pad(var_mask[0], (0, slots - slot_count)).astype(f32)[:, None]
    prep_in = pieces + [agg_query[None], agg_key, agg_value]
    maps = [(HEADS * slots, depth)] * 2 + [(depth, HEADS * slots)] * 2
    prep_out = (
        [((depth, patches), bf16), ((depth, width), bf16)]
        + [(shape, bf16) for shape in maps]
        + [
            ((width, 3 * depth), bf16),
            ((HEADS, 2 * depth, size), bf16),
            ((depth, width), f32),
            ((width, HEADS), bf16),
            ((HEADS, width), bf16),
        ]
    )
    (
        pixels, tables, score_high, score_low, score_high_t, score_low_t, ev_front, ev_back,
        table_keys, query_keys, spread,
    ) = call(
        partial(prep_kernel, n_var, vars_here, patches),
        (1,),
        [whole(array.shape) for array in prep_in],
        [whole(shape) for shape, _ in prep_out],
        [jax.ShapeDtypeStruct(shape, kind) for shape, kind in prep_out],
        [pltpu.VMEM((depth, patches + width), bf16)],
        cost(8 * depth * width * width, 4 * width * width),
        "prep",
        *prep_in,
    )

    gain_one, bias_one = norm1_gain[None], norm1_bias[None]
    gain_two, bias_two = norm2_gain[None], norm2_bias[None]

    if lanes_fit:
        qkv_parts = [attn_qkv] * 3
        qkv_specs = [
            pl.BlockSpec((width, cols), lambda i, at, third=third: (0, third * n_var + at[0]))
            for third in range(3)
        ]
    else:
        qkv_mine = lax.dynamic_index_in_dim(
            attn_qkv.reshape(width, 3, n_var, cols), me, axis=2, keepdims=False
        )
        qkv_parts = [qkv_mine[:, third] for third in range(3)]
        qkv_specs = [whole((width, cols))] * 3

    block = min(512, mine)
    steps = patches // block
    own = mine // block
    heads_shape = jax.ShapeDtypeStruct((here, patches, size), bf16)
    heads_spec = pl.BlockSpec((here, block, size), lambda i, _: (0, i, 0))
    agg_values_t, merged, normed_send, normed_keep, queries, keys, values = call(
        partial(front_kernel, own, n_z),
        (steps,),
        [
            pl.BlockSpec((depth, block), lambda i, _: (0, i)),
            whole(score_high.shape),
            whole(score_low.shape),
            whole(real.shape),
            whole(ev_front.shape),
            whole(agg_out.shape),
            whole(gain_one.shape),
            whole(bias_one.shape),
        ]
        + qkv_specs,
        [
            pl.BlockSpec((width, block), lambda i, _: (0, jnp.minimum(i, own - 1))),
            pl.BlockSpec((block, width), lambda i, _: (jnp.minimum(i, own - 1), 0)),
            pl.BlockSpec((width // 2, block), lambda i, _: (0, i)),
            pl.BlockSpec((width // 2, block), lambda i, _: (0, i)),
            heads_spec,
            heads_spec,
            heads_spec,
        ],
        [
            jax.ShapeDtypeStruct((width, mine), bf16),
            jax.ShapeDtypeStruct((mine, width), f32),
            jax.ShapeDtypeStruct((width // 2, patches), bf16),
            jax.ShapeDtypeStruct((width // 2, patches), bf16),
            heads_shape,
            heads_shape,
            heads_shape,
        ],
        [pltpu.VMEM((width, block), f32), pltpu.VMEM((width, block), bf16)],
        cost(2 * patches * width * (width + 3 * cols + 256), 16 * patches * width),
        "front",
        pixels, score_high, score_low, real, ev_front, agg_out, gain_one, bias_one, *qkv_parts,
    )

    def attend(distance):
        heads = min(2, here) if distance < 2 else here
        return pl.pallas_call(
            attend_kernel,
            grid=(here // heads,),
            in_specs=[
                pl.BlockSpec((heads, mine, size), lambda i: (i, distance, 0)),
                pl.BlockSpec((heads, patches, size), lambda i: (i, 0, 0)),
                pl.BlockSpec((heads, patches, size), lambda i: (i, 0, 0)),
            ],
            out_specs=[
                pl.BlockSpec((mine, heads * size), lambda i: (0, i)),
                pl.BlockSpec((heads, 1, mine), lambda i: (i, 0, 0)),
            ],
            out_shape=[
                jax.ShapeDtypeStruct((mine, cols), bf16),
                jax.ShapeDtypeStruct((here, 1, mine), f32),
            ],
            compiler_params=params(),
            cost_estimate=cost(
                4 * mine * patches * here * 256, 4 * patches * cols * 2, mine * patches * here
            ),
            name=f"attend{distance}",
        )(queries, keys, values)

    attended_by, lse_by, arrived = [None] * n_var, [None] * n_var, [None] * n_var
    for distance in reversed(range(n_var)):
        attended_by[distance], lse_by[distance] = attend(distance)
        arrived[distance] = (
            send(attended_by[distance], distance) if distance else attended_by[distance]
        )
    if not lanes_fit:
        arrived = [canonical(arrived).transpose(1, 0, 2).reshape(mine, width)]

    cot = cotangent[0]
    tile = 2 * hidden_width // n_item
    row_f32 = jax.ShapeDtypeStruct((mine, width), f32)
    row_bf16 = jax.ShapeDtypeStruct((mine, width), bf16)
    row_spec = whole((mine, width))
    tall_spec = whole((width, mine))
    tall_bf16 = jax.ShapeDtypeStruct((width, mine), bf16)
    piece_spec = whole((mine, cols))
    (
        output, attended_t, normed_two_t, active_send, active_keep, g_hidden, g_stream, g_stream_low,
        gains_two,
        *g_attended,
    ) = call(
        partial(mlp_kernel, len(arrived), n_var),
        (hidden_width // tile,),
        [whole(piece.shape) for piece in arrived]
        + [
            row_spec,
            whole((width, width)),
            whole(gain_two.shape),
            whole(bias_two.shape),
            row_spec,
            pl.BlockSpec((width, tile), lambda i, _: (0, i)),
            pl.BlockSpec((tile, width), lambda i, _: (i, 0)),
        ],
        [
            row_spec,
            tall_spec,
            tall_spec,
            pl.BlockSpec((tile // 2, mine), lambda i, _: (i, 0)),
            pl.BlockSpec((tile // 2, mine), lambda i, _: (i, 0)),
            pl.BlockSpec((mine, tile), lambda i, _: (0, i)),
            row_spec,
            row_spec,
            whole((2, width)),
        ]
        + [piece_spec] * n_var,
        [
            row_bf16,
            tall_bf16,
            tall_bf16,
            jax.ShapeDtypeStruct((hidden_width // 2, mine), bf16),
            jax.ShapeDtypeStruct((hidden_width // 2, mine), bf16),
            jax.ShapeDtypeStruct((mine, hidden_width), bf16),
            row_f32,
            row_bf16,
            jax.ShapeDtypeStruct((2, width), f32),
        ]
        + [jax.ShapeDtypeStruct((mine, cols), bf16)] * n_var,
        [
            pltpu.VMEM((mine, width), bf16),
            pltpu.VMEM((mine, width), bf16),
            pltpu.VMEM((mine, width), f32),
            pltpu.VMEM((mine, width), f32),
            pltpu.VMEM((mine, 1), f32),
            pltpu.VMEM((mine, width), f32),
            pltpu.VMEM((mine, width), f32),
            pltpu.VMEM((tile, mine), bf16),
        ],
        cost(
            2 * mine * width * (4 * hidden_width + 2 * width),
            4 * width * hidden_width + 16 * mine * width,
        ),
        "mlp",
        *arrived, merged, attn_proj, gain_two, bias_two, cot, mlp_in, mlp_out,
    )
    g_heads = [g_attended[0]] + [send(g_attended[d], d) for d in range(1, n_var)]

    kept_rows = n_z * shard

    def pair_product(tall, grads):
        return dot(tall, grads).astype(bf16)

    def pair_own(tall, grads, got):
        return (dot(tall, grads) + got.astype(f32)).astype(bf16)

    def column_block(array, start=0, total=None):
        rows = array.shape[0]
        total = total or array.shape[1]
        span = total // n_var
        if span % 128 == 0:
            return array, pl.BlockSpec((rows, span), lambda j, at: (0, start // span + (at[0] ^ j)))
        cut = array[:, start : start + total]
        cut = jnp.take(cut.reshape(rows, n_var, span).transpose(1, 0, 2), rel, axis=0)
        return cut, pl.BlockSpec((None, rows, span), lambda j, at: (j, 0, 0))

    def pair_send_two(main, side):
        spec = pl.BlockSpec((n_z, None, shard, mine), lambda j, at: (0, 1 - at[1], 0, 0))
        tiles = hidden_width // width
        return call(
                send_kernel,
                (tiles + 1,),
                [
                    spec,
                    pl.BlockSpec((mine, width), lambda j, at: (0, jnp.minimum(j, tiles - 1))),
                    spec,
                    whole((mine, width)),
                ],
                pl.BlockSpec((kept_rows, width), lambda j, at: (0, j)),
                jax.ShapeDtypeStruct((kept_rows, hidden_width + width), bf16),
                [],
                cost(2 * kept_rows * mine * (hidden_width + width), 24 * kept_rows * width, share=2),
                "send",
                main[0].reshape(n_z, 2, shard, mine), main[1],
                side[0].reshape(n_z, 2, shard, mine), side[1],
            )

    def pair_keep(main, side, got):
        args, specs, start = [], [], 0
        for tall, grads in (main, side):
            args.append(tall.reshape(n_z, 2, shard, mine))
            specs.append(pl.BlockSpec((n_z, None, shard, mine), lambda j, at: (0, at[1], 0, 0)))
            for array, spec in (column_block(grads), column_block(got, start, grads.shape[1])):
                args.append(array)
                specs.append(spec)
            start += grads.shape[1]
        main_span, side_span = main[1].shape[1] // n_var, side[1].shape[1] // n_var
        first = 3 * main_span // 4
        spans = [first] * n_var + [main_span - first + side_span] * n_var
        outs = call(
            partial(keep_kernel, n_var),
            (n_var,),
            specs,
            [whole((kept_rows, span)) for span in spans],
            [jax.ShapeDtypeStruct((kept_rows, span), bf16) for span in spans],
            [],
            cost(
                2 * kept_rows * mine * (main_span + side_span) * n_var, 24 * kept_rows * main_span, share=2
            ),
            "keep",
            *args,
        )
        return outs[:n_var], outs[n_var:]

    def add_all(first, *others):
        total = first.astype(f32)
        for other in others:
            total = total + other.astype(f32)
        return total.astype(bf16)

    def exchange(pieces):
        return [pieces[0]] + [send(pieces[d], d) for d in range(1, n_var)]


    main, side = (normed_two_t, g_hidden), (attended_t, g_stream_low)
    sent = pair_send_two(main, side)
    sent, g_heads, active_send = lax.optimization_barrier((sent, g_heads, active_send))
    got = swap_core(sent)
    got_mlp_out = swap_core(pair_product(active_send, cot))
    first, second = pair_keep(main, side, got)
    active_keep, first, second = lax.optimization_barrier((active_keep, first, second))
    first = exchange(first)
    g_mlp_out = pair_own(active_keep, cot, got_mlp_out)
    mlp_out_rows = lax.psum_scatter(g_mlp_out, "z", scatter_dimension=0, tiled=True)
    g_heads, _ = lax.optimization_barrier((g_heads, g_mlp_out))

    group = min(2, here)
    parts = here // group
    gcols = group * size
    back_block = min(1024, patches)

    def attend_back(part, queries, extra):
        group_spec = pl.BlockSpec((group, back_block, size), lambda i: (part, i, 0))
        side_spec = pl.BlockSpec((mine, gcols), lambda i: (0, part))
        piece_cols = 3 * gcols + sum(array.shape[1] for array in extra[:1])
        full, *pieces = pl.pallas_call(
            partial(attend_back_kernel, n_var, len(extra), part > 0),
            grid=(patches // back_block,),
            in_specs=[whole(array.shape) for array in extra]
            + [
                pl.BlockSpec((group, patches, size), lambda i: (part, 0, 0)),
                group_spec,
                group_spec,
            ]
            + [pl.BlockSpec((group, 1, mine), lambda i: (part, 0, 0))] * n_var
            + [side_spec] * (2 * n_var),
            out_specs=[whole((patches, 3 * gcols))] + [whole((mine, piece_cols))] * n_var,
            out_shape=[jax.ShapeDtypeStruct((patches, 3 * gcols), bf16)]
            + [jax.ShapeDtypeStruct((mine, piece_cols), bf16)] * n_var,
            scratch_shapes=[
                pltpu.VMEM((group, patches, size), bf16),
                pltpu.VMEM((group, 1, patches), f32),
                pltpu.VMEM((group, 1, patches), f32),
                pltpu.VMEM((group, patches, size) if part else (group, size, patches), f32),
                pltpu.VMEM((group, back_block, patches), bf16),
                pltpu.VMEM((group, back_block, patches), bf16),
            ],
            compiler_params=params(),
            cost_estimate=cost(
                10 * patches * patches * group * 256, 8 * patches * gcols * 2, patches * patches * group
            ),
            name=f"attend_back{part}",
        )(*extra, queries, keys, values, *lse_by, *attended_by, *g_heads)
        return full, pieces

    ride = kept_rows == mine and parts > 1
    g_qkv, packed_pieces = [], []
    for part in range(parts):
        full, pieces = attend_back(part, queries, second if ride and part == 0 else [])
        if part == 0:
            full, first = lax.optimization_barrier((full, first))
            first_sum = add_all(*first)
        if part < parts - 1:
            product = pair_product(normed_send, full)
            queries, first_sum, product = lax.optimization_barrier((queries, first_sum, product))
            g_qkv.append((full, product))
        if part == parts - 1:
            pieces, packed_pieces = lax.optimization_barrier((pieces, packed_pieces))
        packed_pieces += exchange(pieces)
    if ride:
        second = [piece[:, 3 * gcols :] for piece in packed_pieces[:n_var]]
    else:
        second = exchange(second)
    g_qkv.append((full, pair_product(normed_send, full)))
    second_sum = add_all(*second)
    columns = [first_sum, second_sum]
    columns += [pair_own(normed_keep, full, swap_core(product)) for full, product in g_qkv]
    both_sum = jnp.concatenate(columns, axis=1)
    def my_slice(array, axis):
        return lax.dynamic_slice_in_dim(array, item * shard, shard, axis=axis)

    tables_mine = my_slice(tables, 1).T
    packed_pieces, both_sum, tables_mine = lax.optimization_barrier(
        (packed_pieces, both_sum, tables_mine)
    )
    both_rows = lax.psum_scatter(both_sum, "z", scatter_dimension=0, tiled=True)
    count = n_var
    if not lanes_fit:
        packed = [
            canonical(packed_pieces[part * n_var : (part + 1) * n_var]) for part in range(parts)
        ]
        packed = jnp.stack(packed, axis=0).reshape(parts, n_var, mine, 3, gcols)
        packed_pieces = [packed.transpose(2, 3, 1, 0, 4).reshape(mine, 3 * width)]
        count, parts = 1, 1
    packed_cols = 3 * gcols if lanes_fit else 3 * width

    far = pl.BlockSpec(memory_space=pl.ANY)
    table_rows = -(-(depth + 4) // 16) * 16
    late_rows = kept_rows + table_rows
    g_fields, late_send, late_keep = call(
        partial(back_kernel, count, parts, n_z),
        (1,),
        [pl.BlockSpec((block, packed_cols), lambda i, _: (i, 0)) for piece in packed_pieces]
        + [
            far,
            far,
            whole(gain_one.shape),
            far,
            far,
            pl.BlockSpec((depth, block), lambda i, _: (0, i)),
            whole(score_high.shape),
            whole(score_low.shape),
            whole((depth, HEADS * slots)),
            whole((depth, HEADS * slots)),
            whole(real.shape),
            whole(ev_back.shape),
            far,
            whole((2, width)),
        ],
        [
            pl.BlockSpec((depth, block), lambda i, _: (0, i)),
            whole((late_rows + HEADS, width)),
            whole((late_rows + HEADS, width)),
        ],
        [
            jax.ShapeDtypeStruct((depth, mine), bf16),
            jax.ShapeDtypeStruct((late_rows + HEADS, width), bf16),
            jax.ShapeDtypeStruct((late_rows + HEADS, width), f32),
        ],
        [
            pltpu.VMEM((HEADS * slots, block), bf16),
            pltpu.VMEM((block, 3 * width), bf16),
            pltpu.VMEM((table_rows, width), f32),
            pltpu.VMEM((depth, HEADS * slots), f32),
            pltpu.VMEM((3, width, width), bf16),
            pltpu.VMEM((mine, width), f32),
            pltpu.VMEM((mine, width), f32),
            pltpu.VMEM((width, width), bf16),
            pltpu.VMEM((width, mine), bf16),
            pltpu.SemaphoreType.DMA((7,)),
        ],
        cost(2 * mine * width * 4 * width, 8 * width * width + 20 * mine * width),
        "back",
        *packed_pieces, attn_qkv, merged, gain_one, g_stream, agg_out, pixels, score_high, score_low,
        score_high_t, score_low_t, real, ev_back, agg_values_t, gains_two,
    )

    late_send, mlp_out_rows = lax.optimization_barrier((late_send, mlp_out_rows))
    out_block = mlp_out_rows.shape[0] // n_var
    mlp_out_by = exchange(
        [
            lax.dynamic_slice_in_dim(mlp_out_rows, (me ^ d) * out_block, out_block, axis=0)
            for d in range(n_var)
        ]
    )
    mlp_out_rows = add_all(*mlp_out_by).reshape(shard, -1)

    late_got = swap_core(late_send)
    late_span = width // n_var
    n_blocks = -(-depth // late_span)
    n_spec = pl.BlockSpec((HEADS, n_blocks * late_span), lambda j, at: (late_rows // HEADS, 0))
    sum_rows = late_rows + n_blocks * HEADS
    f_rows = -(-channels * vars_here // 16) * 16
    piece_rows = sum_rows + f_rows * (mine // late_span)
    late_args = [late_keep, late_got]
    if late_span % 128:
        late_args = [
            jnp.take(array.reshape(-1, n_var, late_span).transpose(1, 0, 2), rel, axis=0)
            for array in late_args
        ]
    late_pieces = call(
        partial(pair_kernel, n_var, channels, vars_here, late_rows),
        (1,),
        [whole(array.shape) for array in late_args] + [n_spec, n_spec, whole((depth, mine))],
        [whole((piece_rows, late_span))] * n_var,
        [jax.ShapeDtypeStruct((piece_rows, late_span), bf16)] * n_var,
        [],
        cost(piece_rows * width, 8 * piece_rows * width),
        "late_pair",
        *late_args, late_keep, late_got, g_fields,
    )
    late_pieces = exchange(late_pieces)
    late_pieces, both_rows = lax.optimization_barrier((late_pieces, both_rows))
    rows_all = jnp.concatenate([both_rows, mlp_out_rows], axis=1)
    halves = 1 if n_var == 4 and lanes_fit else 0
    if halves:
        near = [send(rows_all, 1), send(rows_all, 2)]
    else:
        rows_all = list(lax.all_gather(rows_all, "var", axis=0))
    z_rows = shard + table_rows + n_blocks * HEADS
    *z_pieces, fields_grad = call(
        partial(z_pieces_kernel, n_var, shard, n_z),
        (1,),
        [whole((piece_rows, late_span))] * n_var,
        [whole((z_rows, late_span))] * n_z + [whole((f_rows, patches))],
        [jax.ShapeDtypeStruct((z_rows, late_span), bf16)] * n_z
        + [jax.ShapeDtypeStruct((f_rows, patches), f32)],
        [pltpu.VMEM((sum_rows, late_span), bf16)],
        cost(piece_rows * width, 2 * piece_rows * width),
        "late_z",
        *late_pieces,
    )
    z_pieces = [z_pieces[0]] + [send_z(z_pieces[d], d) for d in range(1, n_z)]
    late_rows_mine, n_all = pl.pallas_call(
        partial(z_sum_kernel, n_z),
        out_shape=[
            jax.ShapeDtypeStruct((shard + table_rows, late_span), bf16),
            jax.ShapeDtypeStruct((HEADS, n_blocks * late_span), f32),
        ],
        compiler_params=params(),
        cost_estimate=cost(z_rows * width, 2 * z_rows * width),
        name="late_sum",
    )(*z_pieces)

    fields_grad = fields_grad[: channels * vars_here].reshape(1, vars_here, channels, patches)
    if halves:
        late_rows_mine, near = lax.optimization_barrier((late_rows_mine, near))
        half = rows_all.shape[1] // 2
        rows_all = [rows_all] + near + [send(near[0][:, :half], 2), send(near[1][:, half:], 1)]
    late_by = exchange([late_rows_mine] * n_var)
    if late_span % 128:
        late_by = [canonical(late_by).transpose(1, 0, 2).reshape(shard + table_rows, width)]
    small_shapes = [(1, width), (channels * vars_here, shard), (vars_here, shard), (8, width)]
    final_in = [n_all, tables_mine, spread, table_keys]
    item_rows = [
        pl.BlockSpec((shard, width), lambda i, at: (2 * at[2] + at[1], 0)),
        pl.BlockSpec((shard, HEADS), lambda i, at: (2 * at[2] + at[1], 0)),
    ]
    agg_out_grad, agg_value_grad, agg_key_grad, query_row, embed_weight_grad, var_embed_grad, gains = call(
        partial(final_kernel, len(late_by)),
        (1,),
        [whole(array.shape) for array in late_by + final_in] + item_rows,
        [whole((shard, width))] * 3
        + [whole(shape) for shape in small_shapes],
        [jax.ShapeDtypeStruct((shard, width), f32)] * 3
        + [jax.ShapeDtypeStruct(shape, f32) for shape in small_shapes],
        [pltpu.VMEM((table_rows, width), f32)],
        cost(2 * shard * width * 3 * depth, 12 * shard * width),
        "final",
        *late_by, *final_in, agg_value, query_keys,
    )
    gains = my_slice(gains, 1)
    agg_query_grad = my_slice(query_row[0], 0) * scale
    embed_weight_grad = embed_weight_grad.reshape(vars_here, channels, shard)

    row_shapes = [
        jax.ShapeDtypeStruct((shard, hidden_width), f32),
        jax.ShapeDtypeStruct((shard, width), f32),
        jax.ShapeDtypeStruct((shard, 3 * width), f32),
        jax.ShapeDtypeStruct((n_var, shard, out_block * width // shard), f32),
    ]
    mlp_in_grad, attn_proj_grad, attn_qkv_grad, mlp_out_grad = call(
        partial(assemble_kernel, n_var, here // group, gcols, halves),
        (1,),
        [whole(array.shape) for array in rows_all],
        [whole(row.shape) for row in row_shapes],
        row_shapes,
        [],
        cost(shard * 9 * width, 6 * shard * 9 * width),
        "assemble",
        *rows_all,
    )
    mlp_out_grad = mlp_out_grad.reshape(n_var * out_block, width)
    return (
        output[None],
        fields_grad,
        embed_weight_grad,
        var_embed_grad,
        agg_query_grad,
        agg_key_grad,
        agg_value_grad,
        agg_out_grad,
        gains[0],
        gains[1],
        attn_qkv_grad,
        attn_proj_grad,
        gains[2],
        gains[3],
        mlp_in_grad,
        mlp_out_grad,
    )


def solution(mesh):
    n_var, n_item = mesh.shape["var"], mesh.shape["item"]
    items = ("z", "core")
    return jax.shard_map(
        partial(per_device, n_var, n_item // 2),
        mesh=Mesh(mesh.devices.reshape(n_var, n_item // 2, 2), ("var", "z", "core")),
        in_specs=(
            P(items, "var", None, None),
            P(items, None),
            P("var", None, None),
            P("var", None),
            P(),
            P(),
            P(),
            P(),
            P(),
            P(),
            P(),
            P(),
            P(),
            P(),
            P(),
            P(),
            P(items, "var", None),
        ),
        out_specs=(
            P(items, "var", None),
            P(items, "var", None, None),
            P("var", None, items),
            P("var", items),
            P(items),
            P(items, None),
            P(items, None),
            P(items, None),
            P(items),
            P(items),
            P(items, None),
            P(items, None),
            P(items),
            P(items),
            P(items, None),
            P(items, None),
        ),
        check_vma=False,
    )
```

```python
from functools import partial

import jax
import jax.numpy as jnp
from jax import lax
from jax.experimental import pallas as pl
from jax.experimental.pallas import tpu as pltpu
from jax.sharding import Mesh
from jax.sharding import PartitionSpec as P

HEADS = 16
TABLES = 5

epsilon = 1e-05
masked_score = -1e30
highest = lax.Precision.HIGHEST
f32 = jnp.float32
bf16 = jnp.bfloat16
COST = 0.05
VMEM_BYTES = 56 * 1024 * 1024
LOG2E = 1.4426950408889634


def dot(a, b):
    return lax.dot_general(a, b, (((1,), (0,)), ((), ())), preferred_element_type=f32)


def dot_nt(a, b):
    return lax.dot_general(a, b, (((1,), (1,)), ((), ())), preferred_element_type=f32)


def dot_tn(a, b):
    return lax.dot_general(a, b, (((0,), (0,)), ((), ())), preferred_element_type=f32)


def split_two(wide):
    high = wide.astype(bf16)
    return high, (wide - high.astype(f32)).astype(bf16)


def split_three(wide):
    high, rest = split_two(wide)
    low = wide - high.astype(f32) - rest.astype(f32)
    return high, rest, low.astype(bf16)


def columns(parts, rows, width):
    lane = lax.broadcasted_iota(jnp.int32, (rows, width), 1)
    out = jnp.zeros((rows, width), f32)
    for i, part in enumerate(parts):
        out = jnp.where(lane == i, part.astype(f32), out)
    return out.astype(bf16)


def whole(shape):
    return pl.BlockSpec(shape, lambda *_: (0,) * len(shape))


def params(vmem=VMEM_BYTES):
    return pltpu.CompilerParams(vmem_limit_bytes=vmem)


def cost(flops, bytes_accessed, transcendentals=0, share=COST):
    return pl.CostEstimate(
        flops=int(flops * share), bytes_accessed=int(bytes_accessed * share), transcendentals=0
    )


def norm_parts(stream):
    centred = stream - jnp.mean(stream, axis=-1, keepdims=True)
    inverse = lax.rsqrt(jnp.mean(centred * centred, axis=-1, keepdims=True) + epsilon)
    return centred * inverse, inverse


def norm_back(upstream, unit_rows, inverse, gain):
    scaled = upstream * gain
    return inverse * (
        scaled
        - jnp.mean(scaled, axis=-1, keepdims=True)
        - unit_rows * jnp.mean(scaled * unit_rows, axis=-1, keepdims=True)
    )


def variable_probs(pixel_rows, score_high, score_low, real, slots):
    scores = dot(score_high, pixel_rows) + dot(score_low, pixel_rows)
    scores = scores.reshape(HEADS, slots, pixel_rows.shape[1])
    scores = jnp.where(real[None] > 0, scores, masked_score)
    powers = jnp.exp(scores - jnp.max(scores, axis=1, keepdims=True))
    return powers / jnp.sum(powers, axis=1, keepdims=True)


def prep_kernel(count, vars_here, patches, *refs):
    place_ref = refs[0]
    pieces = refs[1 : 1 + count]
    query_ref, key_ref, value_ref = refs[1 + count : 4 + count]
    (
        pix_ref, tables_ref, shi_ref, slo_ref, sthi_ref, stlo_ref, front_ref, back_ref, keys_ref,
        qk_ref, spread_ref, all_s,
    ) = refs[4 + count :]
    me = place_ref[0]
    depth, width = tables_ref.shape
    slots = depth // TABLES
    size = width // HEADS
    rows = TABLES * vars_here
    total = None
    for d in range(count):
        row = lax.broadcasted_iota(jnp.int32, (depth, rows), 0)
        col = lax.broadcasted_iota(jnp.int32, (depth, rows), 1)
        want = (col % TABLES) * slots + (me ^ d) * vars_here + col // TABLES
        part = dot(jnp.where(row == want, 1.0, 0.0).astype(bf16), pieces[d][...])
        total = part if total is None else total + part
    all_s[...] = total.astype(bf16)
    mine = patches // count
    for d in range(count):
        at = pl.multiple_of((me ^ d) * mine, mine)
        pix_ref[:, d * mine : (d + 1) * mine] = all_s[:, pl.ds(at, mine)]
    tables = all_s[:, patches:]
    tables_ref[...] = tables
    head = lax.broadcasted_iota(jnp.int32, (HEADS, width), 0)
    same = lax.broadcasted_iota(jnp.int32, (HEADS, width), 1) // size == head
    spread = jnp.where(same, query_ref[...].astype(f32), 0.0)
    scale = size ** (-0.5)
    spread_ref[...] = (spread * scale).astype(bf16)
    query_keys = (dot_nt(key_ref[...], spread.astype(bf16)) * scale).astype(bf16)
    qk_ref[...] = query_keys
    halves = split_two(dot(tables, query_keys))
    wide = HEADS * slots
    picks = lax.broadcasted_iota(jnp.int32, (wide, HEADS), 0) // slots
    picks = jnp.where(picks == lax.broadcasted_iota(jnp.int32, (wide, HEADS), 1), 1.0, 0.0).astype(bf16)
    for half, tall, flat in zip(halves, (shi_ref, slo_ref), (sthi_ref, stlo_ref)):
        row = lax.broadcasted_iota(jnp.int32, (wide, depth), 0) % slots
        col = lax.broadcasted_iota(jnp.int32, (wide, depth), 1) % slots
        tall[...] = jnp.where(row == col, dot_nt(picks, half), 0.0).astype(bf16)
        row = lax.broadcasted_iota(jnp.int32, (depth, wide), 0) % slots
        col = lax.broadcasted_iota(jnp.int32, (depth, wide), 1) % slots
        flat[...] = jnp.where(row == col, dot_nt(half, picks), 0.0).astype(bf16)
    mixed = dot(tables, value_ref[...])
    high, low = split_two(mixed)
    high_wide, low_wide = high.astype(f32), low.astype(f32)
    front_ref[...] = jnp.concatenate([high_wide, high_wide, low_wide], axis=0).T.astype(bf16)
    both = jnp.concatenate([high, low], axis=0)
    for h in range(HEADS):
        back_ref[h] = both[:, h * size : (h + 1) * size]
    keys_ref[...] = dot(tables, key_ref[...])


def front_kernel(
    own_blocks, n_z, place_ref, pix_ref, shi_ref, slo_ref, real_ref, ev_ref, out_w_ref, gain_ref,
    bias_ref, wq_ref, wk_ref, wv_ref,
    values_ref, merged_ref, send_ref, keep_ref, q_ref, k_ref, v_ref, flat_ref, tall_s,
):
    slots = real_ref.shape[0]
    pixel_rows = pix_ref[...]
    probs = variable_probs(pixel_rows, shi_ref[...], slo_ref[...], real_ref[...], slots)
    weights = probs.astype(bf16).astype(f32)
    pixels = pixel_rows.astype(f32).reshape(TABLES, slots, -1)
    size = ev_ref.shape[0] // HEADS
    for h in range(HEADS):
        mixed = (weights[h][None] * pixels).reshape(pixel_rows.shape)
        high, low = split_two(mixed)
        flat_ref[h * size : (h + 1) * size, :] = dot(
            ev_ref[h * size : (h + 1) * size, :], jnp.concatenate([high, low, high], axis=0)
        )
    values = flat_ref[...].astype(bf16)
    merged = dot(values.T, out_w_ref[...])

    @pl.when(pl.program_id(0) < own_blocks)
    def _():
        values_ref[...] = values
        merged_ref[...] = merged

    unit_rows, _ = norm_parts(merged)
    normed = (unit_rows * gain_ref[...] + bias_ref[...]).astype(bf16)
    tall_s[...] = normed.T
    core, shard = place_ref[1], tall_s.shape[0] // (2 * n_z)
    for zz in range(n_z):
        at = slice(zz * shard, (zz + 1) * shard)
        keep_ref[at] = tall_s[pl.ds(pl.multiple_of((2 * zz + core) * shard, shard), shard), :]
        send_ref[at] = tall_s[pl.ds(pl.multiple_of((2 * zz + 1 - core) * shard, shard), shard), :]
    queries = dot(normed, wq_ref[...]).astype(bf16).astype(f32) * size ** (-0.5)
    keys = dot(normed, wk_ref[...])
    values = dot(normed, wv_ref[...])
    for h in range(q_ref.shape[0]):
        at = h * size
        q_ref[h] = queries[:, at : at + size].astype(bf16)
        k_ref[h] = keys[:, at : at + size].astype(bf16)
        v_ref[h] = values[:, at : at + size].astype(bf16)


def attend_kernel(q_ref, k_ref, v_ref, out_ref, lse_ref):
    here, rows, size = q_ref.shape
    block = min(512, rows)
    pieces = [(h, at) for at in range(0, rows, block) for h in range(here)]

    def scores_of(piece):
        h, at = piece
        return dot_nt(q_ref[h, at : at + block], k_ref[h])

    def finish(piece, powers, top, total):
        h, at = piece
        mixed = dot(powers, v_ref[h]) / total
        lse = jnp.broadcast_to(top + jnp.log(total), (block, 128)).T[0:1]
        return mixed.astype(bf16), lse

    done, waiting = {}, None
    scores = scores_of(pieces[0])
    for i, piece in enumerate(pieces):
        later = scores_of(pieces[i + 1]) if i + 1 < len(pieces) else None
        top = jnp.max(scores, axis=-1, keepdims=True)
        powers = jnp.exp(scores - top)
        total = jnp.sum(powers, axis=-1, keepdims=True)
        if waiting is not None:
            done[waiting[0]] = finish(*waiting)
        waiting = (piece, powers.astype(bf16), top, total)
        scores = later
    done[waiting[0]] = finish(*waiting)
    for h, at in pieces:
        lse_ref[h, :, at : at + block] = done[h, at][1]
    for at in range(0, rows, block):
        out_ref[at : at + block] = jnp.concatenate([done[h, at][0] for h in range(here)], axis=-1)


def attend_back_kernel(count, extra, *refs):
    extra_refs, refs = refs[:extra], refs[extra:]
    q_ref, k_ref, v_ref = refs[:3]
    lse_refs = refs[3 : 3 + count]
    out_refs = refs[3 + count : 3 + 2 * count]
    up_refs = refs[3 + 2 * count : 3 + 3 * count]
    full_ref = refs[3 + 3 * count]
    piece_refs = refs[4 + 3 * count : 4 + 4 * count]
    up_heads, total_rows, lse_rows, gq_ref, prob_s, slope_s = refs[4 + 4 * count :]
    step = pl.program_id(0)
    here, patches, size = q_ref.shape
    block = k_ref.shape[1]
    width = here * size
    mine = patches // count

    @pl.when(step == 0)
    def _():
        for h in range(here):
            at = h * size
            for d in range(count):
                rows = slice(d * mine, (d + 1) * mine)
                upstream = up_refs[d][:, at : at + size]
                up_heads[h, rows] = upstream
                product = upstream.astype(f32) * out_refs[d][:, at : at + size].astype(f32)
                total_rows[h, :, rows] = jnp.sum(product.T, axis=0, keepdims=True)
                lse_rows[h, :, rows] = lse_refs[d][h]
            gq_ref[h] = jnp.zeros(gq_ref.shape[1:], f32)

    chunk = min(256, patches)
    key_parts, value_parts = [], []
    for h in range(here):
        keys, values = k_ref[h], v_ref[h]
        for at in range(0, patches, chunk):
            span = slice(at, at + chunk)
            probs = jnp.exp(dot_nt(keys, q_ref[h, span]) - lse_rows[h, :, span])
            prob_s[h, :, span] = probs.astype(bf16)
            grads = dot_nt(values, up_heads[h, span])
            slope_s[h, :, span] = (probs * (grads - total_rows[h, :, span])).astype(bf16)
        value_parts.append(dot(prob_s[h], up_heads[h]))
        key_parts.append(dot(slope_s[h], q_ref[h]))
        gq_ref[h] += dot(keys.astype(f32).T.astype(bf16), slope_s[h])
    rows = pl.ds(pl.multiple_of(step * block, block), block)
    full_ref[rows, width : 2 * width] = jnp.concatenate(key_parts, axis=-1).astype(bf16)
    full_ref[rows, 2 * width :] = jnp.concatenate(value_parts, axis=-1).astype(bf16)

    @pl.when(step == pl.num_programs(0) - 1)
    def _():
        scale = size ** (-0.5)
        query_parts = [gq_ref[h].T for h in range(here)]
        full_ref[:, :width] = (jnp.concatenate(query_parts, axis=-1) * scale).astype(bf16)
        for d in range(count):
            piece_refs[d][:, : 3 * width] = full_ref[d * mine : (d + 1) * mine, :]

    if extra:

        @pl.when(step == 0)
        def _():
            for d in range(count):
                piece_refs[d][:, 3 * width :] = extra_refs[d][...]


def mlp_kernel(pieces, count, *refs):
    place_ref = refs[0]
    att_refs = refs[1 : 1 + pieces]
    merged_ref, proj_ref, gain_ref, bias_ref, cot_ref, win_ref, wout_ref = refs[1 + pieces : 8 + pieces]
    outs = refs[8 + pieces :]
    (
        out_ref, att_t_ref, normed_t_ref, send_ref, keep_ref, ghid_ref, gstream_ref, glow_ref,
        gains_ref,
    ) = outs[:9]
    gatt_refs = outs[9 : 9 + count]
    att_s, normed_s, stream_s, unit_s, inv_s, out_s, gn_s, tall_s = outs[9 + count :]
    step = pl.program_id(0)
    me = place_ref[0]
    cols = gatt_refs[0].shape[1]

    @pl.when(step == 0)
    def _():
        if pieces == 1:
            attended = att_refs[0][...]
        else:
            for d in range(pieces):
                att_s[:, pl.ds(pl.multiple_of((me ^ d) * cols, cols), cols)] = att_refs[d][...]
            attended = att_s[...]
        att_t_ref[...] = attended.T
        stream = merged_ref[...] + dot(attended, proj_ref[...])
        unit_rows, inverse = norm_parts(stream)
        stream_s[...] = stream
        unit_s[...] = unit_rows
        inv_s[...] = inverse
        normed = (unit_rows * gain_ref[...] + bias_ref[...]).astype(bf16)
        normed_s[...] = normed
        normed_t_ref[...] = normed.T
        out_s[...] = jnp.zeros_like(out_s)
        gn_s[...] = jnp.zeros_like(gn_s)

    tile = ghid_ref.shape[1]
    sub = min(256, tile)
    spans = [slice(at, at + sub) for at in range(0, tile, sub)]
    normed_rows, upstream_rows = normed_s[...], cot_ref[...]

    def products(span):
        return dot(normed_rows, win_ref[:, span]), dot_nt(upstream_rows, wout_ref[span, :])

    def shape(hidden, g_active):
        below = 0.5 + 0.5 * lax.erf(hidden * (0.5**0.5))
        density = jnp.exp(-0.5 * hidden * hidden) * ((2.0 * jnp.pi) ** (-0.5))
        return (hidden * below).astype(bf16), (g_active * (below + hidden * density)).astype(bf16)

    actives, grads, sums = [], [], []

    def add(first, last):
        span = slice(spans[first].start, spans[last].stop)
        active = jnp.concatenate(actives[first : last + 1], axis=1)
        grad = jnp.concatenate(grads[first : last + 1], axis=1)
        sums.append((dot(active, wout_ref[span, :]), dot_nt(grad, win_ref[:, span])))

    ready = products(spans[0])
    for i, span in enumerate(spans):
        later = products(spans[i + 1]) if i + 1 < len(spans) else None
        if i == len(spans) // 2 + 1:
            add(0, len(spans) // 2 - 1)
        active, grad = shape(*ready)
        actives.append(active)
        grads.append(grad)
        ready = later
    add(len(spans) // 2 if sums else 0, len(spans) - 1)
    for span, active, grad in zip(spans, actives, grads):
        ghid_ref[:, span] = grad
        tall_s[span, :] = active.T
    half = tile // 2
    core = place_ref[1]
    send_ref[...] = tall_s[pl.ds(pl.multiple_of((1 - core) * half, half), half), :]
    keep_ref[...] = tall_s[pl.ds(pl.multiple_of(core * half, half), half), :]
    out_s[...] += sum(pair[0] for pair in sums)
    gn_s[...] += sum(pair[1] for pair in sums)

    @pl.when(step == pl.num_programs(0) - 1)
    def _():
        out_ref[...] = (stream_s[...] + out_s[...]).astype(bf16)
        upstream = gn_s[...].astype(bf16).astype(f32)
        unit_rows = unit_s[...]
        g_stream = cot_ref[...].astype(f32) + norm_back(
            upstream, unit_rows, inv_s[...], gain_ref[...]
        )
        gstream_ref[...] = g_stream
        low = g_stream.astype(bf16)
        glow_ref[...] = low
        for d in range(count):
            rows = pl.ds(pl.multiple_of((me ^ d) * cols, cols), cols)
            gatt_refs[d][...] = dot_nt(low, proj_ref[rows, :]).astype(bf16)
        gains_ref[0:1, :] = jnp.sum(upstream * unit_rows, axis=0, keepdims=True)
        gains_ref[1:2, :] = jnp.sum(upstream, axis=0, keepdims=True)


def send_kernel(place_ref, main_rows, main_cols, side_rows, side_cols, out_ref):
    last = pl.program_id(0) == pl.num_programs(0) - 1

    def product(rows_ref, cols_ref):
        tall = rows_ref[...].reshape(-1, rows_ref.shape[-1])
        return dot(tall, cols_ref[...]).astype(bf16)

    @pl.when(jnp.logical_not(last))
    def _():
        out_ref[...] = product(main_rows, main_cols)

    @pl.when(last)
    def _():
        out_ref[...] = product(side_rows, side_cols)


def keep_kernel(count, *refs):
    main_rows, main_cols, main_got, side_rows, side_cols, side_got = refs[1:7]
    outs = refs[7:]
    step = pl.program_id(0)

    def product(rows_ref, cols_ref, got_ref):
        tall = rows_ref[...].reshape(-1, rows_ref.shape[-1])
        return (dot(tall, cols_ref[...]) + got_ref[...].astype(f32)).astype(bf16)

    for d in range(count):

        @pl.when(step == d)
        def _():
            first, second = outs[d], outs[count + d]
            main = product(main_rows, main_cols, main_got)
            cut = first.shape[1]
            rest = main.shape[1] - cut
            first[...] = main[:, :cut]
            second[:, :rest] = main[:, cut:]
            second[:, rest:] = product(side_rows, side_cols, side_got)


def pair_kernel(count, channels, vars_here, late_rows, *refs):
    place_ref = refs[0]
    keep_ref, got_ref, n_keep_ref, n_got_ref, fields_ref = refs[1:6]
    outs = refs[6:]
    depth, mine = fields_ref.shape
    rows = late_rows
    span = outs[0].shape[1]
    slots = depth // TABLES
    n_blocks = n_keep_ref.shape[1] // span
    f_rows = (outs[0].shape[0] - rows - n_blocks * HEADS) // (mine // span)
    row = lax.broadcasted_iota(jnp.int32, (f_rows, depth), 0)
    col = lax.broadcasted_iota(jnp.int32, (f_rows, depth), 1)
    n_total = (n_keep_ref[...] + n_got_ref[...].astype(f32)).astype(bf16)
    for d in range(count):
        q = place_ref[0] ^ d

        def block(ref):
            if len(ref.shape) == 3:
                return ref[d, :rows].astype(f32)
            return ref[:rows, pl.ds(pl.multiple_of(q * span, span), span)].astype(f32)

        outs[d][:rows] = (block(keep_ref) + block(got_ref)).astype(bf16)
        want = (row % channels) * slots + q * vars_here + row // channels
        picks = jnp.where((want == col) & (row < channels * vars_here), 1.0, 0.0).astype(bf16)
        picked = dot(picks, fields_ref[...]).astype(bf16)
        at = rows
        for b in range(n_blocks):
            outs[d][at : at + HEADS] = n_total[:, b * span : (b + 1) * span]
            at += HEADS
        for b in range(mine // span):
            outs[d][at : at + f_rows] = picked[:, b * span : (b + 1) * span]
            at += f_rows


def z_pieces_kernel(count, shard, n_z, *refs):
    pieces, outs, fields_ref, total_s = refs[1 : 1 + count], refs[1 + count : -2], refs[-2], refs[-1]
    me, z_at = refs[0][0], refs[0][2]
    rows, span = total_s.shape
    f_rows = fields_ref.shape[0]
    mine = fields_ref.shape[1] // count
    total = pieces[0][:rows].astype(f32)
    for piece in pieces[1:]:
        total = total + piece[:rows].astype(f32)
    total_s[...] = total.astype(bf16)
    for d in range(n_z):
        start = pl.multiple_of((z_at ^ d) * shard, shard)
        outs[d][:shard] = total_s[pl.ds(start, shard), :]
        outs[d][shard:] = total_s[n_z * shard :, :]
    for d in range(count):
        blocks = [
            pieces[d][rows + b * f_rows : rows + (b + 1) * f_rows] for b in range(mine // span)
        ]
        at = pl.multiple_of((me ^ d) * mine, mine)
        fields_ref[:, pl.ds(at, mine)] = jnp.concatenate(blocks, axis=1).astype(f32)


def assemble_kernel(count, parts, size, halves, *refs):
    me = refs[0][0]
    blocks, outs = refs[1 : 1 + count + halves], refs[1 + count + halves :]
    in_ref, proj_ref, qkv_ref, out_ref = outs
    a = in_ref.shape[1] // count
    b = proj_ref.shape[1] // count
    width = proj_ref.shape[1]
    for d in range(count):
        if halves and d == count - 1:
            rows = jnp.concatenate([ref[...] for ref in blocks[d:]], axis=1)
        else:
            rows = blocks[d][...]
        rows = rows.astype(f32)
        q = me ^ d if halves else d

        def span(at, step):
            return pl.ds(pl.multiple_of(at, step) if halves else at, step)

        in_ref[:, span(q * a, a)] = rows[:, :a]
        proj_ref[:, span(q * b, b)] = rows[:, a : a + b]
        at = a + b
        for part in range(parts):
            for third in range(3):
                to = third * width + q * b + part * size
                qkv_ref[:, span(to, size)] = rows[:, at : at + size]
                at += size
        out_ref[q] = rows[:, at:]


def z_sum_kernel(count, *refs):
    pieces, (rows_ref, n_ref) = refs[:count], refs[count:]
    total = pieces[0][...].astype(f32)
    for piece in pieces[1:]:
        total = total + piece[...].astype(f32)
    rows, span = rows_ref.shape
    rows_ref[...] = total[:rows].astype(bf16)
    for b in range(n_ref.shape[1] // span):
        n_ref[:, b * span : (b + 1) * span] = total[rows + b * HEADS : rows + (b + 1) * HEADS]


def final_kernel(count, *refs):
    place_ref = refs[0]
    pieces = refs[1 : 1 + count]
    n_ref, tables_ref, spread_ref, keys_ref, value_ref, qk_ref = refs[1 + count : 7 + count]
    outg_ref, valg_ref, keyg_ref, queryg_ref, embedg_ref, varg_ref, gains_ref, m_s = refs[7 + count :]
    shard, depth = tables_ref.shape
    width = m_s.shape[1]
    for d in range(count):
        span = pieces[d].shape[1]
        at = 0 if count == 1 else pl.multiple_of((place_ref[0] ^ d) * span, span)
        outg_ref[:, pl.ds(at, span)] = pieces[d][:shard].astype(f32)
        m_s[:, pl.ds(at, span)] = pieces[d][shard:].astype(f32)
    m_low = m_s[:depth, :].astype(bf16)
    n_high, n_low = split_two(n_ref[:, :depth])
    tables = tables_ref[...]
    valg_ref[...] = dot(tables, m_low)
    g_qk = dot_nt(tables, n_high) + dot_nt(tables, n_low)
    qk_high, qk_low = split_two(g_qk)
    spread = spread_ref[...]
    keyg_ref[...] = dot(qk_high, spread) + dot(qk_low, spread)
    head_at = lax.broadcasted_iota(jnp.int32, (HEADS, width), 1) // (width // HEADS)
    same = head_at == lax.broadcasted_iota(jnp.int32, (HEADS, width), 0)
    ones = jnp.where(same, 1.0, 0.0).astype(bf16)
    n_wide = dot(n_high.astype(f32).T.astype(bf16), ones) + dot(n_low.astype(f32).T.astype(bf16), ones)
    queryg_ref[...] = jnp.sum(n_wide * keys_ref[...], axis=0, keepdims=True)
    qk = qk_ref[...]
    table_grad = split_three(
        dot_nt(m_low, value_ref[...])
        + dot_nt(n_high.astype(f32).T.astype(bf16), qk)
        + dot_nt(n_low.astype(f32).T.astype(bf16), qk)
    )
    slots = depth // TABLES
    vars_here = varg_ref.shape[0]
    for ref, first, each in ((embedg_ref, 0, TABLES - 1), (varg_ref, TABLES - 1, 1)):
        row = lax.broadcasted_iota(jnp.int32, (each * vars_here, depth), 0)
        col = lax.broadcasted_iota(jnp.int32, (each * vars_here, depth), 1)
        want = (first + row % each) * slots + place_ref[0] * vars_here + row // each
        picks = jnp.where(want == col, 1.0, 0.0).astype(bf16)
        ref[...] = sum(dot(picks, part) for part in table_grad)
    gains_ref[...] = m_s[depth : depth + 8, :]


def back_kernel(count, parts, n_z, *refs):
    place_ref = refs[0]
    piece_refs = refs[1 : 1 + count * parts]
    (
        qkv_far, merged_far, gain_ref, gs_far, out_w_far, pix_ref, shi_ref, slo_ref, sthi_ref,
        stlo_ref, real_ref, ev_ref, values_far, gains_two_ref,
        fields_ref, send_ref, keep_ref, slope_s, packed_s, m_ref, n_ref,
        qkv_s, merged_ref, gs_ref, out_w_ref, values_ref, copied,
    ) = refs[1 + count * parts :]
    width = merged_ref.shape[1]
    thirds = [
        pltpu.make_async_copy(
            qkv_far.at[:, pl.ds(third * width, width)], qkv_s.at[third], copied.at[third]
        )
        for third in range(3)
    ]
    others = [
        pltpu.make_async_copy(far, near, copied.at[3 + i])
        for i, (far, near) in enumerate(
            [
                (merged_far, merged_ref), (gs_far, gs_ref), (out_w_far, out_w_ref),
                (values_far, values_ref),
            ]
        )
    ]
    for copy in thirds + others:
        copy.start()
    slots = real_ref.shape[0]
    if count == 1:
        packed = piece_refs[0][...]
    else:
        span = piece_refs[0].shape[1] // 3
        for third in range(3):
            for part in range(parts):
                for d in range(count):
                    at = third * (count * parts) + (place_ref[0] ^ d) * parts + part
                    packed_s[:, pl.ds(pl.multiple_of(at * span, span), span)] = piece_refs[
                        part * count + d
                    ][:, third * span : (third + 1) * span]
        packed = packed_s[...]
    pixel_rows = pix_ref[...]
    probs = variable_probs(pixel_rows, shi_ref[...], slo_ref[...], real_ref[...], slots)
    weights = probs.astype(bf16).astype(f32)
    pixels = pixel_rows.astype(f32).reshape(TABLES, slots, -1)
    upstream = None
    for third, copy in enumerate(thirds):
        copy.wait()
        product = dot_nt(packed[:, third * width : (third + 1) * width], qkv_s[third])
        upstream = product if upstream is None else upstream + product
    upstream = upstream.astype(bf16).astype(f32)
    for copy in others:
        copy.wait()
    unit_rows, inverse = norm_parts(merged_ref[...])
    g_merged = gs_ref[...] + norm_back(upstream, unit_rows, inverse, gain_ref[...])
    low = g_merged.astype(bf16)
    depth = pix_ref.shape[0]
    m_ref[...] = jnp.zeros_like(m_ref)
    m_ref[depth + 2 : depth + 4, :] = gains_two_ref[...]
    m_ref[depth : depth + 1, :] = jnp.sum(upstream * unit_rows, axis=0, keepdims=True)
    m_ref[depth + 1 : depth + 2, :] = jnp.sum(upstream, axis=0, keepdims=True)
    g_values = dot_nt(low, out_w_ref[...]).astype(bf16)
    grads = dot(values_ref[...], low)
    size = ev_ref.shape[2]
    g_fields = jnp.zeros(pixels.shape, f32)
    for h in range(HEADS):
        rows = g_values[:, h * size : (h + 1) * size]
        both = dot_nt(ev_ref[h], rows)
        table = (both[:depth] + both[depth:]).reshape(pixels.shape)
        g_weights = jnp.sum(pixels * table, axis=0)
        total = jnp.sum(g_weights * probs[h], axis=0, keepdims=True)
        slope_s[h * slots : (h + 1) * slots, :] = (probs[h] * (g_weights - total)).astype(bf16)
        g_fields += weights[h][None] * table
        mixed = (weights[h][None] * pixels).reshape(pixel_rows.shape)
        pair = dot(jnp.concatenate(split_two(mixed), axis=0), rows)
        m_ref[:depth, h * size : (h + 1) * size] = pair[:depth] + pair[depth:]
    slopes = slope_s[...]
    fields_ref[...] = (
        g_fields.reshape(pixel_rows.shape) + dot(sthi_ref[...], slopes) + dot(stlo_ref[...], slopes)
    ).astype(bf16)
    n_ref[...] = dot_nt(pixel_rows, slopes)

    core = place_ref[1]
    shard = grads.shape[0] // (2 * n_z)
    for zz in range(n_z):
        at = slice(zz * shard, (zz + 1) * shard)
        even = grads[2 * zz * shard : (2 * zz + 1) * shard]
        odd = grads[(2 * zz + 1) * shard : (2 * zz + 2) * shard]
        keep_ref[at] = jnp.where(core == 0, even, odd)
        send_ref[at] = jnp.where(core == 0, odd, even).astype(bf16)
    top = n_z * shard
    middle = top + m_ref.shape[0]
    tables = m_ref[...]
    keep_ref[top:middle] = tables
    send_ref[top:middle] = tables.astype(bf16)
    columns = lax.broadcasted_iota(jnp.int32, n_ref.shape, 1)
    same = columns % slots == lax.broadcasted_iota(jnp.int32, n_ref.shape, 0) % slots
    n_high, n_low = split_two(jnp.where(same, n_ref[...], 0.0))
    heads = (HEADS, n_ref.shape[1])
    picks = lax.broadcasted_iota(jnp.int32, heads, 1) // slots
    picks = jnp.where(picks == lax.broadcasted_iota(jnp.int32, heads, 0), 1.0, 0.0).astype(bf16)
    n_rows = dot_nt(picks, n_high) + dot_nt(picks, n_low)
    keep_ref[middle:] = jnp.zeros((HEADS, keep_ref.shape[1]), f32)
    keep_ref[middle:, :depth] = n_rows
    send_ref[middle:] = keep_ref[middle:].astype(bf16)


def per_device(
    n_var, n_z, fields, var_mask, embed_weight, var_embed, agg_query, agg_key, agg_value, agg_out,
    norm1_gain, norm1_bias, attn_qkv, attn_proj, norm2_gain, norm2_bias, mlp_in, mlp_out, cotangent,
):
    n_item = 2 * n_z
    width = agg_key.shape[0]
    size = width // HEADS
    scale = size ** (-0.5)
    hidden_width = mlp_in.shape[1]
    vars_here, channels, patches = fields.shape[1:]
    slot_count = var_mask.shape[1]
    slots = -(-slot_count // 16) * 16
    mine = patches // n_var
    here = HEADS // n_var
    cols = here * size
    shard = width // n_item
    me = lax.axis_index("var")
    core = lax.axis_index("core")
    z_at = lax.axis_index("z")
    item = z_at * 2 + core
    rel = me ^ jnp.arange(n_var)
    rel_z = z_at ^ jnp.arange(n_z)
    place = jnp.stack([me, core, z_at]).astype(jnp.int32)
    lanes_fit = cols % 128 == 0

    def send(array, other):
        return lax.ppermute(array, "var", [(i, i ^ other) for i in range(n_var)])

    def send_z(array, other):
        return lax.ppermute(array, "z", [(i, i ^ other) for i in range(n_z)])

    def swap_core(array):
        return lax.ppermute(array, "core", [(0, 1), (1, 0)])

    def canonical(by_distance):
        return jnp.take(jnp.stack(by_distance, axis=0), rel, axis=0)

    def call(kernel, grid, in_specs, out_specs, out_shape, scratch, estimate, name, *args):
        return pl.pallas_call(
            kernel,
            grid_spec=pltpu.PrefetchScalarGridSpec(
                num_scalar_prefetch=1,
                grid=grid,
                in_specs=in_specs,
                out_specs=out_specs,
                scratch_shapes=scratch,
            ),
            out_shape=out_shape,
            compiler_params=params(),
            cost_estimate=estimate,
            name=name,
        )(place, *args)

    depth = TABLES * slots
    pixel_part = jnp.concatenate([fields[0], jnp.ones((vars_here, 1, patches), bf16)], axis=1)
    table_part = jnp.concatenate([embed_weight, var_embed[:, None, :]], axis=1)
    piece = jnp.concatenate([pixel_part, table_part], axis=2).reshape(TABLES * vars_here, -1)
    pieces = [piece] + [send(piece, d) for d in range(1, n_var)]
    real = jnp.pad(var_mask[0], (0, slots - slot_count)).astype(f32)[:, None]
    prep_in = pieces + [agg_query[None], agg_key, agg_value]
    maps = [(HEADS * slots, depth)] * 2 + [(depth, HEADS * slots)] * 2
    prep_out = (
        [((depth, patches), bf16), ((depth, width), bf16)]
        + [(shape, bf16) for shape in maps]
        + [
            ((width, 3 * depth), bf16),
            ((HEADS, 2 * depth, size), bf16),
            ((depth, width), f32),
            ((width, HEADS), bf16),
            ((HEADS, width), bf16),
        ]
    )
    (
        pixels, tables, score_high, score_low, score_high_t, score_low_t, ev_front, ev_back,
        table_keys, query_keys, spread,
    ) = call(
        partial(prep_kernel, n_var, vars_here, patches),
        (1,),
        [whole(array.shape) for array in prep_in],
        [whole(shape) for shape, _ in prep_out],
        [jax.ShapeDtypeStruct(shape, kind) for shape, kind in prep_out],
        [pltpu.VMEM((depth, patches + width), bf16)],
        cost(8 * depth * width * width, 4 * width * width),
        "prep",
        *prep_in,
    )

    gain_one, bias_one = norm1_gain[None], norm1_bias[None]
    gain_two, bias_two = norm2_gain[None], norm2_bias[None]

    if lanes_fit:
        qkv_parts = [attn_qkv] * 3
        qkv_specs = [
            pl.BlockSpec((width, cols), lambda i, at, third=third: (0, third * n_var + at[0]))
            for third in range(3)
        ]
    else:
        qkv_mine = lax.dynamic_index_in_dim(
            attn_qkv.reshape(width, 3, n_var, cols), me, axis=2, keepdims=False
        )
        qkv_parts = [qkv_mine[:, third] for third in range(3)]
        qkv_specs = [whole((width, cols))] * 3

    block = min(512, mine)
    steps = patches // block
    own = mine // block
    heads_shape = jax.ShapeDtypeStruct((here, patches, size), bf16)
    heads_spec = pl.BlockSpec((here, block, size), lambda i, _: (0, i, 0))
    agg_values_t, merged, normed_send, normed_keep, queries, keys, values = call(
        partial(front_kernel, own, n_z),
        (steps,),
        [
            pl.BlockSpec((depth, block), lambda i, _: (0, i)),
            whole(score_high.shape),
            whole(score_low.shape),
            whole(real.shape),
            whole(ev_front.shape),
            whole(agg_out.shape),
            whole(gain_one.shape),
            whole(bias_one.shape),
        ]
        + qkv_specs,
        [
            pl.BlockSpec((width, block), lambda i, _: (0, jnp.minimum(i, own - 1))),
            pl.BlockSpec((block, width), lambda i, _: (jnp.minimum(i, own - 1), 0)),
            pl.BlockSpec((width // 2, block), lambda i, _: (0, i)),
            pl.BlockSpec((width // 2, block), lambda i, _: (0, i)),
            heads_spec,
            heads_spec,
            heads_spec,
        ],
        [
            jax.ShapeDtypeStruct((width, mine), bf16),
            jax.ShapeDtypeStruct((mine, width), f32),
            jax.ShapeDtypeStruct((width // 2, patches), bf16),
            jax.ShapeDtypeStruct((width // 2, patches), bf16),
            heads_shape,
            heads_shape,
            heads_shape,
        ],
        [pltpu.VMEM((width, block), f32), pltpu.VMEM((width, block), bf16)],
        cost(2 * patches * width * (width + 3 * cols + 256), 16 * patches * width),
        "front",
        pixels, score_high, score_low, real, ev_front, agg_out, gain_one, bias_one, *qkv_parts,
    )

    def attend(distance):
        heads = here
        return pl.pallas_call(
            attend_kernel,
            grid=(here // heads,),
            in_specs=[
                pl.BlockSpec((heads, mine, size), lambda i: (i, distance, 0)),
                pl.BlockSpec((heads, patches, size), lambda i: (i, 0, 0)),
                pl.BlockSpec((heads, patches, size), lambda i: (i, 0, 0)),
            ],
            out_specs=[
                pl.BlockSpec((mine, heads * size), lambda i: (0, i)),
                pl.BlockSpec((heads, 1, mine), lambda i: (i, 0, 0)),
            ],
            out_shape=[
                jax.ShapeDtypeStruct((mine, cols), bf16),
                jax.ShapeDtypeStruct((here, 1, mine), f32),
            ],
            compiler_params=params(),
            cost_estimate=cost(
                4 * mine * patches * here * 256, 4 * patches * cols * 2, mine * patches * here
            ),
            name=f"attend{distance}",
        )(queries, keys, values)

    attended_by, lse_by, arrived = [None] * n_var, [None] * n_var, [None] * n_var
    for distance in reversed(range(n_var)):
        attended_by[distance], lse_by[distance] = attend(distance)
        arrived[distance] = (
            send(attended_by[distance], distance) if distance else attended_by[distance]
        )
    if not lanes_fit:
        arrived = [canonical(arrived).transpose(1, 0, 2).reshape(mine, width)]

    cot = cotangent[0]
    tile = 2 * hidden_width // n_item
    row_f32 = jax.ShapeDtypeStruct((mine, width), f32)
    row_bf16 = jax.ShapeDtypeStruct((mine, width), bf16)
    row_spec = whole((mine, width))
    tall_spec = whole((width, mine))
    tall_bf16 = jax.ShapeDtypeStruct((width, mine), bf16)
    piece_spec = whole((mine, cols))
    (
        output, attended_t, normed_two_t, active_send, active_keep, g_hidden, g_stream, g_stream_low,
        gains_two,
        *g_attended,
    ) = call(
        partial(mlp_kernel, len(arrived), n_var),
        (hidden_width // tile,),
        [whole(piece.shape) for piece in arrived]
        + [
            row_spec,
            whole((width, width)),
            whole(gain_two.shape),
            whole(bias_two.shape),
            row_spec,
            pl.BlockSpec((width, tile), lambda i, _: (0, i)),
            pl.BlockSpec((tile, width), lambda i, _: (i, 0)),
        ],
        [
            row_spec,
            tall_spec,
            tall_spec,
            pl.BlockSpec((tile // 2, mine), lambda i, _: (i, 0)),
            pl.BlockSpec((tile // 2, mine), lambda i, _: (i, 0)),
            pl.BlockSpec((mine, tile), lambda i, _: (0, i)),
            row_spec,
            row_spec,
            whole((2, width)),
        ]
        + [piece_spec] * n_var,
        [
            row_bf16,
            tall_bf16,
            tall_bf16,
            jax.ShapeDtypeStruct((hidden_width // 2, mine), bf16),
            jax.ShapeDtypeStruct((hidden_width // 2, mine), bf16),
            jax.ShapeDtypeStruct((mine, hidden_width), bf16),
            row_f32,
            row_bf16,
            jax.ShapeDtypeStruct((2, width), f32),
        ]
        + [jax.ShapeDtypeStruct((mine, cols), bf16)] * n_var,
        [
            pltpu.VMEM((mine, width), bf16),
            pltpu.VMEM((mine, width), bf16),
            pltpu.VMEM((mine, width), f32),
            pltpu.VMEM((mine, width), f32),
            pltpu.VMEM((mine, 1), f32),
            pltpu.VMEM((mine, width), f32),
            pltpu.VMEM((mine, width), f32),
            pltpu.VMEM((tile, mine), bf16),
        ],
        cost(
            2 * mine * width * (4 * hidden_width + 2 * width),
            4 * width * hidden_width + 16 * mine * width,
        ),
        "mlp",
        *arrived, merged, attn_proj, gain_two, bias_two, cot, mlp_in, mlp_out,
    )
    g_heads = [g_attended[0]] + [send(g_attended[d], d) for d in range(1, n_var)]

    kept_rows = n_z * shard

    def pair_product(tall, grads):
        return dot(tall, grads).astype(bf16)

    def pair_own(tall, grads, got):
        return (dot(tall, grads) + got.astype(f32)).astype(bf16)

    def column_block(array, start=0, total=None):
        rows = array.shape[0]
        total = total or array.shape[1]
        span = total // n_var
        if span % 128 == 0:
            return array, pl.BlockSpec((rows, span), lambda j, at: (0, start // span + (at[0] ^ j)))
        cut = array[:, start : start + total]
        cut = jnp.take(cut.reshape(rows, n_var, span).transpose(1, 0, 2), rel, axis=0)
        return cut, pl.BlockSpec((None, rows, span), lambda j, at: (j, 0, 0))

    def pair_send_two(main, side):
        spec = pl.BlockSpec((n_z, None, shard, mine), lambda j, at: (0, 1 - at[1], 0, 0))
        tiles = hidden_width // width
        return call(
                send_kernel,
                (tiles + 1,),
                [
                    spec,
                    pl.BlockSpec((mine, width), lambda j, at: (0, jnp.minimum(j, tiles - 1))),
                    spec,
                    whole((mine, width)),
                ],
                pl.BlockSpec((kept_rows, width), lambda j, at: (0, j)),
                jax.ShapeDtypeStruct((kept_rows, hidden_width + width), bf16),
                [],
                cost(2 * kept_rows * mine * (hidden_width + width), 24 * kept_rows * width, share=2),
                "send",
                main[0].reshape(n_z, 2, shard, mine), main[1],
                side[0].reshape(n_z, 2, shard, mine), side[1],
            )

    def pair_keep(main, side, got):
        args, specs, start = [], [], 0
        for tall, grads in (main, side):
            args.append(tall.reshape(n_z, 2, shard, mine))
            specs.append(pl.BlockSpec((n_z, None, shard, mine), lambda j, at: (0, at[1], 0, 0)))
            for array, spec in (column_block(grads), column_block(got, start, grads.shape[1])):
                args.append(array)
                specs.append(spec)
            start += grads.shape[1]
        main_span, side_span = main[1].shape[1] // n_var, side[1].shape[1] // n_var
        first = 3 * main_span // 4
        spans = [first] * n_var + [main_span - first + side_span] * n_var
        outs = call(
            partial(keep_kernel, n_var),
            (n_var,),
            specs,
            [whole((kept_rows, span)) for span in spans],
            [jax.ShapeDtypeStruct((kept_rows, span), bf16) for span in spans],
            [],
            cost(
                2 * kept_rows * mine * (main_span + side_span) * n_var, 24 * kept_rows * main_span, share=2
            ),
            "keep",
            *args,
        )
        return outs[:n_var], outs[n_var:]

    def add_all(first, *others):
        total = first.astype(f32)
        for other in others:
            total = total + other.astype(f32)
        return total.astype(bf16)

    def exchange(pieces):
        return [pieces[0]] + [send(pieces[d], d) for d in range(1, n_var)]


    main, side = (normed_two_t, g_hidden), (attended_t, g_stream_low)
    sent = pair_send_two(main, side)
    sent, g_heads, active_send = lax.optimization_barrier((sent, g_heads, active_send))
    got = swap_core(sent)
    got_mlp_out = swap_core(pair_product(active_send, cot))
    first, second = pair_keep(main, side, got)
    active_keep, first, second = lax.optimization_barrier((active_keep, first, second))
    first = exchange(first)
    g_mlp_out = pair_own(active_keep, cot, got_mlp_out)
    mlp_out_rows = lax.psum_scatter(g_mlp_out, "z", scatter_dimension=0, tiled=True)
    g_heads, _ = lax.optimization_barrier((g_heads, g_mlp_out))

    group = min(2, here)
    parts = here // group
    gcols = group * size
    back_block = min(1024, patches)

    def attend_back(part, queries, extra):
        group_spec = pl.BlockSpec((group, back_block, size), lambda i: (part, i, 0))
        side_spec = pl.BlockSpec((mine, gcols), lambda i: (0, part))
        piece_cols = 3 * gcols + sum(array.shape[1] for array in extra[:1])
        full, *pieces = pl.pallas_call(
            partial(attend_back_kernel, n_var, len(extra)),
            grid=(patches // back_block,),
            in_specs=[whole(array.shape) for array in extra]
            + [
                pl.BlockSpec((group, patches, size), lambda i: (part, 0, 0)),
                group_spec,
                group_spec,
            ]
            + [pl.BlockSpec((group, 1, mine), lambda i: (part, 0, 0))] * n_var
            + [side_spec] * (2 * n_var),
            out_specs=[whole((patches, 3 * gcols))] + [whole((mine, piece_cols))] * n_var,
            out_shape=[jax.ShapeDtypeStruct((patches, 3 * gcols), bf16)]
            + [jax.ShapeDtypeStruct((mine, piece_cols), bf16)] * n_var,
            scratch_shapes=[
                pltpu.VMEM((group, patches, size), bf16),
                pltpu.VMEM((group, 1, patches), f32),
                pltpu.VMEM((group, 1, patches), f32),
                pltpu.VMEM((group, size, patches), f32),
                pltpu.VMEM((group, back_block, patches), bf16),
                pltpu.VMEM((group, back_block, patches), bf16),
            ],
            compiler_params=params(),
            cost_estimate=cost(
                10 * patches * patches * group * 256, 8 * patches * gcols * 2, patches * patches * group
            ),
            name=f"attend_back{part}",
        )(*extra, queries, keys, values, *lse_by, *attended_by, *g_heads)
        return full, pieces

    ride = kept_rows == mine and parts > 1
    g_qkv, packed_pieces = [], []
    for part in range(parts):
        full, pieces = attend_back(part, queries, second if ride and part == 0 else [])
        if part == 0:
            full, first = lax.optimization_barrier((full, first))
            first_sum = add_all(*first)
        if part < parts - 1:
            product = pair_product(normed_send, full)
            queries, first_sum, product = lax.optimization_barrier((queries, first_sum, product))
            g_qkv.append((full, product))
        if part == parts - 1:
            pieces, packed_pieces = lax.optimization_barrier((pieces, packed_pieces))
        packed_pieces += exchange(pieces)
    if ride:
        second = [piece[:, 3 * gcols :] for piece in packed_pieces[:n_var]]
    else:
        second = exchange(second)
    g_qkv.append((full, pair_product(normed_send, full)))
    second_sum = add_all(*second)
    columns = [first_sum, second_sum]
    columns += [pair_own(normed_keep, full, swap_core(product)) for full, product in g_qkv]
    both_sum = jnp.concatenate(columns, axis=1)
    def my_slice(array, axis):
        return lax.dynamic_slice_in_dim(array, item * shard, shard, axis=axis)

    packed_pieces, both_sum = lax.optimization_barrier((packed_pieces, both_sum))
    both_rows = lax.psum_scatter(both_sum, "z", scatter_dimension=0, tiled=True)
    count = n_var
    if not lanes_fit:
        packed = [
            canonical(packed_pieces[part * n_var : (part + 1) * n_var]) for part in range(parts)
        ]
        packed = jnp.stack(packed, axis=0).reshape(parts, n_var, mine, 3, gcols)
        packed_pieces = [packed.transpose(2, 3, 1, 0, 4).reshape(mine, 3 * width)]
        count, parts = 1, 1
    packed_cols = 3 * gcols if lanes_fit else 3 * width

    far = pl.BlockSpec(memory_space=pl.ANY)
    table_rows = -(-(depth + 4) // 16) * 16
    late_rows = kept_rows + table_rows
    g_fields, late_send, late_keep = call(
        partial(back_kernel, count, parts, n_z),
        (1,),
        [pl.BlockSpec((block, packed_cols), lambda i, _: (i, 0)) for piece in packed_pieces]
        + [
            far,
            far,
            whole(gain_one.shape),
            far,
            far,
            pl.BlockSpec((depth, block), lambda i, _: (0, i)),
            whole(score_high.shape),
            whole(score_low.shape),
            whole((depth, HEADS * slots)),
            whole((depth, HEADS * slots)),
            whole(real.shape),
            whole(ev_back.shape),
            far,
            whole((2, width)),
        ],
        [
            pl.BlockSpec((depth, block), lambda i, _: (0, i)),
            whole((late_rows + HEADS, width)),
            whole((late_rows + HEADS, width)),
        ],
        [
            jax.ShapeDtypeStruct((depth, mine), bf16),
            jax.ShapeDtypeStruct((late_rows + HEADS, width), bf16),
            jax.ShapeDtypeStruct((late_rows + HEADS, width), f32),
        ],
        [
            pltpu.VMEM((HEADS * slots, block), bf16),
            pltpu.VMEM((block, 3 * width), bf16),
            pltpu.VMEM((table_rows, width), f32),
            pltpu.VMEM((depth, HEADS * slots), f32),
            pltpu.VMEM((3, width, width), bf16),
            pltpu.VMEM((mine, width), f32),
            pltpu.VMEM((mine, width), f32),
            pltpu.VMEM((width, width), bf16),
            pltpu.VMEM((width, mine), bf16),
            pltpu.SemaphoreType.DMA((7,)),
        ],
        cost(2 * mine * width * 4 * width, 8 * width * width + 20 * mine * width),
        "back",
        *packed_pieces, attn_qkv, merged, gain_one, g_stream, agg_out, pixels, score_high, score_low,
        score_high_t, score_low_t, real, ev_back, agg_values_t, gains_two,
    )

    late_send, mlp_out_rows = lax.optimization_barrier((late_send, mlp_out_rows))
    out_block = mlp_out_rows.shape[0] // n_var
    mlp_out_by = exchange(
        [
            lax.dynamic_slice_in_dim(mlp_out_rows, (me ^ d) * out_block, out_block, axis=0)
            for d in range(n_var)
        ]
    )
    mlp_out_rows = add_all(*mlp_out_by).reshape(shard, -1)

    late_got = swap_core(late_send)
    late_span = width // n_var
    n_blocks = -(-depth // late_span)
    n_spec = pl.BlockSpec((HEADS, n_blocks * late_span), lambda j, at: (late_rows // HEADS, 0))
    sum_rows = late_rows + n_blocks * HEADS
    f_rows = -(-channels * vars_here // 16) * 16
    piece_rows = sum_rows + f_rows * (mine // late_span)
    late_args = [late_keep, late_got]
    if late_span % 128:
        late_args = [
            jnp.take(array.reshape(-1, n_var, late_span).transpose(1, 0, 2), rel, axis=0)
            for array in late_args
        ]
    late_pieces = call(
        partial(pair_kernel, n_var, channels, vars_here, late_rows),
        (1,),
        [whole(array.shape) for array in late_args] + [n_spec, n_spec, whole((depth, mine))],
        [whole((piece_rows, late_span))] * n_var,
        [jax.ShapeDtypeStruct((piece_rows, late_span), bf16)] * n_var,
        [],
        cost(piece_rows * width, 8 * piece_rows * width),
        "late_pair",
        *late_args, late_keep, late_got, g_fields,
    )
    late_pieces = exchange(late_pieces)
    late_pieces, both_rows = lax.optimization_barrier((late_pieces, both_rows))
    rows_all = jnp.concatenate([both_rows, mlp_out_rows], axis=1)
    halves = 1 if n_var == 4 and lanes_fit else 0
    if halves:
        near = [send(rows_all, 1), send(rows_all, 2)]
    else:
        rows_all = list(lax.all_gather(rows_all, "var", axis=0))
    z_rows = shard + table_rows + n_blocks * HEADS
    *z_pieces, fields_grad = call(
        partial(z_pieces_kernel, n_var, shard, n_z),
        (1,),
        [whole((piece_rows, late_span))] * n_var,
        [whole((z_rows, late_span))] * n_z + [whole((f_rows, patches))],
        [jax.ShapeDtypeStruct((z_rows, late_span), bf16)] * n_z
        + [jax.ShapeDtypeStruct((f_rows, patches), f32)],
        [pltpu.VMEM((sum_rows, late_span), bf16)],
        cost(piece_rows * width, 2 * piece_rows * width),
        "late_z",
        *late_pieces,
    )
    z_pieces = [z_pieces[0]] + [send_z(z_pieces[d], d) for d in range(1, n_z)]
    late_rows_mine, n_all = pl.pallas_call(
        partial(z_sum_kernel, n_z),
        out_shape=[
            jax.ShapeDtypeStruct((shard + table_rows, late_span), bf16),
            jax.ShapeDtypeStruct((HEADS, n_blocks * late_span), f32),
        ],
        compiler_params=params(),
        cost_estimate=cost(z_rows * width, 2 * z_rows * width),
        name="late_sum",
    )(*z_pieces)

    fields_grad = fields_grad[: channels * vars_here].reshape(1, vars_here, channels, patches)
    if halves:
        late_rows_mine, near = lax.optimization_barrier((late_rows_mine, near))
        half = rows_all.shape[1] // 2
        rows_all = [rows_all] + near + [send(near[0][:, :half], 2), send(near[1][:, half:], 1)]
    late_by = exchange([late_rows_mine] * n_var)
    if late_span % 128:
        late_by = [canonical(late_by).transpose(1, 0, 2).reshape(shard + table_rows, width)]
    small_shapes = [(1, width), (channels * vars_here, shard), (vars_here, shard), (8, width)]
    final_in = [n_all, my_slice(tables, 1).T, spread, table_keys]
    item_rows = [
        pl.BlockSpec((shard, width), lambda i, at: (2 * at[2] + at[1], 0)),
        pl.BlockSpec((shard, HEADS), lambda i, at: (2 * at[2] + at[1], 0)),
    ]
    agg_out_grad, agg_value_grad, agg_key_grad, query_row, embed_weight_grad, var_embed_grad, gains = call(
        partial(final_kernel, len(late_by)),
        (1,),
        [whole(array.shape) for array in late_by + final_in] + item_rows,
        [whole((shard, width))] * 3
        + [whole(shape) for shape in small_shapes],
        [jax.ShapeDtypeStruct((shard, width), f32)] * 3
        + [jax.ShapeDtypeStruct(shape, f32) for shape in small_shapes],
        [pltpu.VMEM((table_rows, width), f32)],
        cost(2 * shard * width * 3 * depth, 12 * shard * width),
        "final",
        *late_by, *final_in, agg_value, query_keys,
    )
    gains = my_slice(gains, 1)
    agg_query_grad = my_slice(query_row[0], 0) * scale
    embed_weight_grad = embed_weight_grad.reshape(vars_here, channels, shard)

    row_shapes = [
        jax.ShapeDtypeStruct((shard, hidden_width), f32),
        jax.ShapeDtypeStruct((shard, width), f32),
        jax.ShapeDtypeStruct((shard, 3 * width), f32),
        jax.ShapeDtypeStruct((n_var, shard, out_block * width // shard), f32),
    ]
    mlp_in_grad, attn_proj_grad, attn_qkv_grad, mlp_out_grad = call(
        partial(assemble_kernel, n_var, here // group, gcols, halves),
        (1,),
        [whole(array.shape) for array in rows_all],
        [whole(row.shape) for row in row_shapes],
        row_shapes,
        [],
        cost(shard * 9 * width, 6 * shard * 9 * width),
        "assemble",
        *rows_all,
    )
    mlp_out_grad = mlp_out_grad.reshape(n_var * out_block, width)
    return (
        output[None],
        fields_grad,
        embed_weight_grad,
        var_embed_grad,
        agg_query_grad,
        agg_key_grad,
        agg_value_grad,
        agg_out_grad,
        gains[0],
        gains[1],
        attn_qkv_grad,
        attn_proj_grad,
        gains[2],
        gains[3],
        mlp_in_grad,
        mlp_out_grad,
    )


def solution(mesh):
    n_var, n_item = mesh.shape["var"], mesh.shape["item"]
    items = ("z", "core")
    return jax.shard_map(
        partial(per_device, n_var, n_item // 2),
        mesh=Mesh(mesh.devices.reshape(n_var, n_item // 2, 2), ("var", "z", "core")),
        in_specs=(
            P(items, "var", None, None),
            P(items, None),
            P("var", None, None),
            P("var", None),
            P(),
            P(),
            P(),
            P(),
            P(),
            P(),
            P(),
            P(),
            P(),
            P(),
            P(),
            P(),
            P(items, "var", None),
        ),
        out_specs=(
            P(items, "var", None),
            P(items, "var", None, None),
            P("var", None, items),
            P("var", items),
            P(items),
            P(items, None),
            P(items, None),
            P(items, None),
            P(items),
            P(items),
            P(items, None),
            P(items, None),
            P(items),
            P(items),
            P(items, None),
            P(items, None),
        ),
        check_vma=False,
    )
```

```python
from functools import partial

import jax
import jax.numpy as jnp
from jax import lax
from jax.experimental import pallas as pl
from jax.experimental.pallas import tpu as pltpu
from jax.sharding import Mesh
from jax.sharding import PartitionSpec as P

HEADS = 16
TABLES = 5

epsilon = 1e-05
masked_score = -1e30
highest = lax.Precision.HIGHEST
f32 = jnp.float32
bf16 = jnp.bfloat16
COST = 0.05
VMEM_BYTES = 56 * 1024 * 1024
LOG2E = 1.4426950408889634


def dot(a, b):
    return lax.dot_general(a, b, (((1,), (0,)), ((), ())), preferred_element_type=f32)


def dot_nt(a, b):
    return lax.dot_general(a, b, (((1,), (1,)), ((), ())), preferred_element_type=f32)


def dot_tn(a, b):
    return lax.dot_general(a, b, (((0,), (0,)), ((), ())), preferred_element_type=f32)


def split_two(wide):
    high = wide.astype(bf16)
    return high, (wide - high.astype(f32)).astype(bf16)


def split_three(wide):
    high, rest = split_two(wide)
    low = wide - high.astype(f32) - rest.astype(f32)
    return high, rest, low.astype(bf16)


def columns(parts, rows, width):
    lane = lax.broadcasted_iota(jnp.int32, (rows, width), 1)
    out = jnp.zeros((rows, width), f32)
    for i, part in enumerate(parts):
        out = jnp.where(lane == i, part.astype(f32), out)
    return out.astype(bf16)


def whole(shape):
    return pl.BlockSpec(shape, lambda *_: (0,) * len(shape))


def params(vmem=VMEM_BYTES):
    return pltpu.CompilerParams(vmem_limit_bytes=vmem)


def cost(flops, bytes_accessed, transcendentals=0, share=COST):
    return pl.CostEstimate(
        flops=int(flops * share), bytes_accessed=int(bytes_accessed * share), transcendentals=0
    )


def norm_parts(stream):
    centred = stream - jnp.mean(stream, axis=-1, keepdims=True)
    inverse = lax.rsqrt(jnp.mean(centred * centred, axis=-1, keepdims=True) + epsilon)
    return centred * inverse, inverse


def norm_back(upstream, unit_rows, inverse, gain):
    scaled = upstream * gain
    return inverse * (
        scaled
        - jnp.mean(scaled, axis=-1, keepdims=True)
        - unit_rows * jnp.mean(scaled * unit_rows, axis=-1, keepdims=True)
    )


def variable_probs(pixel_rows, score_high, score_low, real, slots):
    scores = dot(score_high, pixel_rows) + dot(score_low, pixel_rows)
    scores = scores.reshape(HEADS, slots, pixel_rows.shape[1])
    scores = jnp.where(real[None] > 0, scores, masked_score)
    powers = jnp.exp(scores - jnp.max(scores, axis=1, keepdims=True))
    return powers / jnp.sum(powers, axis=1, keepdims=True)


def prep_kernel(count, vars_here, patches, *refs):
    place_ref = refs[0]
    pieces = refs[1 : 1 + count]
    query_ref, key_ref, value_ref = refs[1 + count : 4 + count]
    (
        pix_ref, tables_ref, shi_ref, slo_ref, sthi_ref, stlo_ref, front_ref, back_ref, keys_ref,
        qk_ref, spread_ref, all_s,
    ) = refs[4 + count :]
    me = place_ref[0]
    depth, width = tables_ref.shape
    slots = depth // TABLES
    size = width // HEADS
    rows = TABLES * vars_here
    total = None
    for d in range(count):
        row = lax.broadcasted_iota(jnp.int32, (depth, rows), 0)
        col = lax.broadcasted_iota(jnp.int32, (depth, rows), 1)
        want = (col % TABLES) * slots + (me ^ d) * vars_here + col // TABLES
        part = dot(jnp.where(row == want, 1.0, 0.0).astype(bf16), pieces[d][...])
        total = part if total is None else total + part
    all_s[...] = total.astype(bf16)
    mine = patches // count
    for d in range(count):
        at = pl.multiple_of((me ^ d) * mine, mine)
        pix_ref[:, d * mine : (d + 1) * mine] = all_s[:, pl.ds(at, mine)]
    tables = all_s[:, patches:]
    tables_ref[...] = tables
    head = lax.broadcasted_iota(jnp.int32, (HEADS, width), 0)
    same = lax.broadcasted_iota(jnp.int32, (HEADS, width), 1) // size == head
    spread = jnp.where(same, query_ref[...].astype(f32), 0.0)
    scale = size ** (-0.5)
    spread_ref[...] = (spread * scale).astype(bf16)
    query_keys = (dot_nt(key_ref[...], spread.astype(bf16)) * scale).astype(bf16)
    qk_ref[...] = query_keys
    halves = split_two(dot(tables, query_keys))
    wide = HEADS * slots
    picks = lax.broadcasted_iota(jnp.int32, (wide, HEADS), 0) // slots
    picks = jnp.where(picks == lax.broadcasted_iota(jnp.int32, (wide, HEADS), 1), 1.0, 0.0).astype(bf16)
    for half, tall, flat in zip(halves, (shi_ref, slo_ref), (sthi_ref, stlo_ref)):
        row = lax.broadcasted_iota(jnp.int32, (wide, depth), 0) % slots
        col = lax.broadcasted_iota(jnp.int32, (wide, depth), 1) % slots
        tall[...] = jnp.where(row == col, dot_nt(picks, half), 0.0).astype(bf16)
        row = lax.broadcasted_iota(jnp.int32, (depth, wide), 0) % slots
        col = lax.broadcasted_iota(jnp.int32, (depth, wide), 1) % slots
        flat[...] = jnp.where(row == col, dot_nt(half, picks), 0.0).astype(bf16)
    mixed = dot(tables, value_ref[...])
    high, low = split_two(mixed)
    high_wide, low_wide = high.astype(f32), low.astype(f32)
    front_ref[...] = jnp.concatenate([high_wide, high_wide, low_wide], axis=0).T.astype(bf16)
    both = jnp.concatenate([high, low], axis=0)
    for h in range(HEADS):
        back_ref[h] = both[:, h * size : (h + 1) * size]
    keys_ref[...] = dot(tables, key_ref[...])


def front_kernel(
    own_blocks, n_z, place_ref, pix_ref, shi_ref, slo_ref, real_ref, ev_ref, out_w_ref, gain_ref,
    bias_ref, wq_ref, wk_ref, wv_ref,
    values_ref, merged_ref, send_ref, keep_ref, q_ref, k_ref, v_ref, flat_ref, tall_s,
):
    slots = real_ref.shape[0]
    pixel_rows = pix_ref[...]
    probs = variable_probs(pixel_rows, shi_ref[...], slo_ref[...], real_ref[...], slots)
    weights = probs.astype(bf16).astype(f32)
    pixels = pixel_rows.astype(f32).reshape(TABLES, slots, -1)
    size = ev_ref.shape[0] // HEADS
    for h in range(HEADS):
        mixed = (weights[h][None] * pixels).reshape(pixel_rows.shape)
        high, low = split_two(mixed)
        flat_ref[h * size : (h + 1) * size, :] = dot(
            ev_ref[h * size : (h + 1) * size, :], jnp.concatenate([high, low, high], axis=0)
        )
    values = flat_ref[...].astype(bf16)
    merged = dot(values.T, out_w_ref[...])

    @pl.when(pl.program_id(0) < own_blocks)
    def _():
        values_ref[...] = values
        merged_ref[...] = merged

    unit_rows, _ = norm_parts(merged)
    normed = (unit_rows * gain_ref[...] + bias_ref[...]).astype(bf16)
    tall_s[...] = normed.T
    core, shard = place_ref[1], tall_s.shape[0] // (2 * n_z)
    for zz in range(n_z):
        at = slice(zz * shard, (zz + 1) * shard)
        keep_ref[at] = tall_s[pl.ds(pl.multiple_of((2 * zz + core) * shard, shard), shard), :]
        send_ref[at] = tall_s[pl.ds(pl.multiple_of((2 * zz + 1 - core) * shard, shard), shard), :]
    queries = dot(normed, wq_ref[...]).astype(bf16).astype(f32) * size ** (-0.5)
    keys = dot(normed, wk_ref[...])
    values = dot(normed, wv_ref[...])
    for h in range(q_ref.shape[0]):
        at = h * size
        q_ref[h] = queries[:, at : at + size].astype(bf16)
        k_ref[h] = keys[:, at : at + size].astype(bf16)
        v_ref[h] = values[:, at : at + size].astype(bf16)


def attend_kernel(q_ref, k_ref, v_ref, out_ref, lse_ref):
    here, rows, size = q_ref.shape
    block = min(512, rows)
    pieces = [(h, at) for at in range(0, rows, block) for h in range(here)]

    def scores_of(piece):
        h, at = piece
        return dot_nt(q_ref[h, at : at + block], k_ref[h])

    def finish(piece, powers, top, total):
        h, at = piece
        mixed = dot(powers, v_ref[h]) / total
        lse = jnp.broadcast_to(top + jnp.log(total), (block, 128)).T[0:1]
        return mixed.astype(bf16), lse

    done, waiting = {}, None
    scores = scores_of(pieces[0])
    for i, piece in enumerate(pieces):
        later = scores_of(pieces[i + 1]) if i + 1 < len(pieces) else None
        top = jnp.max(scores, axis=-1, keepdims=True)
        powers = jnp.exp(scores - top)
        total = jnp.sum(powers, axis=-1, keepdims=True)
        if waiting is not None:
            done[waiting[0]] = finish(*waiting)
        waiting = (piece, powers.astype(bf16), top, total)
        scores = later
    done[waiting[0]] = finish(*waiting)
    for h, at in pieces:
        lse_ref[h, :, at : at + block] = done[h, at][1]
    for at in range(0, rows, block):
        out_ref[at : at + block] = jnp.concatenate([done[h, at][0] for h in range(here)], axis=-1)


def attend_back_kernel(count, extra, *refs):
    extra_refs, refs = refs[:extra], refs[extra:]
    q_ref, k_ref, v_ref = refs[:3]
    lse_refs = refs[3 : 3 + count]
    out_refs = refs[3 + count : 3 + 2 * count]
    up_refs = refs[3 + 2 * count : 3 + 3 * count]
    full_ref = refs[3 + 3 * count]
    piece_refs = refs[4 + 3 * count : 4 + 4 * count]
    up_heads, total_rows, lse_rows, gq_ref, prob_s, slope_s = refs[4 + 4 * count :]
    step = pl.program_id(0)
    here, patches, size = q_ref.shape
    block = k_ref.shape[1]
    width = here * size
    mine = patches // count

    @pl.when(step == 0)
    def _():
        for h in range(here):
            at = h * size
            for d in range(count):
                rows = slice(d * mine, (d + 1) * mine)
                upstream = up_refs[d][:, at : at + size]
                up_heads[h, rows] = upstream
                product = upstream.astype(f32) * out_refs[d][:, at : at + size].astype(f32)
                total_rows[h, :, rows] = jnp.sum(product.T, axis=0, keepdims=True)
                lse_rows[h, :, rows] = lse_refs[d][h]
            gq_ref[h] = jnp.zeros(gq_ref.shape[1:], f32)

    chunk = min(256, patches)
    key_parts, value_parts = [], []
    for h in range(here):
        keys, values = k_ref[h], v_ref[h]
        for at in range(0, patches, chunk):
            span = slice(at, at + chunk)
            probs = jnp.exp(dot_nt(keys, q_ref[h, span]) - lse_rows[h, :, span])
            prob_s[h, :, span] = probs.astype(bf16)
            grads = dot_nt(values, up_heads[h, span])
            slope_s[h, :, span] = (probs * (grads - total_rows[h, :, span])).astype(bf16)
        value_parts.append(dot(prob_s[h], up_heads[h]))
        key_parts.append(dot(slope_s[h], q_ref[h]))
        gq_ref[h] += dot(keys.astype(f32).T.astype(bf16), slope_s[h])
    rows = pl.ds(pl.multiple_of(step * block, block), block)
    full_ref[rows, width : 2 * width] = jnp.concatenate(key_parts, axis=-1).astype(bf16)
    full_ref[rows, 2 * width :] = jnp.concatenate(value_parts, axis=-1).astype(bf16)

    @pl.when(step == pl.num_programs(0) - 1)
    def _():
        scale = size ** (-0.5)
        query_parts = [gq_ref[h].T for h in range(here)]
        full_ref[:, :width] = (jnp.concatenate(query_parts, axis=-1) * scale).astype(bf16)
        for d in range(count):
            piece_refs[d][:, : 3 * width] = full_ref[d * mine : (d + 1) * mine, :]

    if extra:

        @pl.when(step == 0)
        def _():
            for d in range(count):
                piece_refs[d][:, 3 * width :] = extra_refs[d][...]


def mlp_kernel(pieces, count, *refs):
    place_ref = refs[0]
    att_refs = refs[1 : 1 + pieces]
    merged_ref, proj_ref, gain_ref, bias_ref, cot_ref, win_ref, wout_ref = refs[1 + pieces : 8 + pieces]
    outs = refs[8 + pieces :]
    (
        out_ref, att_t_ref, normed_t_ref, send_ref, keep_ref, ghid_ref, gstream_ref, glow_ref,
        gains_ref,
    ) = outs[:9]
    gatt_refs = outs[9 : 9 + count]
    att_s, normed_s, stream_s, unit_s, inv_s, out_s, gn_s, tall_s = outs[9 + count :]
    step = pl.program_id(0)
    me = place_ref[0]
    cols = gatt_refs[0].shape[1]

    @pl.when(step == 0)
    def _():
        if pieces == 1:
            attended = att_refs[0][...]
        else:
            for d in range(pieces):
                att_s[:, pl.ds(pl.multiple_of((me ^ d) * cols, cols), cols)] = att_refs[d][...]
            attended = att_s[...]
        att_t_ref[...] = attended.T
        stream = merged_ref[...] + dot(attended, proj_ref[...])
        unit_rows, inverse = norm_parts(stream)
        stream_s[...] = stream
        unit_s[...] = unit_rows
        inv_s[...] = inverse
        normed = (unit_rows * gain_ref[...] + bias_ref[...]).astype(bf16)
        normed_s[...] = normed
        normed_t_ref[...] = normed.T
        out_s[...] = jnp.zeros_like(out_s)
        gn_s[...] = jnp.zeros_like(gn_s)

    tile = ghid_ref.shape[1]
    sub = min(256, tile)
    spans = [slice(at, at + sub) for at in range(0, tile, sub)]
    normed_rows, upstream_rows = normed_s[...], cot_ref[...]

    def products(span):
        return dot(normed_rows, win_ref[:, span]), dot_nt(upstream_rows, wout_ref[span, :])

    def shape(hidden, g_active):
        below = 0.5 + 0.5 * lax.erf(hidden * (0.5**0.5))
        density = jnp.exp(-0.5 * hidden * hidden) * ((2.0 * jnp.pi) ** (-0.5))
        return (hidden * below).astype(bf16), (g_active * (below + hidden * density)).astype(bf16)

    actives, grads, sums = [], [], []

    def add(first, last):
        span = slice(spans[first].start, spans[last].stop)
        active = jnp.concatenate(actives[first : last + 1], axis=1)
        grad = jnp.concatenate(grads[first : last + 1], axis=1)
        sums.append((dot(active, wout_ref[span, :]), dot_nt(grad, win_ref[:, span])))

    ready = products(spans[0])
    for i, span in enumerate(spans):
        later = products(spans[i + 1]) if i + 1 < len(spans) else None
        if i == len(spans) // 2 + 1:
            add(0, len(spans) // 2 - 1)
        active, grad = shape(*ready)
        actives.append(active)
        grads.append(grad)
        ready = later
    add(len(spans) // 2 if sums else 0, len(spans) - 1)
    for span, active, grad in zip(spans, actives, grads):
        ghid_ref[:, span] = grad
        tall_s[span, :] = active.T
    half = tile // 2
    core = place_ref[1]
    send_ref[...] = tall_s[pl.ds(pl.multiple_of((1 - core) * half, half), half), :]
    keep_ref[...] = tall_s[pl.ds(pl.multiple_of(core * half, half), half), :]
    out_s[...] += sum(pair[0] for pair in sums)
    gn_s[...] += sum(pair[1] for pair in sums)

    @pl.when(step == pl.num_programs(0) - 1)
    def _():
        out_ref[...] = (stream_s[...] + out_s[...]).astype(bf16)
        upstream = gn_s[...].astype(bf16).astype(f32)
        unit_rows = unit_s[...]
        g_stream = cot_ref[...].astype(f32) + norm_back(
            upstream, unit_rows, inv_s[...], gain_ref[...]
        )
        gstream_ref[...] = g_stream
        low = g_stream.astype(bf16)
        glow_ref[...] = low
        for d in range(count):
            rows = pl.ds(pl.multiple_of((me ^ d) * cols, cols), cols)
            gatt_refs[d][...] = dot_nt(low, proj_ref[rows, :]).astype(bf16)
        gains_ref[0:1, :] = jnp.sum(upstream * unit_rows, axis=0, keepdims=True)
        gains_ref[1:2, :] = jnp.sum(upstream, axis=0, keepdims=True)


def send_kernel(place_ref, main_rows, main_cols, side_rows, side_cols, out_ref):
    last = pl.program_id(0) == pl.num_programs(0) - 1

    def product(rows_ref, cols_ref):
        tall = rows_ref[...].reshape(-1, rows_ref.shape[-1])
        return dot(tall, cols_ref[...]).astype(bf16)

    @pl.when(jnp.logical_not(last))
    def _():
        out_ref[...] = product(main_rows, main_cols)

    @pl.when(last)
    def _():
        out_ref[...] = product(side_rows, side_cols)


def keep_kernel(count, *refs):
    main_rows, main_cols, main_got, side_rows, side_cols, side_got = refs[1:7]
    outs = refs[7:]
    step = pl.program_id(0)

    def product(rows_ref, cols_ref, got_ref):
        tall = rows_ref[...].reshape(-1, rows_ref.shape[-1])
        return (dot(tall, cols_ref[...]) + got_ref[...].astype(f32)).astype(bf16)

    for d in range(count):

        @pl.when(step == d)
        def _():
            first, second = outs[d], outs[count + d]
            main = product(main_rows, main_cols, main_got)
            cut = first.shape[1]
            rest = main.shape[1] - cut
            first[...] = main[:, :cut]
            second[:, :rest] = main[:, cut:]
            second[:, rest:] = product(side_rows, side_cols, side_got)


def pair_kernel(count, channels, vars_here, late_rows, *refs):
    place_ref = refs[0]
    keep_ref, got_ref, n_keep_ref, n_got_ref, fields_ref = refs[1:6]
    outs = refs[6:]
    depth, mine = fields_ref.shape
    rows = late_rows
    span = outs[0].shape[1]
    slots = depth // TABLES
    n_blocks = n_keep_ref.shape[1] // span
    f_rows = (outs[0].shape[0] - rows - n_blocks * HEADS) // (mine // span)
    row = lax.broadcasted_iota(jnp.int32, (f_rows, depth), 0)
    col = lax.broadcasted_iota(jnp.int32, (f_rows, depth), 1)
    n_total = (n_keep_ref[...] + n_got_ref[...].astype(f32)).astype(bf16)
    for d in range(count):
        q = place_ref[0] ^ d

        def block(ref):
            if len(ref.shape) == 3:
                return ref[d, :rows].astype(f32)
            return ref[:rows, pl.ds(pl.multiple_of(q * span, span), span)].astype(f32)

        outs[d][:rows] = (block(keep_ref) + block(got_ref)).astype(bf16)
        want = (row % channels) * slots + q * vars_here + row // channels
        picks = jnp.where((want == col) & (row < channels * vars_here), 1.0, 0.0).astype(bf16)
        picked = dot(picks, fields_ref[...]).astype(bf16)
        at = rows
        for b in range(n_blocks):
            outs[d][at : at + HEADS] = n_total[:, b * span : (b + 1) * span]
            at += HEADS
        for b in range(mine // span):
            outs[d][at : at + f_rows] = picked[:, b * span : (b + 1) * span]
            at += f_rows


def z_pieces_kernel(count, shard, n_z, *refs):
    pieces, outs, fields_ref, total_s = refs[1 : 1 + count], refs[1 + count : -2], refs[-2], refs[-1]
    me, z_at = refs[0][0], refs[0][2]
    rows, span = total_s.shape
    vars_here, channels, patches = fields_ref.shape
    mine = patches // count
    f_rows = (pieces[0].shape[0] - rows) // (mine // span)
    total = pieces[0][:rows].astype(f32)
    for piece in pieces[1:]:
        total = total + piece[:rows].astype(f32)
    total_s[...] = total.astype(bf16)
    for d in range(n_z):
        start = pl.multiple_of((z_at ^ d) * shard, shard)
        outs[d][:shard] = total_s[pl.ds(start, shard), :]
        outs[d][shard:] = total_s[n_z * shard :, :]
    for d in range(count):
        blocks = [
            pieces[d][rows + b * f_rows : rows + (b + 1) * f_rows] for b in range(mine // span)
        ]
        at = pl.multiple_of((me ^ d) * mine, mine)
        block = jnp.concatenate(blocks, axis=1).astype(f32)
        for v in range(vars_here):
            fields_ref[v, :, pl.ds(at, mine)] = block[v * channels : (v + 1) * channels]


def assemble_kernel(count, parts, size, halves, *refs):
    me = refs[0][0]
    blocks, outs = refs[1 : 1 + count + halves], refs[1 + count + halves :]
    in_ref, proj_ref, qkv_ref, out_ref = outs
    a = in_ref.shape[1] // count
    b = proj_ref.shape[1] // count
    width = proj_ref.shape[1]
    for d in range(count):
        if halves and d == count - 1:
            rows = jnp.concatenate([ref[...] for ref in blocks[d:]], axis=1)
        else:
            rows = blocks[d][...]
        rows = rows.astype(f32)
        q = me ^ d if halves else d

        def span(at, step):
            return pl.ds(pl.multiple_of(at, step) if halves else at, step)

        in_ref[:, span(q * a, a)] = rows[:, :a]
        proj_ref[:, span(q * b, b)] = rows[:, a : a + b]
        at = a + b
        for part in range(parts):
            for third in range(3):
                to = third * width + q * b + part * size
                qkv_ref[:, span(to, size)] = rows[:, at : at + size]
                at += size
        out_ref[q] = rows[:, at:]


def z_sum_kernel(count, *refs):
    pieces, (rows_ref, n_ref) = refs[:count], refs[count:]
    total = pieces[0][...].astype(f32)
    for piece in pieces[1:]:
        total = total + piece[...].astype(f32)
    rows, span = rows_ref.shape
    rows_ref[...] = total[:rows].astype(bf16)
    for b in range(n_ref.shape[1] // span):
        n_ref[:, b * span : (b + 1) * span] = total[rows + b * HEADS : rows + (b + 1) * HEADS]


def final_kernel(count, *refs):
    place_ref = refs[0]
    pieces = refs[1 : 1 + count]
    n_ref, tables_ref, spread_ref, keys_ref, value_ref, qk_ref = refs[1 + count : 7 + count]
    outg_ref, valg_ref, keyg_ref, embedg_ref, varg_ref = refs[7 + count : 12 + count]
    *row_refs, m_s, row_s = refs[12 + count :]
    shard, depth = tables_ref.shape
    width = m_s.shape[1]
    for d in range(count):
        span = pieces[d].shape[1]
        at = 0 if count == 1 else pl.multiple_of((place_ref[0] ^ d) * span, span)
        outg_ref[:, pl.ds(at, span)] = pieces[d][:shard].astype(f32)
        m_s[:, pl.ds(at, span)] = pieces[d][shard:].astype(f32)
    m_low = m_s[:depth, :].astype(bf16)
    n_high, n_low = split_two(n_ref[:, :depth])
    tables = tables_ref[...]
    valg_ref[...] = dot(tables, m_low)
    g_qk = dot_nt(tables, n_high) + dot_nt(tables, n_low)
    qk_high, qk_low = split_two(g_qk)
    spread = spread_ref[...]
    keyg_ref[...] = dot(qk_high, spread) + dot(qk_low, spread)
    head_at = lax.broadcasted_iota(jnp.int32, (HEADS, width), 1) // (width // HEADS)
    same = head_at == lax.broadcasted_iota(jnp.int32, (HEADS, width), 0)
    ones = jnp.where(same, 1.0, 0.0).astype(bf16)
    n_wide = dot(n_high.astype(f32).T.astype(bf16), ones) + dot(n_low.astype(f32).T.astype(bf16), ones)
    row_s[4:5] = jnp.sum(n_wide * keys_ref[...], axis=0, keepdims=True) * (width // HEADS) ** (-0.5)
    qk = qk_ref[...]
    table_grad = split_three(
        dot_nt(m_low, value_ref[...])
        + dot_nt(n_high.astype(f32).T.astype(bf16), qk)
        + dot_nt(n_low.astype(f32).T.astype(bf16), qk)
    )
    slots = depth // TABLES
    vars_here = varg_ref.shape[0]
    for first, each in ((0, TABLES - 1), (TABLES - 1, 1)):
        row = lax.broadcasted_iota(jnp.int32, (each * vars_here, depth), 0)
        col = lax.broadcasted_iota(jnp.int32, (each * vars_here, depth), 1)
        want = (first + row % each) * slots + place_ref[0] * vars_here + row // each
        picks = jnp.where(want == col, 1.0, 0.0).astype(bf16)
        rows = sum(dot(picks, part) for part in table_grad)
        if each == 1:
            varg_ref[...] = rows
        else:
            for v in range(vars_here):
                embedg_ref[v] = rows[v * each : (v + 1) * each]
    row_s[0:4] = m_s[depth : depth + 4, :]
    at = (2 * place_ref[2] + place_ref[1]) * shard
    for i, ref in enumerate(row_refs):
        if shard % 128:
            ref[...] = row_s[i : i + 1]
        else:
            ref[...] = row_s[i : i + 1, pl.ds(pl.multiple_of(at, shard), shard)]


def back_kernel(count, parts, n_z, *refs):
    place_ref = refs[0]
    piece_refs = refs[1 : 1 + count * parts]
    (
        qkv_far, merged_far, gain_ref, gs_far, out_w_far, pix_ref, shi_ref, slo_ref, sthi_ref,
        stlo_ref, real_ref, ev_ref, values_far, gains_two_ref,
        fields_ref, send_ref, keep_ref, slope_s, packed_s, m_ref, n_ref,
        qkv_s, merged_ref, gs_ref, out_w_ref, values_ref, copied,
    ) = refs[1 + count * parts :]
    width = merged_ref.shape[1]
    thirds = [
        pltpu.make_async_copy(
            qkv_far.at[:, pl.ds(third * width, width)], qkv_s.at[third], copied.at[third]
        )
        for third in range(3)
    ]
    others = [
        pltpu.make_async_copy(far, near, copied.at[3 + i])
        for i, (far, near) in enumerate(
            [
                (merged_far, merged_ref), (gs_far, gs_ref), (out_w_far, out_w_ref),
                (values_far, values_ref),
            ]
        )
    ]
    for copy in thirds + others:
        copy.start()
    slots = real_ref.shape[0]
    if count == 1:
        packed = piece_refs[0][...]
    else:
        span = piece_refs[0].shape[1] // 3
        for third in range(3):
            for part in range(parts):
                for d in range(count):
                    at = third * (count * parts) + (place_ref[0] ^ d) * parts + part
                    packed_s[:, pl.ds(pl.multiple_of(at * span, span), span)] = piece_refs[
                        part * count + d
                    ][:, third * span : (third + 1) * span]
        packed = packed_s[...]
    pixel_rows = pix_ref[...]
    probs = variable_probs(pixel_rows, shi_ref[...], slo_ref[...], real_ref[...], slots)
    weights = probs.astype(bf16).astype(f32)
    pixels = pixel_rows.astype(f32).reshape(TABLES, slots, -1)
    upstream = None
    for third, copy in enumerate(thirds):
        copy.wait()
        product = dot_nt(packed[:, third * width : (third + 1) * width], qkv_s[third])
        upstream = product if upstream is None else upstream + product
    upstream = upstream.astype(bf16).astype(f32)
    for copy in others:
        copy.wait()
    unit_rows, inverse = norm_parts(merged_ref[...])
    g_merged = gs_ref[...] + norm_back(upstream, unit_rows, inverse, gain_ref[...])
    low = g_merged.astype(bf16)
    depth = pix_ref.shape[0]
    m_ref[...] = jnp.zeros_like(m_ref)
    m_ref[depth + 2 : depth + 4, :] = gains_two_ref[...]
    m_ref[depth : depth + 1, :] = jnp.sum(upstream * unit_rows, axis=0, keepdims=True)
    m_ref[depth + 1 : depth + 2, :] = jnp.sum(upstream, axis=0, keepdims=True)
    g_values = dot_nt(low, out_w_ref[...]).astype(bf16)
    grads = dot(values_ref[...], low)
    size = ev_ref.shape[2]
    g_fields = jnp.zeros(pixels.shape, f32)
    for h in range(HEADS):
        rows = g_values[:, h * size : (h + 1) * size]
        both = dot_nt(ev_ref[h], rows)
        table = (both[:depth] + both[depth:]).reshape(pixels.shape)
        g_weights = jnp.sum(pixels * table, axis=0)
        total = jnp.sum(g_weights * probs[h], axis=0, keepdims=True)
        slope_s[h * slots : (h + 1) * slots, :] = (probs[h] * (g_weights - total)).astype(bf16)
        g_fields += weights[h][None] * table
        mixed = (weights[h][None] * pixels).reshape(pixel_rows.shape)
        pair = dot(jnp.concatenate(split_two(mixed), axis=0), rows)
        m_ref[:depth, h * size : (h + 1) * size] = pair[:depth] + pair[depth:]
    slopes = slope_s[...]
    fields_ref[...] = (
        g_fields.reshape(pixel_rows.shape) + dot(sthi_ref[...], slopes) + dot(stlo_ref[...], slopes)
    ).astype(bf16)
    n_ref[...] = dot_nt(pixel_rows, slopes)

    core = place_ref[1]
    shard = grads.shape[0] // (2 * n_z)
    for zz in range(n_z):
        at = slice(zz * shard, (zz + 1) * shard)
        even = grads[2 * zz * shard : (2 * zz + 1) * shard]
        odd = grads[(2 * zz + 1) * shard : (2 * zz + 2) * shard]
        keep_ref[at] = jnp.where(core == 0, even, odd)
        send_ref[at] = jnp.where(core == 0, odd, even).astype(bf16)
    top = n_z * shard
    middle = top + m_ref.shape[0]
    tables = m_ref[...]
    keep_ref[top:middle] = tables
    send_ref[top:middle] = tables.astype(bf16)
    columns = lax.broadcasted_iota(jnp.int32, n_ref.shape, 1)
    same = columns % slots == lax.broadcasted_iota(jnp.int32, n_ref.shape, 0) % slots
    n_high, n_low = split_two(jnp.where(same, n_ref[...], 0.0))
    heads = (HEADS, n_ref.shape[1])
    picks = lax.broadcasted_iota(jnp.int32, heads, 1) // slots
    picks = jnp.where(picks == lax.broadcasted_iota(jnp.int32, heads, 0), 1.0, 0.0).astype(bf16)
    n_rows = dot_nt(picks, n_high) + dot_nt(picks, n_low)
    keep_ref[middle:] = jnp.zeros((HEADS, keep_ref.shape[1]), f32)
    keep_ref[middle:, :depth] = n_rows
    send_ref[middle:] = keep_ref[middle:].astype(bf16)


def per_device(
    n_var, n_z, fields, var_mask, embed_weight, var_embed, agg_query, agg_key, agg_value, agg_out,
    norm1_gain, norm1_bias, attn_qkv, attn_proj, norm2_gain, norm2_bias, mlp_in, mlp_out, cotangent,
):
    n_item = 2 * n_z
    width = agg_key.shape[0]
    size = width // HEADS
    scale = size ** (-0.5)
    hidden_width = mlp_in.shape[1]
    vars_here, channels, patches = fields.shape[1:]
    slot_count = var_mask.shape[1]
    slots = -(-slot_count // 16) * 16
    mine = patches // n_var
    here = HEADS // n_var
    cols = here * size
    shard = width // n_item
    me = lax.axis_index("var")
    core = lax.axis_index("core")
    z_at = lax.axis_index("z")
    item = z_at * 2 + core
    rel = me ^ jnp.arange(n_var)
    rel_z = z_at ^ jnp.arange(n_z)
    place = jnp.stack([me, core, z_at]).astype(jnp.int32)
    lanes_fit = cols % 128 == 0

    def send(array, other):
        return lax.ppermute(array, "var", [(i, i ^ other) for i in range(n_var)])

    def send_z(array, other):
        return lax.ppermute(array, "z", [(i, i ^ other) for i in range(n_z)])

    def swap_core(array):
        return lax.ppermute(array, "core", [(0, 1), (1, 0)])

    def canonical(by_distance):
        return jnp.take(jnp.stack(by_distance, axis=0), rel, axis=0)

    def call(kernel, grid, in_specs, out_specs, out_shape, scratch, estimate, name, *args):
        return pl.pallas_call(
            kernel,
            grid_spec=pltpu.PrefetchScalarGridSpec(
                num_scalar_prefetch=1,
                grid=grid,
                in_specs=in_specs,
                out_specs=out_specs,
                scratch_shapes=scratch,
            ),
            out_shape=out_shape,
            compiler_params=params(),
            cost_estimate=estimate,
            name=name,
        )(place, *args)

    depth = TABLES * slots
    pixel_part = jnp.concatenate([fields[0], jnp.ones((vars_here, 1, patches), bf16)], axis=1)
    table_part = jnp.concatenate([embed_weight, var_embed[:, None, :]], axis=1)
    piece = jnp.concatenate([pixel_part, table_part], axis=2).reshape(TABLES * vars_here, -1)
    pieces = [piece] + [send(piece, d) for d in range(1, n_var)]
    real = jnp.pad(var_mask[0], (0, slots - slot_count)).astype(f32)[:, None]
    prep_in = pieces + [agg_query[None], agg_key, agg_value]
    maps = [(HEADS * slots, depth)] * 2 + [(depth, HEADS * slots)] * 2
    prep_out = (
        [((depth, patches), bf16), ((depth, width), bf16)]
        + [(shape, bf16) for shape in maps]
        + [
            ((width, 3 * depth), bf16),
            ((HEADS, 2 * depth, size), bf16),
            ((depth, width), f32),
            ((width, HEADS), bf16),
            ((HEADS, width), bf16),
        ]
    )
    (
        pixels, tables, score_high, score_low, score_high_t, score_low_t, ev_front, ev_back,
        table_keys, query_keys, spread,
    ) = call(
        partial(prep_kernel, n_var, vars_here, patches),
        (1,),
        [whole(array.shape) for array in prep_in],
        [whole(shape) for shape, _ in prep_out],
        [jax.ShapeDtypeStruct(shape, kind) for shape, kind in prep_out],
        [pltpu.VMEM((depth, patches + width), bf16)],
        cost(8 * depth * width * width, 4 * width * width),
        "prep",
        *prep_in,
    )

    gain_one, bias_one = norm1_gain[None], norm1_bias[None]
    gain_two, bias_two = norm2_gain[None], norm2_bias[None]

    if lanes_fit:
        qkv_parts = [attn_qkv] * 3
        qkv_specs = [
            pl.BlockSpec((width, cols), lambda i, at, third=third: (0, third * n_var + at[0]))
            for third in range(3)
        ]
    else:
        qkv_mine = lax.dynamic_index_in_dim(
            attn_qkv.reshape(width, 3, n_var, cols), me, axis=2, keepdims=False
        )
        qkv_parts = [qkv_mine[:, third] for third in range(3)]
        qkv_specs = [whole((width, cols))] * 3

    block = min(512, mine)
    steps = patches // block
    own = mine // block
    heads_shape = jax.ShapeDtypeStruct((here, patches, size), bf16)
    heads_spec = pl.BlockSpec((here, block, size), lambda i, _: (0, i, 0))
    agg_values_t, merged, normed_send, normed_keep, queries, keys, values = call(
        partial(front_kernel, own, n_z),
        (steps,),
        [
            pl.BlockSpec((depth, block), lambda i, _: (0, i)),
            whole(score_high.shape),
            whole(score_low.shape),
            whole(real.shape),
            whole(ev_front.shape),
            whole(agg_out.shape),
            whole(gain_one.shape),
            whole(bias_one.shape),
        ]
        + qkv_specs,
        [
            pl.BlockSpec((width, block), lambda i, _: (0, jnp.minimum(i, own - 1))),
            pl.BlockSpec((block, width), lambda i, _: (jnp.minimum(i, own - 1), 0)),
            pl.BlockSpec((width // 2, block), lambda i, _: (0, i)),
            pl.BlockSpec((width // 2, block), lambda i, _: (0, i)),
            heads_spec,
            heads_spec,
            heads_spec,
        ],
        [
            jax.ShapeDtypeStruct((width, mine), bf16),
            jax.ShapeDtypeStruct((mine, width), f32),
            jax.ShapeDtypeStruct((width // 2, patches), bf16),
            jax.ShapeDtypeStruct((width // 2, patches), bf16),
            heads_shape,
            heads_shape,
            heads_shape,
        ],
        [pltpu.VMEM((width, block), f32), pltpu.VMEM((width, block), bf16)],
        cost(2 * patches * width * (width + 3 * cols + 256), 16 * patches * width),
        "front",
        pixels, score_high, score_low, real, ev_front, agg_out, gain_one, bias_one, *qkv_parts,
    )

    def attend(distance):
        heads = here
        return pl.pallas_call(
            attend_kernel,
            grid=(here // heads,),
            in_specs=[
                pl.BlockSpec((heads, mine, size), lambda i: (i, distance, 0)),
                pl.BlockSpec((heads, patches, size), lambda i: (i, 0, 0)),
                pl.BlockSpec((heads, patches, size), lambda i: (i, 0, 0)),
            ],
            out_specs=[
                pl.BlockSpec((mine, heads * size), lambda i: (0, i)),
                pl.BlockSpec((heads, 1, mine), lambda i: (i, 0, 0)),
            ],
            out_shape=[
                jax.ShapeDtypeStruct((mine, cols), bf16),
                jax.ShapeDtypeStruct((here, 1, mine), f32),
            ],
            compiler_params=params(),
            cost_estimate=cost(
                4 * mine * patches * here * 256, 4 * patches * cols * 2, mine * patches * here
            ),
            name=f"attend{distance}",
        )(queries, keys, values)

    attended_by, lse_by, arrived = [None] * n_var, [None] * n_var, [None] * n_var
    for distance in reversed(range(n_var)):
        attended_by[distance], lse_by[distance] = attend(distance)
        arrived[distance] = (
            send(attended_by[distance], distance) if distance else attended_by[distance]
        )
    if not lanes_fit:
        arrived = [canonical(arrived).transpose(1, 0, 2).reshape(mine, width)]

    cot = cotangent[0]
    tile = 2 * hidden_width // n_item
    row_f32 = jax.ShapeDtypeStruct((mine, width), f32)
    row_bf16 = jax.ShapeDtypeStruct((mine, width), bf16)
    row_spec = whole((mine, width))
    tall_spec = whole((width, mine))
    tall_bf16 = jax.ShapeDtypeStruct((width, mine), bf16)
    piece_spec = whole((mine, cols))
    (
        output, attended_t, normed_two_t, active_send, active_keep, g_hidden, g_stream, g_stream_low,
        gains_two,
        *g_attended,
    ) = call(
        partial(mlp_kernel, len(arrived), n_var),
        (hidden_width // tile,),
        [whole(piece.shape) for piece in arrived]
        + [
            row_spec,
            whole((width, width)),
            whole(gain_two.shape),
            whole(bias_two.shape),
            row_spec,
            pl.BlockSpec((width, tile), lambda i, _: (0, i)),
            pl.BlockSpec((tile, width), lambda i, _: (i, 0)),
        ],
        [
            row_spec,
            tall_spec,
            tall_spec,
            pl.BlockSpec((tile // 2, mine), lambda i, _: (i, 0)),
            pl.BlockSpec((tile // 2, mine), lambda i, _: (i, 0)),
            pl.BlockSpec((mine, tile), lambda i, _: (0, i)),
            row_spec,
            row_spec,
            whole((2, width)),
        ]
        + [piece_spec] * n_var,
        [
            row_bf16,
            tall_bf16,
            tall_bf16,
            jax.ShapeDtypeStruct((hidden_width // 2, mine), bf16),
            jax.ShapeDtypeStruct((hidden_width // 2, mine), bf16),
            jax.ShapeDtypeStruct((mine, hidden_width), bf16),
            row_f32,
            row_bf16,
            jax.ShapeDtypeStruct((2, width), f32),
        ]
        + [jax.ShapeDtypeStruct((mine, cols), bf16)] * n_var,
        [
            pltpu.VMEM((mine, width), bf16),
            pltpu.VMEM((mine, width), bf16),
            pltpu.VMEM((mine, width), f32),
            pltpu.VMEM((mine, width), f32),
            pltpu.VMEM((mine, 1), f32),
            pltpu.VMEM((mine, width), f32),
            pltpu.VMEM((mine, width), f32),
            pltpu.VMEM((tile, mine), bf16),
        ],
        cost(
            2 * mine * width * (4 * hidden_width + 2 * width),
            4 * width * hidden_width + 16 * mine * width,
        ),
        "mlp",
        *arrived, merged, attn_proj, gain_two, bias_two, cot, mlp_in, mlp_out,
    )
    g_heads = [g_attended[0]] + [send(g_attended[d], d) for d in range(1, n_var)]

    kept_rows = n_z * shard

    def pair_product(tall, grads):
        return dot(tall, grads).astype(bf16)

    def pair_own(tall, grads, got):
        return (dot(tall, grads) + got.astype(f32)).astype(bf16)

    def column_block(array, start=0, total=None):
        rows = array.shape[0]
        total = total or array.shape[1]
        span = total // n_var
        if span % 128 == 0:
            return array, pl.BlockSpec((rows, span), lambda j, at: (0, start // span + (at[0] ^ j)))
        cut = array[:, start : start + total]
        cut = jnp.take(cut.reshape(rows, n_var, span).transpose(1, 0, 2), rel, axis=0)
        return cut, pl.BlockSpec((None, rows, span), lambda j, at: (j, 0, 0))

    def pair_send_two(main, side):
        spec = pl.BlockSpec((n_z, None, shard, mine), lambda j, at: (0, 1 - at[1], 0, 0))
        tiles = hidden_width // width
        return call(
                send_kernel,
                (tiles + 1,),
                [
                    spec,
                    pl.BlockSpec((mine, width), lambda j, at: (0, jnp.minimum(j, tiles - 1))),
                    spec,
                    whole((mine, width)),
                ],
                pl.BlockSpec((kept_rows, width), lambda j, at: (0, j)),
                jax.ShapeDtypeStruct((kept_rows, hidden_width + width), bf16),
                [],
                cost(2 * kept_rows * mine * (hidden_width + width), 24 * kept_rows * width, share=2),
                "send",
                main[0].reshape(n_z, 2, shard, mine), main[1],
                side[0].reshape(n_z, 2, shard, mine), side[1],
            )

    def pair_keep(main, side, got):
        args, specs, start = [], [], 0
        for tall, grads in (main, side):
            args.append(tall.reshape(n_z, 2, shard, mine))
            specs.append(pl.BlockSpec((n_z, None, shard, mine), lambda j, at: (0, at[1], 0, 0)))
            for array, spec in (column_block(grads), column_block(got, start, grads.shape[1])):
                args.append(array)
                specs.append(spec)
            start += grads.shape[1]
        main_span, side_span = main[1].shape[1] // n_var, side[1].shape[1] // n_var
        first = 3 * main_span // 4
        spans = [first] * n_var + [main_span - first + side_span] * n_var
        outs = call(
            partial(keep_kernel, n_var),
            (n_var,),
            specs,
            [whole((kept_rows, span)) for span in spans],
            [jax.ShapeDtypeStruct((kept_rows, span), bf16) for span in spans],
            [],
            cost(
                2 * kept_rows * mine * (main_span + side_span) * n_var, 24 * kept_rows * main_span, share=2
            ),
            "keep",
            *args,
        )
        return outs[:n_var], outs[n_var:]

    def add_all(first, *others):
        total = first.astype(f32)
        for other in others:
            total = total + other.astype(f32)
        return total.astype(bf16)

    def exchange(pieces):
        return [pieces[0]] + [send(pieces[d], d) for d in range(1, n_var)]


    main, side = (normed_two_t, g_hidden), (attended_t, g_stream_low)
    sent = pair_send_two(main, side)
    sent, g_heads, active_send = lax.optimization_barrier((sent, g_heads, active_send))
    got = swap_core(sent)
    got_mlp_out = swap_core(pair_product(active_send, cot))
    first, second = pair_keep(main, side, got)
    active_keep, first, second = lax.optimization_barrier((active_keep, first, second))
    first = exchange(first)
    g_mlp_out = pair_own(active_keep, cot, got_mlp_out)
    mlp_out_rows = lax.psum_scatter(g_mlp_out, "z", scatter_dimension=0, tiled=True)
    g_heads, _ = lax.optimization_barrier((g_heads, g_mlp_out))

    group = min(2, here)
    parts = here // group
    gcols = group * size
    back_block = min(1024, patches)

    def attend_back(part, queries, extra):
        group_spec = pl.BlockSpec((group, back_block, size), lambda i: (part, i, 0))
        side_spec = pl.BlockSpec((mine, gcols), lambda i: (0, part))
        piece_cols = 3 * gcols + sum(array.shape[1] for array in extra[:1])
        full, *pieces = pl.pallas_call(
            partial(attend_back_kernel, n_var, len(extra)),
            grid=(patches // back_block,),
            in_specs=[whole(array.shape) for array in extra]
            + [
                pl.BlockSpec((group, patches, size), lambda i: (part, 0, 0)),
                group_spec,
                group_spec,
            ]
            + [pl.BlockSpec((group, 1, mine), lambda i: (part, 0, 0))] * n_var
            + [side_spec] * (2 * n_var),
            out_specs=[whole((patches, 3 * gcols))] + [whole((mine, piece_cols))] * n_var,
            out_shape=[jax.ShapeDtypeStruct((patches, 3 * gcols), bf16)]
            + [jax.ShapeDtypeStruct((mine, piece_cols), bf16)] * n_var,
            scratch_shapes=[
                pltpu.VMEM((group, patches, size), bf16),
                pltpu.VMEM((group, 1, patches), f32),
                pltpu.VMEM((group, 1, patches), f32),
                pltpu.VMEM((group, size, patches), f32),
                pltpu.VMEM((group, back_block, patches), bf16),
                pltpu.VMEM((group, back_block, patches), bf16),
            ],
            compiler_params=params(),
            cost_estimate=cost(
                10 * patches * patches * group * 256, 8 * patches * gcols * 2, patches * patches * group
            ),
            name=f"attend_back{part}",
        )(*extra, queries, keys, values, *lse_by, *attended_by, *g_heads)
        return full, pieces

    ride = kept_rows == mine and parts > 1
    g_qkv, packed_pieces = [], []
    for part in range(parts):
        full, pieces = attend_back(part, queries, second if ride and part == 0 else [])
        if part == 0:
            full, first = lax.optimization_barrier((full, first))
            first_sum = add_all(*first)
        if part < parts - 1:
            product = pair_product(normed_send, full)
            queries, first_sum, product = lax.optimization_barrier((queries, first_sum, product))
            g_qkv.append((full, product))
        if part == parts - 1:
            pieces, packed_pieces = lax.optimization_barrier((pieces, packed_pieces))
        packed_pieces += exchange(pieces)
    if ride:
        second = [piece[:, 3 * gcols :] for piece in packed_pieces[:n_var]]
    else:
        second = exchange(second)
    g_qkv.append((full, pair_product(normed_send, full)))
    second_sum = add_all(*second)
    columns = [first_sum, second_sum]
    columns += [pair_own(normed_keep, full, swap_core(product)) for full, product in g_qkv]
    both_sum = jnp.concatenate(columns, axis=1)
    def my_slice(array, axis):
        return lax.dynamic_slice_in_dim(array, item * shard, shard, axis=axis)

    packed_pieces, both_sum = lax.optimization_barrier((packed_pieces, both_sum))
    both_rows = lax.psum_scatter(both_sum, "z", scatter_dimension=0, tiled=True)
    count = n_var
    if not lanes_fit:
        packed = [
            canonical(packed_pieces[part * n_var : (part + 1) * n_var]) for part in range(parts)
        ]
        packed = jnp.stack(packed, axis=0).reshape(parts, n_var, mine, 3, gcols)
        packed_pieces = [packed.transpose(2, 3, 1, 0, 4).reshape(mine, 3 * width)]
        count, parts = 1, 1
    packed_cols = 3 * gcols if lanes_fit else 3 * width

    far = pl.BlockSpec(memory_space=pl.ANY)
    table_rows = -(-(depth + 4) // 16) * 16
    late_rows = kept_rows + table_rows
    g_fields, late_send, late_keep = call(
        partial(back_kernel, count, parts, n_z),
        (1,),
        [pl.BlockSpec((block, packed_cols), lambda i, _: (i, 0)) for piece in packed_pieces]
        + [
            far,
            far,
            whole(gain_one.shape),
            far,
            far,
            pl.BlockSpec((depth, block), lambda i, _: (0, i)),
            whole(score_high.shape),
            whole(score_low.shape),
            whole((depth, HEADS * slots)),
            whole((depth, HEADS * slots)),
            whole(real.shape),
            whole(ev_back.shape),
            far,
            whole((2, width)),
        ],
        [
            pl.BlockSpec((depth, block), lambda i, _: (0, i)),
            whole((late_rows + HEADS, width)),
            whole((late_rows + HEADS, width)),
        ],
        [
            jax.ShapeDtypeStruct((depth, mine), bf16),
            jax.ShapeDtypeStruct((late_rows + HEADS, width), bf16),
            jax.ShapeDtypeStruct((late_rows + HEADS, width), f32),
        ],
        [
            pltpu.VMEM((HEADS * slots, block), bf16),
            pltpu.VMEM((block, 3 * width), bf16),
            pltpu.VMEM((table_rows, width), f32),
            pltpu.VMEM((depth, HEADS * slots), f32),
            pltpu.VMEM((3, width, width), bf16),
            pltpu.VMEM((mine, width), f32),
            pltpu.VMEM((mine, width), f32),
            pltpu.VMEM((width, width), bf16),
            pltpu.VMEM((width, mine), bf16),
            pltpu.SemaphoreType.DMA((7,)),
        ],
        cost(2 * mine * width * 4 * width, 8 * width * width + 20 * mine * width),
        "back",
        *packed_pieces, attn_qkv, merged, gain_one, g_stream, agg_out, pixels, score_high, score_low,
        score_high_t, score_low_t, real, ev_back, agg_values_t, gains_two,
    )

    late_send, mlp_out_rows = lax.optimization_barrier((late_send, mlp_out_rows))
    out_block = mlp_out_rows.shape[0] // n_var
    mlp_out_by = exchange(
        [
            lax.dynamic_slice_in_dim(mlp_out_rows, (me ^ d) * out_block, out_block, axis=0)
            for d in range(n_var)
        ]
    )
    mlp_out_rows = add_all(*mlp_out_by).reshape(shard, -1)

    late_got = swap_core(late_send)
    late_span = width // n_var
    n_blocks = -(-depth // late_span)
    n_spec = pl.BlockSpec((HEADS, n_blocks * late_span), lambda j, at: (late_rows // HEADS, 0))
    sum_rows = late_rows + n_blocks * HEADS
    f_rows = -(-channels * vars_here // 16) * 16
    piece_rows = sum_rows + f_rows * (mine // late_span)
    late_args = [late_keep, late_got]
    if late_span % 128:
        late_args = [
            jnp.take(array.reshape(-1, n_var, late_span).transpose(1, 0, 2), rel, axis=0)
            for array in late_args
        ]
    late_pieces = call(
        partial(pair_kernel, n_var, channels, vars_here, late_rows),
        (1,),
        [whole(array.shape) for array in late_args] + [n_spec, n_spec, whole((depth, mine))],
        [whole((piece_rows, late_span))] * n_var,
        [jax.ShapeDtypeStruct((piece_rows, late_span), bf16)] * n_var,
        [],
        cost(piece_rows * width, 8 * piece_rows * width),
        "late_pair",
        *late_args, late_keep, late_got, g_fields,
    )
    late_pieces = exchange(late_pieces)
    late_pieces, both_rows = lax.optimization_barrier((late_pieces, both_rows))
    rows_all = jnp.concatenate([both_rows, mlp_out_rows], axis=1)
    halves = 1 if n_var == 4 and lanes_fit else 0
    if halves:
        near = [send(rows_all, 1), send(rows_all, 2)]
    else:
        rows_all = list(lax.all_gather(rows_all, "var", axis=0))
    z_rows = shard + table_rows + n_blocks * HEADS
    *z_pieces, fields_grad = call(
        partial(z_pieces_kernel, n_var, shard, n_z),
        (1,),
        [whole((piece_rows, late_span))] * n_var,
        [whole((z_rows, late_span))] * n_z + [whole((vars_here, channels, patches))],
        [jax.ShapeDtypeStruct((z_rows, late_span), bf16)] * n_z
        + [jax.ShapeDtypeStruct((vars_here, channels, patches), f32)],
        [pltpu.VMEM((sum_rows, late_span), bf16)],
        cost(piece_rows * width, 2 * piece_rows * width),
        "late_z",
        *late_pieces,
    )
    z_pieces = [z_pieces[0]] + [send_z(z_pieces[d], d) for d in range(1, n_z)]
    late_rows_mine, n_all = pl.pallas_call(
        partial(z_sum_kernel, n_z),
        out_shape=[
            jax.ShapeDtypeStruct((shard + table_rows, late_span), bf16),
            jax.ShapeDtypeStruct((HEADS, n_blocks * late_span), f32),
        ],
        compiler_params=params(),
        cost_estimate=cost(z_rows * width, 2 * z_rows * width),
        name="late_sum",
    )(*z_pieces)

    fields_grad = fields_grad[None]
    if halves:
        late_rows_mine, near = lax.optimization_barrier((late_rows_mine, near))
        half = rows_all.shape[1] // 2
        rows_all = [rows_all] + near + [send(near[0][:, :half], 2), send(near[1][:, half:], 1)]
    late_by = exchange([late_rows_mine] * n_var)
    if late_span % 128:
        late_by = [canonical(late_by).transpose(1, 0, 2).reshape(shard + table_rows, width)]
    row_width = width if shard % 128 else shard
    small_shapes = [(vars_here, channels, shard), (vars_here, shard)] + [(1, row_width)] * 5
    final_in = [n_all, my_slice(tables, 1).T, spread, table_keys]
    item_rows = [
        pl.BlockSpec((shard, width), lambda i, at: (2 * at[2] + at[1], 0)),
        pl.BlockSpec((shard, HEADS), lambda i, at: (2 * at[2] + at[1], 0)),
    ]
    agg_out_grad, agg_value_grad, agg_key_grad, embed_weight_grad, var_embed_grad, *rows = call(
        partial(final_kernel, len(late_by)),
        (1,),
        [whole(array.shape) for array in late_by + final_in] + item_rows,
        [whole((shard, width))] * 3
        + [whole(shape) for shape in small_shapes],
        [jax.ShapeDtypeStruct((shard, width), f32)] * 3
        + [jax.ShapeDtypeStruct(shape, f32) for shape in small_shapes],
        [pltpu.VMEM((table_rows, width), f32), pltpu.VMEM((8, width), f32)],
        cost(2 * shard * width * 3 * depth, 12 * shard * width),
        "final",
        *late_by, *final_in, agg_value, query_keys,
    )
    *gains, agg_query_grad = [
        row[0] if row_width == shard else my_slice(row[0], 0) for row in rows
    ]

    row_shapes = [
        jax.ShapeDtypeStruct((shard, hidden_width), f32),
        jax.ShapeDtypeStruct((shard, width), f32),
        jax.ShapeDtypeStruct((shard, 3 * width), f32),
        jax.ShapeDtypeStruct((n_var, shard, out_block * width // shard), f32),
    ]
    mlp_in_grad, attn_proj_grad, attn_qkv_grad, mlp_out_grad = call(
        partial(assemble_kernel, n_var, here // group, gcols, halves),
        (1,),
        [whole(array.shape) for array in rows_all],
        [whole(row.shape) for row in row_shapes],
        row_shapes,
        [],
        cost(shard * 9 * width, 6 * shard * 9 * width),
        "assemble",
        *rows_all,
    )
    mlp_out_grad = mlp_out_grad.reshape(n_var * out_block, width)
    return (
        output[None],
        fields_grad,
        embed_weight_grad,
        var_embed_grad,
        agg_query_grad,
        agg_key_grad,
        agg_value_grad,
        agg_out_grad,
        gains[0],
        gains[1],
        attn_qkv_grad,
        attn_proj_grad,
        gains[2],
        gains[3],
        mlp_in_grad,
        mlp_out_grad,
    )


def solution(mesh):
    n_var, n_item = mesh.shape["var"], mesh.shape["item"]
    items = ("z", "core")
    return jax.shard_map(
        partial(per_device, n_var, n_item // 2),
        mesh=Mesh(mesh.devices.reshape(n_var, n_item // 2, 2), ("var", "z", "core")),
        in_specs=(
            P(items, "var", None, None),
            P(items, None),
            P("var", None, None),
            P("var", None),
            P(),
            P(),
            P(),
            P(),
            P(),
            P(),
            P(),
            P(),
            P(),
            P(),
            P(),
            P(),
            P(items, "var", None),
        ),
        out_specs=(
            P(items, "var", None),
            P(items, "var", None, None),
            P("var", None, items),
            P("var", items),
            P(items),
            P(items, None),
            P(items, None),
            P(items, None),
            P(items),
            P(items),
            P(items, None),
            P(items, None),
            P(items),
            P(items),
            P(items, None),
            P(items, None),
        ),
        check_vma=False,
    )
```
